32 devices in a mesh: row: 4 (over z), col: 8 (over y, x, core).
Axes of the slice: x: 2, y: 2, z: 4, core: 2. Of those that a mesh axis runs over, the one named last changes fastest.
Arguments:
- tile_values: bfloat16 [4, 8, 256, 128, 128], P('row', 'col'), may hold values from -0.125 to 0.125
- tile_rows: int32 [4, 8, 256], P('row', 'col'), may hold values from 0 to 127
- tile_cols: int32 [4, 8, 256], P('row', 'col'), may hold values from 0 to 255
- increments: float32 [16, 128, 2048], P('row', None, 'col'), may hold values from 0 to 0.1
- dual_vars: float32 [16, 65536], P(None, 'row'), may hold values from 0 to 1
- flight_cost: float32 [128, 2048], P(None, 'col'), may hold values from -0.5 to 0.5
- win_start: int32 [2048], P('col'), may hold values from 0 to 63
- win_len: int32 [2048], P('col'), may hold values from 32 to 64
- capacity: int32 [16, 65536], P(None, 'row'), may hold values from 0 to 3
Outputs:
- primal: float32 [16, 128, 2048], P('row', None, 'col')
- duals_out: float32 [16, 65536], P(None, 'row')
The draws below stay inside these ranges and needn't reach their ends.
Inputs may be any that keep to these rules, and one draw needn't show every extreme that they name: `tile_rows`: a block position may occur more than once in a device's list; such blocks add.
All inputs are finite; a program needn't handle non-finite values.
Results may differ from the reference program's by a relative error of at most 0.0056.
Values may be sent and summed in bfloat16 or wider, within the bound.
No kernel may reach another device: no remote copies, remote signals or barrier semaphores. Data moves between devices by JAX's collectives and lax.ppermute only.
A program may use at most 64 MiB of HBM per device.

```python
import math
import jax
import jax.numpy as jnp
from jax import lax

TILE = 128
SCEN = 16
WINDOW = 128
ITERS = 2
ROW_TILES = 128
TILES_DEV = 256
FLIGHTS = 2048
COL_TILES = 256
ROWS = 65536
N_ROW = 4
N_COL = 8


def set_ends(array, key, least, largest):
    longest = array.shape.index(max(array.shape))
    spots = []
    for shift in (0, 1):
        where = [jax.random.randint(jax.random.fold_in(key, axis), (), 0, length) for axis, length in enumerate(array.shape)]
        where[longest] = (where[longest] + shift) % array.shape[longest]
        spots.append(tuple(where))
    return array.at[spots[0]].set(least).at[spots[1]].set(largest)


def levels(own_key, dims, shards, low, high):
    factor_of, own = 1.0, jax.random.fold_in(own_key, 6)
    for position, blocks in shards:
        steps = jnp.exp(jax.random.uniform(jax.random.fold_in(own, position), (blocks,), jnp.float32, low / len(shards), high / len(shards)))
        factor_of = factor_of * jnp.repeat(steps, dims[position] // blocks).reshape([-1 if axis == position else 1 for axis in range(len(dims))])
    return factor_of


def bell_draw(key, extent, spread, limit, pieces=(), dtype=jnp.bfloat16):
    array = spread * jax.random.normal(key, extent, jnp.float32)
    if pieces:
        array = array * levels(key, extent, pieces, -0.22, 0.18)
    return jnp.clip(array, -limit, limit).astype(dtype)


def setup_inputs(seed: int = 0) -> dict:
    key_list = jax.random.split(jax.random.key(seed), 10)
    return {
        "tile_values": bell_draw(key_list[0], (N_ROW, N_COL, TILES_DEV, TILE, TILE), (TILE * N_COL * TILES_DEV // ROW_TILES) ** -0.5, 0.125, ((0, 4), (1, 8))),
        "tile_rows": set_ends(jax.random.randint(key_list[1], (N_ROW, N_COL, TILES_DEV), 0, ROW_TILES), jax.random.fold_in(key_list[1], 1), 0, ROW_TILES - 1).astype(jnp.int32),
        "tile_cols": set_ends(jax.random.randint(key_list[2], (N_ROW, N_COL, TILES_DEV), 0, COL_TILES), jax.random.fold_in(key_list[2], 1), 0, COL_TILES - 1).astype(jnp.int32),
        "increments": jnp.clip(0.1 * jax.random.uniform(key_list[3], (SCEN, WINDOW, FLIGHTS), jnp.float32) ** levels(key_list[3], (SCEN, WINDOW, FLIGHTS), ((0, 4), (2, 8)), -0.2, 0.2), 0.0, 0.1),
        "dual_vars": jnp.clip(1.0 * jax.random.uniform(key_list[4], (SCEN, ROWS), jnp.float32) ** levels(key_list[4], (SCEN, ROWS), ((1, 4),), -0.2, 0.2), 0.0, 1.0),
        "flight_cost": jnp.clip(jax.random.uniform(key_list[5], (WINDOW, FLIGHTS), jnp.float32, -0.5, 0.5) * levels(key_list[5], (WINDOW, FLIGHTS), ((1, 8),), -0.4, 0.0), -0.5, 0.5),
        "win_start": set_ends(jax.random.randint(key_list[6], (FLIGHTS,), 0, WINDOW // 2), jax.random.fold_in(key_list[6], 1), 0, (WINDOW // 2) - 1).astype(jnp.int32),
        "win_len": set_ends(jax.random.randint(key_list[7], (FLIGHTS,), WINDOW // 4, WINDOW // 2 + 1), jax.random.fold_in(key_list[7], 1), WINDOW // 4, (WINDOW // 2 + 1) - 1).astype(jnp.int32),
        "capacity": set_ends(jax.random.randint(key_list[8], (SCEN, ROWS), 0, 4), jax.random.fold_in(key_list[8], 1), 0, 3).astype(jnp.int32),
    }


SIGMA_STEP = 0.2

def running_total(values):
    length = values.shape[1]
    row_iota = lax.broadcasted_iota(jnp.int32, (length, length), 0)
    col_iota = lax.broadcasted_iota(jnp.int32, (length, length), 1)
    triangle = (row_iota >= col_iota).astype(jnp.float32)
    return jnp.einsum('kj,sjf->skf', triangle, values, precision=lax.Precision.HIGHEST)

def trailing_total(values):
    length = values.shape[1]
    row_iota = lax.broadcasted_iota(jnp.int32, (length, length), 0)
    col_iota = lax.broadcasted_iota(jnp.int32, (length, length), 1)
    triangle = (row_iota >= col_iota).astype(jnp.float32)
    return jnp.einsum('jk,sjf->skf', triangle, values, precision=lax.Precision.HIGHEST)

def forward_blocks(tile_values, tile_rows, tile_cols, probe_blocks):
    row_iota = jnp.arange(ROW_TILES).astype(jnp.int32)

    def one_group(group):

        def add_block(carried, column):
            picked = jnp.take(probe_blocks[:, column], tile_cols[group, column], axis=0 + 1).astype(jnp.float32)
            products = jnp.einsum('nij,snj->sni', tile_values[group, column].astype(jnp.float32), picked)
            hot_rows = (tile_rows[group, column][None, :] == row_iota[:, None]).astype(jnp.float32)
            return (carried + jnp.einsum('rn,sni->sri', hot_rows, products), None)
        start_sum = jnp.zeros((SCEN, ROW_TILES, TILE), jnp.float32)
        summed, _ = lax.scan(add_block, start_sum, jnp.arange(N_COL).astype(jnp.int32))
        return summed
    stacked = lax.map(one_group, jnp.arange(N_ROW).astype(jnp.int32))
    return jnp.transpose(stacked, (1, 0, 2, 3))

def backward_blocks(tile_values, tile_rows, tile_cols, dual_blocks):
    col_iota = jnp.arange(COL_TILES).astype(jnp.int32)

    def one_group(column):

        def add_block(carried, group):
            picked = jnp.take(dual_blocks[:, group], tile_rows[group, column], axis=1).astype(jnp.float32)
            products = jnp.einsum('nij,sni->snj', tile_values[group, column].astype(jnp.float32), picked)
            hot_cols = (tile_cols[group, column][None, :] == col_iota[:, None]).astype(jnp.float32)
            return (carried + jnp.einsum('cn,snj->scj', hot_cols, products), None)
        start_sum = jnp.zeros((SCEN, COL_TILES, TILE), jnp.float32)
        summed, _ = lax.scan(add_block, start_sum, jnp.arange(N_ROW).astype(jnp.int32))
        return summed
    stacked = lax.map(one_group, jnp.arange(N_COL).astype(jnp.int32))
    return jnp.transpose(stacked, (1, 0, 2, 3))

def reference(tile_values, tile_rows, tile_cols, increments, dual_vars, flight_cost, win_start, win_len, capacity):
    tau_step = 0.6 / math.sqrt(WINDOW)
    minutes = lax.broadcasted_iota(jnp.int32, (WINDOW, FLIGHTS), 0)
    upper_bound = ((minutes >= win_start[None, :]) & (minutes < (win_start + win_len)[None, :])).astype(jnp.float32)
    capacity_f = capacity.astype(jnp.float32)
    primal = increments
    cumulative = running_total(primal)
    for sweep_index in range(ITERS):
        dual_blocks = dual_vars.astype(jnp.bfloat16).reshape(SCEN, N_ROW, ROW_TILES, TILE)
        slope_all = backward_blocks(tile_values, tile_rows, tile_cols, dual_blocks).reshape(SCEN, WINDOW, FLIGHTS) + flight_cost[None]
        gradient = trailing_total(slope_all)
        primal = jnp.clip(primal - tau_step * gradient, 0.0, upper_bound[None])
        fresh_sum = running_total(primal)
        probe_vec = (2.0 * fresh_sum - cumulative).astype(jnp.bfloat16)
        image_rows = forward_blocks(tile_values, tile_rows, tile_cols, probe_vec.reshape(SCEN, N_COL, COL_TILES, TILE)).reshape(SCEN, ROWS)
        dual_vars = jnp.maximum(dual_vars + SIGMA_STEP * (image_rows - capacity_f), 0.0)
        cumulative = fresh_sum
    return (primal, dual_vars)
```

```python
import functools
import math

import jax
import jax.numpy as jnp
from jax import lax
from jax.experimental import pallas as pl
from jax.experimental.pallas import tpu as pltpu
from jax.sharding import PartitionSpec as P

ITERS = 2
SIGMA_STEP = 0.2
UNROLL = 16
VMEM_BYTES = 40 * 1024 * 1024


def params():
    return pltpu.CompilerParams(vmem_limit_bytes=VMEM_BYTES)


def whole_vmem():
    return pl.BlockSpec(memory_space=pltpu.VMEM)


def backward_kernel(dims, rows_ref, cols_ref, duals_ref, tiles_ref, out_ref, acc_ref):
    n_row, n_col, scen_local, time_block, flight_tiles, own_tiles = dims
    scen = n_row * scen_local
    step = pl.program_id(0)
    chunk = tiles_ref.shape[0]

    @pl.when(step == 0)
    def _():
        acc_ref[...] = jnp.zeros_like(acc_ref)

    def body(index, _):
        start = index * UNROLL
        products = [
            jnp.dot(
                duals_ref[rows_ref[step * chunk + start + u]],
                tiles_ref[start + u],
                preferred_element_type=jnp.float32,
            )
            for u in range(UNROLL)
        ]
        for u in range(UNROLL):
            place = pl.multiple_of(cols_ref[step * chunk + start + u] * scen, scen)
            acc_ref[pl.ds(place, scen), :] += products[u]
        return 0

    lax.fori_loop(0, chunk // UNROLL, body, 0)

    @pl.when(step == pl.num_programs(0) - 1)
    def _():
        piece = own_tiles * time_block
        for group in range(n_row):
            for column in range(n_col):
                for j in range(scen_local):
                    s = group * scen_local + j
                    parts = [
                        acc_ref[
                            pl.ds((column * own_tiles + f) * scen + s, time_block, stride=flight_tiles * scen), :
                        ]
                        for f in range(own_tiles)
                    ]
                    out_ref[group * n_col + column, pl.ds(j * piece, piece), :] = jnp.concatenate(
                        parts, axis=0
                    ).astype(jnp.bfloat16)


def forward_kernel(dims, rows_ref, cols_ref, probe_ref, tiles_ref, out_ref, flat_ref, acc_ref):
    n_row, n_col, scen_local, time_block, flight_tiles, own_tiles = dims
    scen = n_row * scen_local
    step = pl.program_id(0)
    chunk = tiles_ref.shape[0]

    @pl.when(step == 0)
    def _():
        acc_ref[...] = jnp.zeros_like(acc_ref)
        piece = own_tiles * time_block
        for group in range(n_row):
            for column in range(n_col):
                for j in range(scen_local):
                    s = group * scen_local + j
                    block = probe_ref[group * n_col + column, pl.ds(j * piece, piece), :].astype(jnp.float32)
                    for f in range(own_tiles):
                        flat_ref[
                            pl.ds((column * own_tiles + f) * scen + s, time_block, stride=flight_tiles * scen), :
                        ] = block[f * time_block : (f + 1) * time_block]

    def body(index, _):
        start = index * UNROLL
        products = []
        for u in range(UNROLL):
            place = pl.multiple_of(cols_ref[step * chunk + start + u] * scen, scen)
            products.append(
                lax.dot_general(
                    flat_ref[pl.ds(place, scen), :].astype(jnp.bfloat16),
                    tiles_ref[start + u],
                    (((1,), (1,)), ((), ())),
                    preferred_element_type=jnp.float32,
                )
            )
        for u in range(UNROLL):
            place = pl.multiple_of(rows_ref[step * chunk + start + u] * scen, scen)
            acc_ref[pl.ds(place, scen), :] += products[u]
        return 0

    lax.fori_loop(0, chunk // UNROLL, body, 0)

    @pl.when(step == pl.num_programs(0) - 1)
    def _():
        out_ref[...] = acc_ref[...].astype(jnp.bfloat16)


def running(values, trailing):
    length = values.shape[0]
    row_iota = lax.broadcasted_iota(jnp.int32, (length, length), 0)
    col_iota = lax.broadcasted_iota(jnp.int32, (length, length), 1)
    keep = (col_iota >= row_iota) if trailing else (row_iota >= col_iota)
    return jnp.dot(
        keep.astype(jnp.float32), values, precision=lax.Precision.HIGHEST, preferred_element_type=jnp.float32
    )


def primal_kernel(dims, first, *refs):
    n_row, n_col, scen_local, time_block, flight_tiles, own_tiles = dims
    if first:
        recv_ref, inc_ref, cost_ref, start_ref, len_ref, inc_out, cum_out, send_ref = refs
    else:
        recv_ref, inc_ref, cum_ref, cost_ref, start_ref, len_ref, inc_out, cum_out, send_ref = refs
    window, flight_local = cost_ref.shape
    side = flight_local // own_tiles
    piece = own_tiles * time_block
    tau_step = 0.6 / math.sqrt(window)
    minutes = lax.broadcasted_iota(jnp.int32, (window, flight_local), 0)
    begin = start_ref[...]
    upper = ((minutes >= begin) & (minutes < begin + len_ref[...])).astype(jnp.float32)
    for j in range(scen_local):
        bands = []
        for h in range(n_col):
            total = recv_ref[h, pl.ds(j * piece, piece), :].astype(jnp.float32)
            for g in range(1, n_row):
                total = total + recv_ref[g * n_col + h, pl.ds(j * piece, piece), :].astype(jnp.float32)
            bands.append(
                jnp.concatenate([total[f * time_block : (f + 1) * time_block] for f in range(own_tiles)], axis=1)
            )
        slope = jnp.concatenate(bands, axis=0) + cost_ref[...]
        gradient = running(slope, True)
        old = inc_ref[j]
        old_sum = running(old, False) if first else cum_ref[j]
        fresh = jnp.clip(old - tau_step * gradient, 0.0, upper)
        inc_out[j] = fresh
        fresh_sum = running(fresh, False)
        cum_out[j] = fresh_sum
        probe = (2.0 * fresh_sum - old_sum).astype(jnp.bfloat16)
        for h in range(n_col):
            band = probe[h * time_block : (h + 1) * time_block]
            block = jnp.concatenate([band[:, f * side : (f + 1) * side] for f in range(own_tiles)], axis=0)
            for g in range(n_row):
                send_ref[g * n_col + h, pl.ds(j * piece, piece), :] = block


def pair_kernel(own_ref, other_ref, out_ref):
    out_ref[...] = (own_ref[...].astype(jnp.float32) + other_ref[...].astype(jnp.float32)).astype(jnp.bfloat16)


def dual_kernel(count, *refs):
    parts, (dual_ref, cap_ref, dual_out, round_out) = refs[:count], refs[count:]
    total = parts[0][...].astype(jnp.float32)
    for part in parts[1:]:
        total = total + part[...].astype(jnp.float32)
    fresh = jnp.maximum(dual_ref[...] + SIGMA_STEP * (total - cap_ref[...].astype(jnp.float32)), 0.0)
    dual_out[...] = fresh
    round_out[...] = fresh.astype(jnp.bfloat16)


def per_device(
    tile_values, tile_rows, tile_cols, increments, dual_vars, flight_cost, win_start, win_len, capacity
):
    n_row, n_col = lax.axis_size("row"), lax.axis_size("col")
    count, side = tile_values.shape[2], tile_values.shape[3]
    scen_local, window, flight_local = increments.shape
    scen, row_length = dual_vars.shape
    row_tiles = row_length // side
    time_block = window // n_col
    flight_tiles = flight_local * n_col // side
    own_tiles = flight_local // side
    col_tiles = time_block * flight_tiles
    dims = (n_row, n_col, scen_local, time_block, flight_tiles, own_tiles)
    devices = n_row * n_col
    message = (devices, scen_local * own_tiles * time_block, side)
    half = row_tiles * scen // 2

    blocks = tile_values.reshape(count, side, side)
    rows, cols = tile_rows.reshape(count), tile_cols.reshape(count)
    core = lax.axis_index("col") % 2
    chunk = min(count, 64)
    flops = 2 * count * scen * side * side

    tile_spec = pl.BlockSpec((chunk, side, side), lambda i, *_: (i, 0, 0))
    cost = pl.CostEstimate(flops=flops, bytes_accessed=2 * count * side * side, transcendentals=0)

    def backward(duals):
        return pl.pallas_call(
            functools.partial(backward_kernel, dims),
            grid_spec=pltpu.PrefetchScalarGridSpec(
                num_scalar_prefetch=2,
                grid=(count // chunk,),
                in_specs=[pl.BlockSpec((row_tiles, scen, side), lambda i, *_: (0, 0, 0)), tile_spec],
                out_specs=pl.BlockSpec(message, lambda i, *_: (0, 0, 0)),
                scratch_shapes=[pltpu.VMEM((col_tiles * scen, side), jnp.float32)],
            ),
            out_shape=jax.ShapeDtypeStruct(message, jnp.bfloat16),
            compiler_params=params(),
            cost_estimate=cost,
            name="backward_products",
        )(rows, cols, duals, blocks)

    def forward(probe):
        return pl.pallas_call(
            functools.partial(forward_kernel, dims),
            grid_spec=pltpu.PrefetchScalarGridSpec(
                num_scalar_prefetch=2,
                grid=(count // chunk,),
                in_specs=[pl.BlockSpec(message, lambda i, *_: (0, 0, 0)), tile_spec],
                out_specs=pl.BlockSpec((row_tiles * scen, side), lambda i, *_: (0, 0)),
                scratch_shapes=[
                    pltpu.VMEM((col_tiles * scen, side), jnp.float32),
                    pltpu.VMEM((row_tiles * scen, side), jnp.float32),
                ],
            ),
            out_shape=jax.ShapeDtypeStruct((row_tiles * scen, side), jnp.bfloat16),
            compiler_params=params(),
            cost_estimate=cost,
            name="forward_products",
        )(rows, cols, probe, blocks)

    def primal_step(recv, primal, cumulative):
        first = cumulative is None
        state = (primal,) if first else (primal, cumulative)
        shape = jax.ShapeDtypeStruct(primal.shape, jnp.float32)
        return pl.pallas_call(
            functools.partial(primal_kernel, dims, first),
            in_specs=[whole_vmem()] * (4 + len(state)),
            out_specs=[whole_vmem()] * 3,
            out_shape=[shape, shape, jax.ShapeDtypeStruct(message, jnp.bfloat16)],
            compiler_params=params(),
            name="primal_update",
        )(recv, *state, flight_cost, win_start.reshape(1, -1), win_len.reshape(1, -1))

    def swap_core(value):
        return lax.ppermute(value, "col", [(i, i ^ 1) for i in range(n_col)])

    def all_chips(value):
        return [
            lax.ppermute(value, "col", [(i, i ^ (2 * d)) for i in range(n_col)]) for d in range(1, n_col // 2)
        ]

    def dual_step(partial, dual, cap):
        own = lax.dynamic_slice_in_dim(partial, core * half, half, 0)
        away = lax.dynamic_slice_in_dim(partial, (1 - core) * half, half, 0)
        pair = pl.pallas_call(
            pair_kernel,
            in_specs=[whole_vmem()] * 2,
            out_specs=whole_vmem(),
            out_shape=jax.ShapeDtypeStruct(own.shape, jnp.bfloat16),
            compiler_params=params(),
            name="core_pair_sum",
        )(own, swap_core(away))
        parts = [pair, *all_chips(pair)]
        return pl.pallas_call(
            functools.partial(dual_kernel, len(parts)),
            in_specs=[whole_vmem()] * (len(parts) + 2),
            out_specs=[whole_vmem()] * 2,
            out_shape=[
                jax.ShapeDtypeStruct(own.shape, jnp.float32),
                jax.ShapeDtypeStruct(own.shape, jnp.bfloat16),
            ],
            compiler_params=params(),
            name="dual_update",
        )(*parts, dual, cap)

    def by_row_block(array):
        return array.reshape(scen, row_tiles, side).transpose(1, 0, 2)

    def both_halves(own):
        other = swap_core(own)
        pieces = jnp.concatenate([jnp.where(core == 0, own, other), jnp.where(core == 0, other, own)], axis=0)
        return pieces.reshape(row_tiles, scen, side)

    rounded = by_row_block(dual_vars.astype(jnp.bfloat16))
    start = core * (row_tiles // 2)
    dual = lax.dynamic_slice_in_dim(by_row_block(dual_vars), start, row_tiles // 2, 0).reshape(half, side)
    cap = lax.dynamic_slice_in_dim(by_row_block(capacity), start, row_tiles // 2, 0).reshape(half, side)
    primal, cumulative = increments, None
    for sweep in range(ITERS):
        recv = lax.all_to_all(backward(rounded), ("row", "col"), 0, 0, tiled=True)
        primal, cumulative, send = primal_step(recv, primal, cumulative)
        probe = lax.all_to_all(send, ("row", "col"), 0, 0, tiled=True)
        dual, half_round = dual_step(forward(probe), dual, cap)
        if sweep + 1 < ITERS:
            rounded = both_halves(half_round)
    duals_out = both_halves(dual).transpose(1, 0, 2).reshape(scen, row_length)
    return (primal, duals_out)


def solution(mesh):
    placed = (
        P("row", "col", None, None, None),
        P("row", "col", None),
        P("row", "col", None),
        P("row", None, "col"),
        P(None, "row"),
        P(None, "col"),
        P("col"),
        P("col"),
        P(None, "row"),
    )
    return jax.shard_map(
        per_device,
        mesh=mesh,
        in_specs=placed,
        out_specs=(P("row", None, "col"), P(None, "row")),
        check_vma=False,
    )
```

```python
import functools
import math

import jax
import jax.numpy as jnp
from jax import lax
from jax.experimental import pallas as pl
from jax.experimental.pallas import tpu as pltpu
from jax.sharding import PartitionSpec as P

ITERS = 2
SIGMA_STEP = 0.2
UNROLL = 32
PITCH_PAD = 8
VMEM_BYTES = 24 * 1024 * 1024
TRANSPOSED = (((1,), (1,)), ((), ()))


def params():
    return pltpu.CompilerParams(vmem_limit_bytes=VMEM_BYTES)


def whole():
    return pl.BlockSpec(memory_space=pltpu.VMEM)


def scalars():
    return pl.BlockSpec(memory_space=pltpu.SMEM)


def stacked_pair(first, second):
    zero = jnp.zeros_like(first)
    return jnp.concatenate(
        [jnp.concatenate([first, zero], axis=1), jnp.concatenate([zero, second], axis=1)], axis=0
    )


def column_place(dims, column, pitch):
    time_block, flight_tiles = dims[3], dims[4]
    return pl.multiple_of((column % flight_tiles * time_block + column // flight_tiles) * pitch, 8)


def backward_blocks(dims, pitch, rows_ref, cols_ref, duals_ref, tiles_ref, acc_ref, start):
    scen = dims[0] * dims[2]
    products = []
    for u in range(0, UNROLL, 2):
        pair = stacked_pair(duals_ref[rows_ref[start + u]], duals_ref[rows_ref[start + u + 1]])
        both = tiles_ref[pl.ds(start + u, 2)]
        result = jnp.dot(pair, both.reshape(-1, both.shape[2]), preferred_element_type=jnp.float32)
        products += [result[:scen], result[scen:]]
    for u in range(UNROLL):
        place = column_place(dims, cols_ref[start + u], pitch)
        acc_ref[pl.ds(place, scen), :] += products[u]


def write_messages(dims, pitch, acc_ref, out_ref):
    n_row, n_col, scen_local, time_block, _, own_tiles = dims
    piece = own_tiles * time_block
    for group in range(n_row):
        for column in range(n_col):
            for j in range(scen_local):
                base = column * own_tiles * time_block * pitch + group * scen_local + j
                parts = [
                    acc_ref[pl.ds(base + f * time_block * pitch, time_block, stride=pitch), :]
                    for f in range(own_tiles)
                ]
                out_ref[group * n_col + column, pl.ds(j * piece, piece), :] = jnp.concatenate(
                    parts, axis=0
                ).astype(jnp.bfloat16)


def first_backward_kernel(dims, pitch, rows_ref, cols_ref, dual_ref, source_ref, out_ref, tiles_ref, duals_ref, acc_ref, sems):
    count, parts = tiles_ref.shape[0], sems.shape[0]
    chunk = count // parts
    copies = [
        pltpu.make_async_copy(source_ref.at[pl.ds(i * chunk, chunk)], tiles_ref.at[pl.ds(i * chunk, chunk)], sems.at[i])
        for i in range(parts)
    ]
    for copy in copies:
        copy.start()
    bands = [dual_ref[a].astype(jnp.bfloat16) for a in range(dual_ref.shape[0])]
    duals_ref[...] = jnp.concatenate(bands, axis=1)
    acc_ref[...] = jnp.zeros_like(acc_ref)

    def body(index, _):
        backward_blocks(dims, pitch, rows_ref, cols_ref, duals_ref, tiles_ref, acc_ref, index * UNROLL)
        return 0

    for i, copy in enumerate(copies):
        copy.wait()
        lax.fori_loop(i * chunk // UNROLL, (i + 1) * chunk // UNROLL, body, 0)
    write_messages(dims, pitch, acc_ref, out_ref)


def backward_kernel(dims, pitch, core_ref, rows_ref, cols_ref, own_ref, other_ref, tiles_ref, out_ref, duals_ref, acc_ref):
    core = core_ref[0]
    half, scen, side = duals_ref.shape[0] // 2, duals_ref.shape[1], duals_ref.shape[2]
    duals_ref[pl.ds(core * half, half)] = own_ref[...].reshape(half, scen, side)
    duals_ref[pl.ds((1 - core) * half, half)] = other_ref[...].reshape(half, scen, side)
    acc_ref[...] = jnp.zeros_like(acc_ref)

    def body(index, _):
        backward_blocks(dims, pitch, rows_ref, cols_ref, duals_ref, tiles_ref, acc_ref, index * UNROLL)
        return 0

    lax.fori_loop(0, tiles_ref.shape[0] // UNROLL, body, 0)
    write_messages(dims, pitch, acc_ref, out_ref)


def forward_kernel(dims, pitch, core_ref, rows_ref, cols_ref, probe_ref, tiles_ref, own_ref, away_ref, flat_ref, acc_ref):
    n_row, n_col, scen_local, time_block, _, own_tiles = dims
    scen = n_row * scen_local
    piece = own_tiles * time_block
    core = core_ref[0]
    acc_ref[...] = jnp.zeros_like(acc_ref)
    for group in range(n_row):
        for column in range(n_col):
            for j in range(scen_local):
                base = column * own_tiles * time_block * pitch + group * scen_local + j
                block = probe_ref[group * n_col + column, pl.ds(j * piece, piece), :].astype(jnp.float32)
                for f in range(own_tiles):
                    flat_ref[pl.ds(base + f * time_block * pitch, time_block, stride=pitch), :] = block[
                        f * time_block : (f + 1) * time_block
                    ]

    def picked(index):
        return flat_ref[pl.ds(column_place(dims, cols_ref[index], pitch), scen), :].astype(jnp.bfloat16)

    def body(index, _):
        start = index * UNROLL
        products = []
        for u in range(0, UNROLL, 2):
            both = jnp.concatenate([tiles_ref[start + u], tiles_ref[start + u + 1]], axis=1)
            result = lax.dot_general(
                stacked_pair(picked(start + u), picked(start + u + 1)),
                both,
                TRANSPOSED,
                preferred_element_type=jnp.float32,
            )
            products += [result[:scen], result[scen:]]
        for u in range(UNROLL):
            place = pl.multiple_of(rows_ref[start + u] * scen, scen)
            acc_ref[pl.ds(place, scen), :] += products[u]
        return 0

    lax.fori_loop(0, tiles_ref.shape[0] // UNROLL, body, 0)
    half = acc_ref.shape[0] // 2
    own_ref[...] = acc_ref[pl.ds(pl.multiple_of(core * half, half), half), :]
    away_ref[...] = acc_ref[pl.ds(pl.multiple_of((1 - core) * half, half), half), :]


def running(values, trailing):
    length = values.shape[0]
    row_iota = lax.broadcasted_iota(jnp.int32, (length, length), 0)
    col_iota = lax.broadcasted_iota(jnp.int32, (length, length), 1)
    keep = (col_iota >= row_iota) if trailing else (row_iota >= col_iota)
    return jnp.dot(
        keep.astype(jnp.float32), values, precision=lax.Precision.HIGHEST, preferred_element_type=jnp.float32
    )


def primal_kernel(dims, first, *refs):
    n_row, n_col, scen_local, time_block, _, own_tiles = dims
    if first:
        recv_ref, inc_ref, cost_ref, start_ref, len_ref, inc_out, cum_out, send_ref = refs
    else:
        recv_ref, inc_ref, cum_ref, cost_ref, start_ref, len_ref, inc_out, cum_out, send_ref = refs
    window, flight_local = cost_ref.shape
    side = flight_local // own_tiles
    piece = own_tiles * time_block
    tau_step = 0.6 / math.sqrt(window)
    minutes = lax.broadcasted_iota(jnp.int32, (window, flight_local), 0)
    begin = start_ref[...]
    upper = ((minutes >= begin) & (minutes < begin + len_ref[...])).astype(jnp.float32)
    for j in range(scen_local):
        bands = []
        for h in range(n_col):
            total = recv_ref[h, pl.ds(j * piece, piece), :].astype(jnp.float32)
            for g in range(1, n_row):
                total = total + recv_ref[g * n_col + h, pl.ds(j * piece, piece), :].astype(jnp.float32)
            bands.append(
                jnp.concatenate([total[f * time_block : (f + 1) * time_block] for f in range(own_tiles)], axis=1)
            )
        slope = jnp.concatenate(bands, axis=0) + cost_ref[...]
        gradient = running(slope, True)
        old = inc_ref[j]
        old_sum = running(old, False) if first else cum_ref[j]
        fresh = jnp.clip(old - tau_step * gradient, 0.0, upper)
        inc_out[j] = fresh
        fresh_sum = running(fresh, False)
        cum_out[j] = fresh_sum
        probe = (2.0 * fresh_sum - old_sum).astype(jnp.bfloat16)
        for h in range(n_col):
            band = probe[h * time_block : (h + 1) * time_block]
            block = jnp.concatenate([band[:, f * side : (f + 1) * side] for f in range(own_tiles)], axis=0)
            for g in range(n_row):
                send_ref[g * n_col + h, pl.ds(j * piece, piece), :] = block


def pair_kernel(own_ref, other_ref, out_ref):
    out_ref[...] = (own_ref[...] + other_ref[...]).astype(jnp.bfloat16)


def dual_kernel(remote, first, core_ref, own_ref, other_ref, *refs):
    parts, (dual_ref, cap_ref, dual_out, round_out) = refs[:remote], refs[remote:]
    total = own_ref[...] + other_ref[...]
    for part in parts:
        total = total + part[...].astype(jnp.float32)
    bands, row_tiles, band, side = cap_ref.shape
    half = row_tiles // 2
    begin = core_ref[0] * half

    def own_half(ref):
        return jnp.concatenate([ref[a, pl.ds(begin, half)] for a in range(bands)], axis=1).reshape(-1, side)

    old = own_half(dual_ref) if first else dual_ref[...]
    fresh = jnp.maximum(old + SIGMA_STEP * (total - own_half(cap_ref).astype(jnp.float32)), 0.0)
    dual_out[...] = fresh
    round_out[...] = fresh.astype(jnp.bfloat16)


def assemble_kernel(core_ref, own_ref, other_ref, out_ref):
    bands, row_tiles, band, side = out_ref.shape
    half = row_tiles // 2
    for ref, begin in ((own_ref, core_ref[0] * half), (other_ref, (1 - core_ref[0]) * half)):
        value = ref[...].reshape(half, bands * band, side)
        for a in range(bands):
            out_ref[a, pl.ds(begin, half)] = value[:, a * band : (a + 1) * band]


def per_device(
    tile_values, tile_rows, tile_cols, increments, dual_vars, flight_cost, win_start, win_len, capacity
):
    n_row, n_col = lax.axis_size("row"), lax.axis_size("col")
    count, side = tile_values.shape[2], tile_values.shape[3]
    scen_local, window, flight_local = increments.shape
    scen, row_length = dual_vars.shape
    row_tiles = row_length // side
    time_block = window // n_col
    flight_tiles = flight_local * n_col // side
    own_tiles = flight_local // side
    col_tiles = time_block * flight_tiles
    dims = (n_row, n_col, scen_local, time_block, flight_tiles, own_tiles)
    message = (n_row * n_col, scen_local * own_tiles * time_block, side)
    half = row_tiles * scen // 2
    pitch = scen + PITCH_PAD
    band = 8

    rows, cols = tile_rows.reshape(count), tile_cols.reshape(count)
    core = (lax.axis_index("col") % 2).reshape(1)
    cost = pl.CostEstimate(flops=2 * count * scen * side * side, bytes_accessed=count * side * side, transcendentals=0)
    acc_cols = pltpu.VMEM((col_tiles * pitch, side), jnp.float32)
    picked_duals = pltpu.VMEM((row_tiles, scen, side), jnp.bfloat16)
    messages = jax.ShapeDtypeStruct(message, jnp.bfloat16)
    half_f32 = jax.ShapeDtypeStruct((half, side), jnp.float32)
    half_bf16 = jax.ShapeDtypeStruct((half, side), jnp.bfloat16)

    def banded(array):
        return array.reshape(scen // band, band, row_tiles, side).transpose(0, 2, 1, 3)

    def first_backward(duals):
        return pl.pallas_call(
            functools.partial(first_backward_kernel, dims, pitch),
            in_specs=[scalars(), scalars(), whole(), pl.BlockSpec(memory_space=pltpu.HBM)],
            out_specs=[whole(), whole()],
            out_shape=[messages, pltpu.VMEM((count, side, side), jnp.bfloat16)],
            scratch_shapes=[picked_duals, acc_cols, pltpu.SemaphoreType.DMA((8,))],
            compiler_params=params(),
            cost_estimate=cost,
            name="first_backward_products",
        )(rows, cols, duals, pltpu.with_memory_space_constraint(tile_values.reshape(count, side, side), pltpu.HBM))

    def backward(own, other, tiles):
        return pl.pallas_call(
            functools.partial(backward_kernel, dims, pitch),
            in_specs=[scalars()] * 3 + [whole()] * 3,
            out_specs=whole(),
            out_shape=messages,
            scratch_shapes=[picked_duals, acc_cols],
            compiler_params=params(),
            cost_estimate=cost,
            name="backward_products",
        )(core, rows, cols, own, other, pltpu.with_memory_space_constraint(tiles, pltpu.VMEM))

    def forward(probe, tiles):
        return pl.pallas_call(
            functools.partial(forward_kernel, dims, pitch),
            in_specs=[scalars()] * 3 + [whole()] * 2,
            out_specs=[whole()] * 2,
            out_shape=[half_f32] * 2,
            scratch_shapes=[acc_cols, pltpu.VMEM((row_tiles * scen, side), jnp.float32)],
            compiler_params=params(),
            cost_estimate=cost,
            name="forward_products",
        )(core, rows, cols, probe, pltpu.with_memory_space_constraint(tiles, pltpu.VMEM))

    def primal_step(recv, primal, cumulative):
        first = cumulative is None
        state = (primal,) if first else (primal, cumulative)
        shape = jax.ShapeDtypeStruct(primal.shape, jnp.float32)
        return pl.pallas_call(
            functools.partial(primal_kernel, dims, first),
            in_specs=[whole()] * (4 + len(state)),
            out_specs=[whole()] * 3,
            out_shape=[shape, shape, messages],
            compiler_params=params(),
            name="primal_update",
        )(recv, *state, flight_cost, win_start.reshape(1, -1), win_len.reshape(1, -1))

    def swap_core(value):
        return lax.ppermute(value, "col", [(i, i ^ 1) for i in range(n_col)])

    def all_chips(value):
        return [
            lax.ppermute(value, "col", [(i, i ^ (2 * d)) for i in range(n_col)]) for d in range(1, n_col // 2)
        ]

    def dual_step(own, away, dual, first):
        other = swap_core(away)
        pair = pl.pallas_call(
            pair_kernel,
            in_specs=[whole()] * 2,
            out_specs=whole(),
            out_shape=half_bf16,
            compiler_params=params(),
            name="core_pair_sum",
        )(own, other)
        parts = all_chips(pair)
        return pl.pallas_call(
            functools.partial(dual_kernel, len(parts), first),
            in_specs=[scalars()] + [whole()] * (len(parts) + 4),
            out_specs=[whole()] * 2,
            out_shape=[half_f32, half_bf16],
            compiler_params=params(),
            name="dual_update",
        )(core, own, other, *parts, dual, banded(capacity))

    def assemble(own):
        return pl.pallas_call(
            assemble_kernel,
            in_specs=[scalars()] + [whole()] * 2,
            out_specs=whole(),
            out_shape=jax.ShapeDtypeStruct((scen // band, row_tiles, band, side), jnp.float32),
            compiler_params=params(),
            name="assemble_duals",
        )(core, own, swap_core(own))

    send, tiles = first_backward(banded(dual_vars))
    dual, primal, cumulative = banded(dual_vars), increments, None
    for sweep in range(ITERS):
        if sweep:
            send = backward(half_round, swap_core(half_round), tiles)
        recv = lax.all_to_all(send, ("row", "col"), 0, 0, tiled=True)
        primal, cumulative, send = primal_step(recv, primal, cumulative)
        probe = lax.all_to_all(send, ("row", "col"), 0, 0, tiled=True)
        own, away = forward(probe, tiles)
        dual, half_round = dual_step(own, away, dual, sweep == 0)
    duals_out = assemble(dual).transpose(0, 2, 1, 3).reshape(scen, row_length)
    return (primal, duals_out)


def solution(mesh):
    placed = (
        P("row", "col", None, None, None),
        P("row", "col", None),
        P("row", "col", None),
        P("row", None, "col"),
        P(None, "row"),
        P(None, "col"),
        P("col"),
        P("col"),
        P(None, "row"),
    )
    return jax.shard_map(
        per_device,
        mesh=mesh,
        in_specs=placed,
        out_specs=(P("row", None, "col"), P(None, "row")),
        check_vma=False,
    )
```

```python
import functools
import math

import jax
import jax.numpy as jnp
from jax import lax
from jax.experimental import pallas as pl
from jax.experimental.pallas import tpu as pltpu
from jax.sharding import PartitionSpec as P

ITERS = 2
SIGMA_STEP = 0.2
UNROLL = 32
PITCH_PAD = 8
VMEM_BYTES = 24 * 1024 * 1024
TRANSPOSED = (((1,), (1,)), ((), ()))


def params():
    return pltpu.CompilerParams(vmem_limit_bytes=VMEM_BYTES)


def whole():
    return pl.BlockSpec(memory_space=pltpu.VMEM)


def scalars():
    return pl.BlockSpec(memory_space=pltpu.SMEM)


def stacked_pair(first, second):
    zero = jnp.zeros_like(first)
    return jnp.concatenate(
        [jnp.concatenate([first, zero], axis=1), jnp.concatenate([zero, second], axis=1)], axis=0
    )


def column_place(dims, column, pitch):
    time_block, flight_tiles = dims[3], dims[4]
    return pl.multiple_of((column % flight_tiles * time_block + column // flight_tiles) * pitch, 8)


def backward_blocks(dims, pitch, rows_ref, cols_ref, duals_ref, tiles_ref, acc_ref, start):
    scen = dims[0] * dims[2]
    products = []
    for u in range(0, UNROLL, 2):
        pair = stacked_pair(duals_ref[rows_ref[start + u]], duals_ref[rows_ref[start + u + 1]])
        both = tiles_ref[pl.ds(start + u, 2)]
        result = jnp.dot(pair, both.reshape(-1, both.shape[2]), preferred_element_type=jnp.float32)
        products += [result[:scen], result[scen:]]
    for u in range(UNROLL):
        place = column_place(dims, cols_ref[start + u], pitch)
        acc_ref[pl.ds(place, scen), :] += products[u]


def write_messages(dims, pitch, acc_ref, out_ref):
    n_row, n_col, scen_local, time_block, _, own_tiles = dims
    piece = own_tiles * time_block
    for group in range(n_row):
        for column in range(n_col):
            for j in range(scen_local):
                base = column * own_tiles * time_block * pitch + group * scen_local + j
                parts = [
                    acc_ref[pl.ds(base + f * time_block * pitch, time_block, stride=pitch), :]
                    for f in range(own_tiles)
                ]
                out_ref[group * n_col + column, pl.ds(j * piece, piece), :] = jnp.concatenate(
                    parts, axis=0
                ).astype(jnp.bfloat16)


def first_backward_kernel(
    dims, pitch, core_ref, row_source, col_source, dual_source, source_ref, out_ref, tiles_ref,
    rows_ref, cols_ref, bands_ref, duals_ref, acc_ref, sems
):
    count, parts = tiles_ref.shape[0], sems.shape[0] - 3
    chunk = count // parts
    lists = [
        pltpu.make_async_copy(row_source, rows_ref, sems.at[parts]),
        pltpu.make_async_copy(col_source, cols_ref, sems.at[parts + 1]),
        pltpu.make_async_copy(dual_source, bands_ref, sems.at[parts + 2]),
    ]
    copies = [
        pltpu.make_async_copy(source_ref.at[pl.ds(i * chunk, chunk)], tiles_ref.at[pl.ds(i * chunk, chunk)], sems.at[i])
        for i in range(parts)
    ]
    for copy in lists + copies:
        copy.start()
    acc_ref[...] = jnp.zeros_like(acc_ref)
    for copy in lists:
        copy.wait()
    bands = [bands_ref[a].astype(jnp.bfloat16) for a in range(bands_ref.shape[0])]
    duals_ref[...] = jnp.concatenate(bands, axis=1)

    def body(index, _):
        backward_blocks(dims, pitch, rows_ref, cols_ref, duals_ref, tiles_ref, acc_ref, index * UNROLL)
        return 0

    for i, copy in enumerate(copies):
        copy.wait()
        lax.fori_loop(i * chunk // UNROLL, (i + 1) * chunk // UNROLL, body, 0)
    write_messages(dims, pitch, acc_ref, out_ref)


def backward_kernel(dims, pitch, core_ref, rows_ref, cols_ref, own_ref, other_ref, tiles_ref, out_ref, duals_ref, acc_ref):
    core = core_ref[0]
    half, scen, side = duals_ref.shape[0] // 2, duals_ref.shape[1], duals_ref.shape[2]
    duals_ref[pl.ds(core * half, half)] = own_ref[...].reshape(half, scen, side)
    duals_ref[pl.ds((1 - core) * half, half)] = other_ref[...].reshape(half, scen, side)
    acc_ref[...] = jnp.zeros_like(acc_ref)

    def body(index, _):
        backward_blocks(dims, pitch, rows_ref, cols_ref, duals_ref, tiles_ref, acc_ref, index * UNROLL)
        return 0

    lax.fori_loop(0, tiles_ref.shape[0] // UNROLL, body, 0)
    write_messages(dims, pitch, acc_ref, out_ref)


def forward_kernel(dims, pitch, core_ref, rows_ref, cols_ref, probe_ref, tiles_ref, own_ref, away_ref, flat_ref, acc_ref):
    n_row, n_col, scen_local, time_block, _, own_tiles = dims
    scen = n_row * scen_local
    piece = own_tiles * time_block
    core = core_ref[0]
    acc_ref[...] = jnp.zeros_like(acc_ref)
    for group in range(n_row):
        for column in range(n_col):
            for j in range(scen_local):
                base = column * own_tiles * time_block * pitch + group * scen_local + j
                block = probe_ref[group * n_col + column, pl.ds(j * piece, piece), :].astype(jnp.float32)
                for f in range(own_tiles):
                    flat_ref[pl.ds(base + f * time_block * pitch, time_block, stride=pitch), :] = block[
                        f * time_block : (f + 1) * time_block
                    ]

    def picked(index):
        return flat_ref[pl.ds(column_place(dims, cols_ref[index], pitch), scen), :].astype(jnp.bfloat16)

    def body(index, _):
        start = index * UNROLL
        products = []
        for u in range(0, UNROLL, 2):
            both = jnp.concatenate([tiles_ref[start + u], tiles_ref[start + u + 1]], axis=1)
            result = lax.dot_general(
                stacked_pair(picked(start + u), picked(start + u + 1)),
                both,
                TRANSPOSED,
                preferred_element_type=jnp.float32,
            )
            products += [result[:scen], result[scen:]]
        for u in range(UNROLL):
            place = pl.multiple_of(rows_ref[start + u] * scen, scen)
            acc_ref[pl.ds(place, scen), :] += products[u]
        return 0

    lax.fori_loop(0, tiles_ref.shape[0] // UNROLL, body, 0)
    half = acc_ref.shape[0] // 2
    own_ref[...] = acc_ref[pl.ds(pl.multiple_of(core * half, half), half), :]
    away_ref[...] = acc_ref[pl.ds(pl.multiple_of((1 - core) * half, half), half), :]


def running(values, trailing):
    length = values.shape[0]
    row_iota = lax.broadcasted_iota(jnp.int32, (length, length), 0)
    col_iota = lax.broadcasted_iota(jnp.int32, (length, length), 1)
    keep = (col_iota >= row_iota) if trailing else (row_iota >= col_iota)
    return jnp.dot(
        keep.astype(jnp.float32), values, precision=lax.Precision.HIGHEST, preferred_element_type=jnp.float32
    )


def primal_kernel(dims, first, *refs):
    n_row, n_col, scen_local, time_block, _, own_tiles = dims
    if first:
        recv_ref, inc_ref, cost_ref, start_ref, len_ref, inc_out, cum_out, send_ref = refs
    else:
        recv_ref, inc_ref, cum_ref, cost_ref, start_ref, len_ref, inc_out, cum_out, send_ref = refs
    window, flight_local = cost_ref.shape
    side = flight_local // own_tiles
    piece = own_tiles * time_block
    tau_step = 0.6 / math.sqrt(window)
    minutes = lax.broadcasted_iota(jnp.int32, (window, flight_local), 0)
    begin = start_ref[...]
    upper = ((minutes >= begin) & (minutes < begin + len_ref[...])).astype(jnp.float32)
    for j in range(scen_local):
        bands = []
        for h in range(n_col):
            total = recv_ref[h, pl.ds(j * piece, piece), :].astype(jnp.float32)
            for g in range(1, n_row):
                total = total + recv_ref[g * n_col + h, pl.ds(j * piece, piece), :].astype(jnp.float32)
            bands.append(
                jnp.concatenate([total[f * time_block : (f + 1) * time_block] for f in range(own_tiles)], axis=1)
            )
        slope = jnp.concatenate(bands, axis=0) + cost_ref[...]
        gradient = running(slope, True)
        old = inc_ref[j]
        old_sum = running(old, False) if first else cum_ref[j]
        fresh = jnp.clip(old - tau_step * gradient, 0.0, upper)
        inc_out[j] = fresh
        fresh_sum = running(fresh, False)
        cum_out[j] = fresh_sum
        probe = (2.0 * fresh_sum - old_sum).astype(jnp.bfloat16)
        for h in range(n_col):
            band = probe[h * time_block : (h + 1) * time_block]
            block = jnp.concatenate([band[:, f * side : (f + 1) * side] for f in range(own_tiles)], axis=0)
            for g in range(n_row):
                send_ref[g * n_col + h, pl.ds(j * piece, piece), :] = block


def sum_kernel(*refs):
    total = refs[0][...].astype(jnp.float32)
    for ref in refs[1:-1]:
        total = total + ref[...].astype(jnp.float32)
    refs[-1][...] = total.astype(jnp.bfloat16)


def pair_kernel(own_ref, other_ref, *outs):
    rows = outs[0].shape[0]
    for i, out_ref in enumerate(outs):
        piece = pl.ds(i * rows, rows)
        out_ref[...] = (own_ref[piece, :] + other_ref[piece, :]).astype(jnp.bfloat16)


def dual_kernel(split, remote, first, core_ref, own_ref, other_ref, *refs):
    parts, (dual_ref, cap_ref, dual_out, round_out) = refs[: split * remote], refs[split * remote :]
    total = own_ref[...] + other_ref[...]
    for r in range(remote):
        piece = [part[...].astype(jnp.float32) for part in parts[r * split : (r + 1) * split]]
        total = total + jnp.concatenate(piece, axis=0)
    bands, row_tiles, band, side = cap_ref.shape
    half = row_tiles // 2
    begin = core_ref[0] * half

    def own_half(ref):
        return jnp.concatenate([ref[a, pl.ds(begin, half)] for a in range(bands)], axis=1).reshape(-1, side)

    old = own_half(dual_ref) if first else dual_ref[...]
    fresh = jnp.maximum(old + SIGMA_STEP * (total - own_half(cap_ref).astype(jnp.float32)), 0.0)
    dual_out[...] = fresh
    round_out[...] = fresh.astype(jnp.bfloat16)


def assemble_kernel(core_ref, own_ref, other_ref, out_ref):
    bands, row_tiles, band, side = out_ref.shape
    half = row_tiles // 2
    for ref, begin in ((own_ref, core_ref[0] * half), (other_ref, (1 - core_ref[0]) * half)):
        value = ref[...].reshape(half, bands * band, side)
        for a in range(bands):
            out_ref[a, pl.ds(begin, half)] = value[:, a * band : (a + 1) * band]


def per_device(
    tile_values, tile_rows, tile_cols, increments, dual_vars, flight_cost, win_start, win_len, capacity
):
    n_row, n_col = lax.axis_size("row"), lax.axis_size("col")
    count, side = tile_values.shape[2], tile_values.shape[3]
    scen_local, window, flight_local = increments.shape
    scen, row_length = dual_vars.shape
    row_tiles = row_length // side
    time_block = window // n_col
    flight_tiles = flight_local * n_col // side
    own_tiles = flight_local // side
    col_tiles = time_block * flight_tiles
    dims = (n_row, n_col, scen_local, time_block, flight_tiles, own_tiles)
    message = (n_row * n_col, scen_local * own_tiles * time_block, side)
    half = row_tiles * scen // 2
    pitch = scen + PITCH_PAD
    band = 8

    rows, cols = tile_rows.reshape(count), tile_cols.reshape(count)
    core = (lax.axis_index("col") % 2).reshape(1)
    cost = pl.CostEstimate(flops=2 * count * scen * side * side, bytes_accessed=count * side * side, transcendentals=0)
    acc_cols = pltpu.VMEM((col_tiles * pitch, side), jnp.float32)
    picked_duals = pltpu.VMEM((row_tiles, scen, side), jnp.bfloat16)
    messages = jax.ShapeDtypeStruct(message, jnp.bfloat16)
    half_f32 = jax.ShapeDtypeStruct((half, side), jnp.float32)
    half_bf16 = jax.ShapeDtypeStruct((half, side), jnp.bfloat16)

    def banded(array):
        return array.reshape(scen // band, band, row_tiles, side).transpose(0, 2, 1, 3)

    def in_hbm(array):
        return pltpu.with_memory_space_constraint(array, pltpu.HBM)

    def first_backward(duals):
        return pl.pallas_call(
            functools.partial(first_backward_kernel, dims, pitch),
            in_specs=[scalars()] + [pl.BlockSpec(memory_space=pltpu.HBM)] * 4,
            out_specs=[whole(), whole()],
            out_shape=[messages, pltpu.VMEM((count, side, side), jnp.bfloat16)],
            scratch_shapes=[
                pltpu.SMEM((count,), jnp.int32),
                pltpu.SMEM((count,), jnp.int32),
                pltpu.VMEM(duals.shape, jnp.float32),
                picked_duals,
                acc_cols,
                pltpu.SemaphoreType.DMA((8 + 3,)),
            ],
            compiler_params=params(),
            cost_estimate=cost,
            name="first_backward_products",
        )(core, in_hbm(rows), in_hbm(cols), in_hbm(duals), in_hbm(tile_values.reshape(count, side, side)))

    def backward(own, other, tiles):
        return pl.pallas_call(
            functools.partial(backward_kernel, dims, pitch),
            in_specs=[scalars()] * 3 + [whole()] * 3,
            out_specs=whole(),
            out_shape=messages,
            scratch_shapes=[picked_duals, acc_cols],
            compiler_params=params(),
            cost_estimate=cost,
            name="backward_products",
        )(core, rows, cols, own, other, pltpu.with_memory_space_constraint(tiles, pltpu.VMEM))

    def forward(probe, tiles):
        return pl.pallas_call(
            functools.partial(forward_kernel, dims, pitch),
            in_specs=[scalars()] * 3 + [whole()] * 2,
            out_specs=[whole()] * 2,
            out_shape=[half_f32] * 2,
            scratch_shapes=[acc_cols, pltpu.VMEM((row_tiles * scen, side), jnp.float32)],
            compiler_params=params(),
            cost_estimate=cost,
            name="forward_products",
        )(core, rows, cols, probe, pltpu.with_memory_space_constraint(tiles, pltpu.VMEM))

    def primal_step(recv, primal, cumulative):
        first = cumulative is None
        state = (primal,) if first else (primal, cumulative)
        shape = jax.ShapeDtypeStruct(primal.shape, jnp.float32)
        return pl.pallas_call(
            functools.partial(primal_kernel, dims, first),
            in_specs=[whole()] * (4 + len(state)),
            out_specs=[whole()] * 3,
            out_shape=[shape, shape, messages],
            compiler_params=params(),
            name="primal_update",
        )(recv, *state, flight_cost, win_start.reshape(1, -1), win_len.reshape(1, -1))

    def swap_core(value):
        return lax.ppermute(value, "col", [(i, i ^ 1) for i in range(n_col)])

    def swap_chip(value, bit):
        return lax.ppermute(value, "col", [(i, i ^ (2 << bit)) for i in range(n_col)])

    def dual_step(own, away, dual, first):
        bits = (n_col // 2).bit_length() - 1
        split = min(bits, 2)
        piece = jax.ShapeDtypeStruct((half // split, side), jnp.bfloat16)
        other = swap_core(away)
        sums = pl.pallas_call(
            pair_kernel,
            in_specs=[whole()] * 2,
            out_specs=[whole()] * split,
            out_shape=[piece] * split,
            compiler_params=params(),
            name="core_pair_sum",
        )(own, other)
        parts = []
        for step in range(bits):
            got = [swap_chip(sums[i], (step + i) % bits) for i in range(split)]
            parts += got
            if step + 1 < bits:
                sums = [
                    pl.pallas_call(
                        sum_kernel,
                        in_specs=[whole()] * 2,
                        out_specs=whole(),
                        out_shape=piece,
                        compiler_params=params(),
                        name="chip_sum",
                    )(sums[i], got[i])
                    for i in range(split)
                ]
        return pl.pallas_call(
            functools.partial(dual_kernel, split, bits, first),
            in_specs=[scalars()] + [whole()] * (len(parts) + 4),
            out_specs=[whole()] * 2,
            out_shape=[half_f32, half_bf16],
            compiler_params=params(),
            name="dual_update",
        )(core, own, other, *parts, dual, banded(capacity))

    def assemble(own):
        return pl.pallas_call(
            assemble_kernel,
            in_specs=[scalars()] + [whole()] * 2,
            out_specs=whole(),
            out_shape=jax.ShapeDtypeStruct((scen // band, row_tiles, band, side), jnp.float32),
            compiler_params=params(),
            name="assemble_duals",
        )(core, own, swap_core(own))

    send, tiles = first_backward(banded(dual_vars))
    dual, primal, cumulative = banded(dual_vars), increments, None
    for sweep in range(ITERS):
        if sweep:
            send = backward(half_round, swap_core(half_round), tiles)
        recv = lax.all_to_all(send, ("row", "col"), 0, 0, tiled=True)
        primal, cumulative, send = primal_step(recv, primal, cumulative)
        probe = lax.all_to_all(send, ("row", "col"), 0, 0, tiled=True)
        own, away = forward(probe, tiles)
        dual, half_round = dual_step(own, away, dual, sweep == 0)
    duals_out = assemble(dual).transpose(0, 2, 1, 3).reshape(scen, row_length)
    return (primal, duals_out)


def solution(mesh):
    placed = (
        P("row", "col", None, None, None),
        P("row", "col", None),
        P("row", "col", None),
        P("row", None, "col"),
        P(None, "row"),
        P(None, "col"),
        P("col"),
        P("col"),
        P(None, "row"),
    )
    return jax.shard_map(
        per_device,
        mesh=mesh,
        in_specs=placed,
        out_specs=(P("row", None, "col"), P(None, "row")),
        check_vma=False,
    )
```

```python
import functools
import math

import jax
import jax.numpy as jnp
from jax import lax
from jax.experimental import pallas as pl
from jax.experimental.pallas import tpu as pltpu
from jax.sharding import PartitionSpec as P

ITERS = 2
SIGMA_STEP = 0.2
UNROLL = 64
PITCH_PAD = 8
VMEM_BYTES = 24 * 1024 * 1024
TRANSPOSED = (((1,), (1,)), ((), ()))


def params():
    return pltpu.CompilerParams(vmem_limit_bytes=VMEM_BYTES)


def whole():
    return pl.BlockSpec(memory_space=pltpu.VMEM)


def scalars():
    return pl.BlockSpec(memory_space=pltpu.SMEM)


def stacked_pair(first, second):
    zero = jnp.zeros_like(first)
    return jnp.concatenate(
        [jnp.concatenate([first, zero], axis=1), jnp.concatenate([zero, second], axis=1)], axis=0
    )


def column_place(dims, column, pitch):
    time_block, flight_tiles = dims[3], dims[4]
    return pl.multiple_of((column % flight_tiles * time_block + column // flight_tiles) * pitch, 8)


def backward_blocks(dims, pitch, rows_ref, cols_ref, duals_ref, tiles_ref, acc_ref, start):
    scen = dims[0] * dims[2]
    products = []
    for u in range(0, UNROLL, 2):
        pair = stacked_pair(duals_ref[rows_ref[start + u]], duals_ref[rows_ref[start + u + 1]])
        both = tiles_ref[pl.ds(start + u, 2)]
        result = jnp.dot(pair, both.reshape(-1, both.shape[2]), preferred_element_type=jnp.float32)
        products += [result[:scen], result[scen:]]
    for u in range(UNROLL):
        place = column_place(dims, cols_ref[start + u], pitch)
        acc_ref[pl.ds(place, scen), :] += products[u]


def write_messages(dims, pitch, acc_ref, out_ref):
    n_row, n_col, scen_local, time_block, _, own_tiles = dims
    piece = own_tiles * time_block
    for group in range(n_row):
        for column in range(n_col):
            for j in range(scen_local):
                base = column * own_tiles * time_block * pitch + group * scen_local + j
                parts = [
                    acc_ref[pl.ds(base + f * time_block * pitch, time_block, stride=pitch), :]
                    for f in range(own_tiles)
                ]
                out_ref[group * n_col + column, pl.ds(j * piece, piece), :] = jnp.concatenate(
                    parts, axis=0
                ).astype(jnp.bfloat16)


def first_backward_kernel(
    dims, pitch, core_ref, row_source, col_source, dual_source, source_ref, out_ref, tiles_ref,
    rows_ref, cols_ref, bands_ref, duals_ref, acc_ref, sems
):
    count, parts = tiles_ref.shape[0], sems.shape[0] - 3
    chunk = count // parts
    lists = [
        pltpu.make_async_copy(row_source, rows_ref, sems.at[parts]),
        pltpu.make_async_copy(col_source, cols_ref, sems.at[parts + 1]),
        pltpu.make_async_copy(dual_source, bands_ref, sems.at[parts + 2]),
    ]
    copies = [
        pltpu.make_async_copy(source_ref.at[pl.ds(i * chunk, chunk)], tiles_ref.at[pl.ds(i * chunk, chunk)], sems.at[i])
        for i in range(parts)
    ]
    for copy in lists + copies:
        copy.start()
    acc_ref[...] = jnp.zeros_like(acc_ref)
    for copy in lists:
        copy.wait()
    bands = [bands_ref[a].astype(jnp.bfloat16) for a in range(bands_ref.shape[0])]
    duals_ref[...] = jnp.concatenate(bands, axis=1)

    def body(index, _):
        backward_blocks(dims, pitch, rows_ref, cols_ref, duals_ref, tiles_ref, acc_ref, index * UNROLL)
        return 0

    for i, copy in enumerate(copies):
        copy.wait()
        lax.fori_loop(i * chunk // UNROLL, (i + 1) * chunk // UNROLL, body, 0)
    write_messages(dims, pitch, acc_ref, out_ref)


def backward_kernel(dims, pitch, core_ref, rows_ref, cols_ref, own_ref, other_ref, tiles_ref, out_ref, duals_ref, acc_ref):
    core = core_ref[0]
    half, scen, side = duals_ref.shape[0] // 2, duals_ref.shape[1], duals_ref.shape[2]
    duals_ref[pl.ds(core * half, half)] = own_ref[...].reshape(half, scen, side)
    duals_ref[pl.ds((1 - core) * half, half)] = other_ref[...].reshape(half, scen, side)
    acc_ref[...] = jnp.zeros_like(acc_ref)

    def body(index, _):
        backward_blocks(dims, pitch, rows_ref, cols_ref, duals_ref, tiles_ref, acc_ref, index * UNROLL)
        return 0

    lax.fori_loop(0, tiles_ref.shape[0] // UNROLL, body, 0)
    write_messages(dims, pitch, acc_ref, out_ref)


def forward_kernel(dims, pitch, core_ref, rows_ref, cols_ref, probe_ref, tiles_ref, own_ref, away_ref, flat_ref, acc_ref):
    n_row, n_col, scen_local, time_block, _, own_tiles = dims
    scen = n_row * scen_local
    piece = own_tiles * time_block
    core = core_ref[0]
    acc_ref[...] = jnp.zeros_like(acc_ref)
    for group in range(n_row):
        for column in range(n_col):
            for j in range(scen_local):
                base = column * own_tiles * time_block * pitch + group * scen_local + j
                block = probe_ref[group * n_col + column, pl.ds(j * piece, piece), :].astype(jnp.float32)
                for f in range(own_tiles):
                    flat_ref[pl.ds(base + f * time_block * pitch, time_block, stride=pitch), :] = block[
                        f * time_block : (f + 1) * time_block
                    ]

    def picked(index):
        return flat_ref[pl.ds(column_place(dims, cols_ref[index], pitch), scen), :].astype(jnp.bfloat16)

    def body(index, _):
        start = index * UNROLL
        products = []
        for u in range(0, UNROLL, 2):
            both = jnp.concatenate([tiles_ref[start + u], tiles_ref[start + u + 1]], axis=1)
            result = lax.dot_general(
                stacked_pair(picked(start + u), picked(start + u + 1)),
                both,
                TRANSPOSED,
                preferred_element_type=jnp.float32,
            )
            products += [result[:scen], result[scen:]]
        for u in range(UNROLL):
            place = pl.multiple_of(rows_ref[start + u] * scen, scen)
            acc_ref[pl.ds(place, scen), :] += products[u]
        return 0

    lax.fori_loop(0, tiles_ref.shape[0] // UNROLL, body, 0)
    half = acc_ref.shape[0] // 2
    own_ref[...] = acc_ref[pl.ds(pl.multiple_of(core * half, half), half), :]
    away_ref[...] = acc_ref[pl.ds(pl.multiple_of((1 - core) * half, half), half), :]


def running(values, trailing, terms):
    length = values.shape[0]
    row_iota = lax.broadcasted_iota(jnp.int32, (length, length), 0)
    col_iota = lax.broadcasted_iota(jnp.int32, (length, length), 1)
    keep = ((col_iota >= row_iota) if trailing else (row_iota >= col_iota)).astype(jnp.float32).astype(jnp.bfloat16)
    total = None
    for _ in range(terms):
        term = values.astype(jnp.bfloat16)
        values = values - term.astype(jnp.float32)
        part = jnp.dot(keep, term, preferred_element_type=jnp.float32)
        total = part if total is None else total + part
    return total


def primal_kernel(dims, first, last, *refs):
    n_row, n_col, scen_local, time_block, _, own_tiles = dims
    refs = list(refs)
    recv_ref, inc_ref = refs[:2]
    cum_ref = None if first else refs[2]
    cost_ref, start_ref, len_ref, inc_out, send_ref = refs[2 + (not first) :][:5]
    cum_out = None if last else refs[-1]
    window, flight_local = cost_ref.shape
    side = flight_local // own_tiles
    piece = own_tiles * time_block
    tau_step = 0.6 / math.sqrt(window)
    minutes = lax.broadcasted_iota(jnp.int32, (window, flight_local), 0)
    begin = start_ref[...]
    upper = ((minutes >= begin) & (minutes < begin + len_ref[...])).astype(jnp.float32)
    slopes = []
    for j in range(scen_local):
        bands = []
        for h in range(n_col):
            total = recv_ref[h, pl.ds(j * piece, piece), :].astype(jnp.float32)
            for g in range(1, n_row):
                total = total + recv_ref[g * n_col + h, pl.ds(j * piece, piece), :].astype(jnp.float32)
            bands.append(
                jnp.concatenate([total[f * time_block : (f + 1) * time_block] for f in range(own_tiles)], axis=1)
            )
        slopes.append(jnp.concatenate(bands, axis=0) + cost_ref[...])
    gradient = running(jnp.concatenate(slopes, axis=1), True, 2)
    old = jnp.concatenate([inc_ref[j] for j in range(scen_local)], axis=1)
    if first:
        old_sum = running(old, False, 3)
    else:
        old_sum = jnp.concatenate([cum_ref[j] for j in range(scen_local)], axis=1)
    fresh = jnp.clip(old - tau_step * gradient, 0.0, jnp.concatenate([upper] * scen_local, axis=1))
    fresh_sum = running(fresh, False, 3)
    probe = (2.0 * fresh_sum - old_sum).astype(jnp.bfloat16)
    for j in range(scen_local):
        lanes = slice(j * flight_local, (j + 1) * flight_local)
        inc_out[j] = fresh[:, lanes]
        if not last:
            cum_out[j] = fresh_sum[:, lanes]
        for h in range(n_col):
            band = probe[h * time_block : (h + 1) * time_block, lanes]
            block = jnp.concatenate([band[:, f * side : (f + 1) * side] for f in range(own_tiles)], axis=0)
            for g in range(n_row):
                send_ref[g * n_col + h, pl.ds(j * piece, piece), :] = block


def sum_kernel(first_ref, second_ref, out_ref):
    out_ref[...] = (first_ref[...].astype(jnp.float32) + second_ref[...].astype(jnp.float32)).astype(jnp.bfloat16)


def dual_kernel(remote, first, last, core_ref, own_ref, other_ref, *refs):
    parts, (dual_ref, cap_ref, dual_out) = refs[:remote], refs[remote : remote + 3]
    total = own_ref[...] + other_ref[...]
    for part in parts:
        total = total + part[...].astype(jnp.float32)
    bands, row_tiles, band, side = cap_ref.shape
    half = row_tiles // 2
    begin = core_ref[0] * half

    def own_half(ref):
        return jnp.concatenate([ref[a, pl.ds(begin, half)] for a in range(bands)], axis=1).reshape(-1, side)

    old = own_half(dual_ref) if first else dual_ref[...]
    fresh = jnp.maximum(old + SIGMA_STEP * (total - own_half(cap_ref).astype(jnp.float32)), 0.0)
    dual_out[...] = fresh
    if not last:
        refs[-1][...] = fresh.astype(jnp.bfloat16)


def assemble_kernel(core_ref, own_ref, other_ref, out_ref):
    bands, row_tiles, band, side = out_ref.shape
    half = row_tiles // 2
    for ref, begin in ((own_ref, core_ref[0] * half), (other_ref, (1 - core_ref[0]) * half)):
        value = ref[...].reshape(half, bands * band, side)
        for a in range(bands):
            out_ref[a, pl.ds(begin, half)] = value[:, a * band : (a + 1) * band]


def per_device(
    tile_values, tile_rows, tile_cols, increments, dual_vars, flight_cost, win_start, win_len, capacity
):
    n_row, n_col = lax.axis_size("row"), lax.axis_size("col")
    count, side = tile_values.shape[2], tile_values.shape[3]
    scen_local, window, flight_local = increments.shape
    scen, row_length = dual_vars.shape
    row_tiles = row_length // side
    time_block = window // n_col
    flight_tiles = flight_local * n_col // side
    own_tiles = flight_local // side
    col_tiles = time_block * flight_tiles
    dims = (n_row, n_col, scen_local, time_block, flight_tiles, own_tiles)
    message = (n_row * n_col, scen_local * own_tiles * time_block, side)
    half = row_tiles * scen // 2
    pitch = scen + PITCH_PAD
    band = 8

    rows, cols = tile_rows.reshape(count), tile_cols.reshape(count)
    core = (lax.axis_index("col") % 2).reshape(1)
    cost = pl.CostEstimate(flops=2 * count * scen * side * side, bytes_accessed=count * side * side, transcendentals=0)
    acc_cols = pltpu.VMEM((col_tiles * pitch, side), jnp.float32)
    picked_duals = pltpu.VMEM((row_tiles, scen, side), jnp.bfloat16)
    messages = jax.ShapeDtypeStruct(message, jnp.bfloat16)
    half_f32 = jax.ShapeDtypeStruct((half, side), jnp.float32)
    half_bf16 = jax.ShapeDtypeStruct((half, side), jnp.bfloat16)

    def banded(array):
        return array.reshape(scen // band, band, row_tiles, side).transpose(0, 2, 1, 3)

    def in_hbm(array):
        return pltpu.with_memory_space_constraint(array, pltpu.HBM)

    def first_backward(duals):
        return pl.pallas_call(
            functools.partial(first_backward_kernel, dims, pitch),
            in_specs=[scalars()] + [pl.BlockSpec(memory_space=pltpu.HBM)] * 4,
            out_specs=[whole(), whole()],
            out_shape=[messages, pltpu.VMEM((count, side, side), jnp.bfloat16)],
            scratch_shapes=[
                pltpu.SMEM((count,), jnp.int32),
                pltpu.SMEM((count,), jnp.int32),
                pltpu.VMEM(duals.shape, jnp.float32),
                picked_duals,
                acc_cols,
                pltpu.SemaphoreType.DMA((count // UNROLL + 3,)),
            ],
            compiler_params=params(),
            cost_estimate=cost,
            name="first_backward_products",
        )(core, in_hbm(rows), in_hbm(cols), in_hbm(duals), in_hbm(tile_values.reshape(count, side, side)))

    def backward(own, other, tiles):
        return pl.pallas_call(
            functools.partial(backward_kernel, dims, pitch),
            in_specs=[scalars()] * 3 + [whole()] * 3,
            out_specs=whole(),
            out_shape=messages,
            scratch_shapes=[picked_duals, acc_cols],
            compiler_params=params(),
            cost_estimate=cost,
            name="backward_products",
        )(core, rows, cols, own, other, pltpu.with_memory_space_constraint(tiles, pltpu.VMEM))

    def forward(probe, tiles):
        return pl.pallas_call(
            functools.partial(forward_kernel, dims, pitch),
            in_specs=[scalars()] * 3 + [whole()] * 2,
            out_specs=[whole()] * 2,
            out_shape=[half_f32] * 2,
            scratch_shapes=[acc_cols, pltpu.VMEM((row_tiles * scen, side), jnp.float32)],
            compiler_params=params(),
            cost_estimate=cost,
            name="forward_products",
        )(core, rows, cols, probe, pltpu.with_memory_space_constraint(tiles, pltpu.VMEM))

    def primal_step(recv, primal, cumulative, last):
        first = cumulative is None
        state = (primal,) if first else (primal, cumulative)
        shape = jax.ShapeDtypeStruct(primal.shape, jnp.float32)
        out_shape = [shape, messages] if last else [shape, messages, shape]
        return pl.pallas_call(
            functools.partial(primal_kernel, dims, first, last),
            in_specs=[whole()] * (4 + len(state)),
            out_specs=[whole()] * len(out_shape),
            out_shape=out_shape,
            compiler_params=params(),
            name="primal_update",
        )(recv, *state, flight_cost, win_start.reshape(1, -1), win_len.reshape(1, -1))

    def swap_core(value):
        return lax.ppermute(value, "col", [(i, i ^ 1) for i in range(n_col)])

    bits = (n_col // 2).bit_length() - 1

    def swap_chip(value, step):
        return lax.ppermute(value, "col", [(i, i ^ (2 << (step + i % 2) % bits)) for i in range(n_col)])

    def bf16_sum(first, second, name):
        return pl.pallas_call(
            sum_kernel,
            in_specs=[whole()] * 2,
            out_specs=whole(),
            out_shape=half_bf16,
            compiler_params=params(),
            name=name,
        )(first, second)

    def dual_step(own, away, dual, first, last):
        other = swap_core(away)
        partial = bf16_sum(own, other, "core_pair_sum")
        parts = []
        for step in range(bits):
            parts.append(swap_chip(partial, step))
            if step + 1 < bits:
                partial = bf16_sum(partial, parts[-1], "chip_sum")
        out_shape = [half_f32] if last else [half_f32, half_bf16]
        return pl.pallas_call(
            functools.partial(dual_kernel, bits, first, last),
            in_specs=[scalars()] + [whole()] * (bits + 4),
            out_specs=[whole()] * len(out_shape),
            out_shape=out_shape,
            compiler_params=params(),
            name="dual_update",
        )(core, own, other, *parts, dual, banded(capacity))

    def assemble(own):
        return pl.pallas_call(
            assemble_kernel,
            in_specs=[scalars()] + [whole()] * 2,
            out_specs=whole(),
            out_shape=jax.ShapeDtypeStruct((scen // band, row_tiles, band, side), jnp.float32),
            compiler_params=params(),
            name="assemble_duals",
        )(core, own, swap_core(own))

    send, tiles = first_backward(banded(dual_vars))
    dual, primal, cumulative = banded(dual_vars), increments, None
    for sweep in range(ITERS):
        last = sweep + 1 == ITERS
        if sweep:
            send = backward(half_round, swap_core(half_round), tiles)
        recv = lax.all_to_all(send, ("row", "col"), 0, 0, tiled=True)
        primal, send, *cumulative = primal_step(recv, primal, cumulative, last)
        cumulative = None if last else cumulative[0]
        probe = lax.all_to_all(send, ("row", "col"), 0, 0, tiled=True)
        own, away = forward(probe, tiles)
        dual, *rounded = dual_step(own, away, dual, sweep == 0, last)
        half_round = None if last else rounded[0]
    duals_out = assemble(dual).transpose(0, 2, 1, 3).reshape(scen, row_length)
    return (primal, duals_out)


def solution(mesh):
    placed = (
        P("row", "col", None, None, None),
        P("row", "col", None),
        P("row", "col", None),
        P("row", None, "col"),
        P(None, "row"),
        P(None, "col"),
        P("col"),
        P("col"),
        P(None, "row"),
    )
    return jax.shard_map(
        per_device,
        mesh=mesh,
        in_specs=placed,
        out_specs=(P("row", None, "col"), P(None, "row")),
        check_vma=False,
    )
```

```python
import functools
import math

import jax
import jax.numpy as jnp
from jax import lax
from jax.experimental import pallas as pl
from jax.experimental.pallas import tpu as pltpu
from jax.sharding import PartitionSpec as P

ITERS = 2
SIGMA_STEP = 0.2
PARTS = 2
WIDE = 64
NARROW = 16
FIRST = 32
PITCH_PAD = 8
VMEM_BYTES = 24 * 1024 * 1024
TRANSPOSED = (((1,), (1,)), ((), ()))


def params():
    return pltpu.CompilerParams(vmem_limit_bytes=VMEM_BYTES)


def whole():
    return pl.BlockSpec(memory_space=pltpu.VMEM)


def scalars():
    return pl.BlockSpec(memory_space=pltpu.SMEM)


def stacked_pair(first, second):
    zero = jnp.zeros_like(first)
    return jnp.concatenate(
        [jnp.concatenate([first, zero], axis=1), jnp.concatenate([zero, second], axis=1)], axis=0
    )


def column_place(dims, column):
    time_block, flight_tiles = dims[3], dims[4]
    return column % flight_tiles * time_block + column // flight_tiles


def list_size(count):
    return PARTS * 3 * (count + NARROW) + PARTS


def list_base(count, part, field):
    return (part * 3 + field) * (count + NARROW)


def over_list(count, part, lists_ref, body):
    def entry(field, index):
        return lists_ref[list_base(count, part, field) + index]

    total = lists_ref[list_base(count, PARTS, 0) + part]
    wide = total // WIDE

    def wide_body(index, _):
        body(entry, index * WIDE, WIDE)
        return 0

    def narrow_body(index, _):
        body(entry, wide * WIDE + index * NARROW, NARROW)
        return 0

    lax.fori_loop(0, wide, wide_body, 0)
    lax.fori_loop(0, (total - wide * WIDE + NARROW - 1) // NARROW, narrow_body, 0)


def row_part(core, part, quarter):
    return (core * PARTS + part) * quarter


def backward_blocks(scen, pitch, width, entry, start, duals_ref, tiles_ref, acc_ref):
    products = []
    for u in range(0, width, 2):
        block, row, _ = entry(start + u)
        next_block, next_row, _ = entry(start + u + 1)
        result = jnp.dot(
            stacked_pair(duals_ref[row], duals_ref[next_row]),
            jnp.concatenate([tiles_ref[block], tiles_ref[next_block]], axis=0),
            preferred_element_type=jnp.float32,
        )
        products += [result[:scen], result[scen:]]
    for u in range(width):
        place = pl.multiple_of(entry(start + u)[2] * pitch, 8)
        acc_ref[pl.ds(place, scen), :] += products[u]


def write_messages(dims, pitch, acc_ref, out_ref):
    n_row, n_col, scen_local, time_block, _, own_tiles = dims
    piece = own_tiles * time_block
    for group in range(n_row):
        for column in range(n_col):
            for j in range(scen_local):
                base = column * own_tiles * time_block * pitch + group * scen_local + j
                parts = [
                    acc_ref[pl.ds(base + f * time_block * pitch, time_block, stride=pitch), :]
                    for f in range(own_tiles)
                ]
                out_ref[group * n_col + column, pl.ds(j * piece, piece), :] = jnp.concatenate(
                    parts, axis=0
                ).astype(jnp.bfloat16)


def first_backward_kernel(
    dims, pitch, core_ref, row_source, col_source, dual_source, source_ref, out_ref, tiles_ref, lists_ref,
    rows_ref, cols_ref, bands_ref, duals_ref, acc_ref, sems
):
    scen = dims[0] * dims[2]
    count, pieces = tiles_ref.shape[0], sems.shape[0] - 3
    chunk = count // pieces
    quarter = duals_ref.shape[0] // (2 * PARTS)
    lists = [
        pltpu.make_async_copy(row_source, rows_ref, sems.at[pieces]),
        pltpu.make_async_copy(col_source, cols_ref, sems.at[pieces + 1]),
        pltpu.make_async_copy(dual_source, bands_ref, sems.at[pieces + 2]),
    ]
    copies = [
        pltpu.make_async_copy(source_ref.at[pl.ds(i * chunk, chunk)], tiles_ref.at[pl.ds(i * chunk, chunk)], sems.at[i])
        for i in range(pieces)
    ]
    for copy in lists + copies:
        copy.start()
    acc_ref[...] = jnp.zeros_like(acc_ref)
    for copy in lists:
        copy.wait()
    bands = [bands_ref[a].astype(jnp.bfloat16) for a in range(bands_ref.shape[0])]
    duals_ref[...] = jnp.concatenate(bands, axis=1)

    def put(part, index, block, row, place):
        base = part * 3 * (count + NARROW) + index
        lists_ref[base] = block
        lists_ref[base + count + NARROW] = row
        lists_ref[base + 2 * (count + NARROW)] = place

    def body(index, totals):
        start = index * FIRST

        def entry(block):
            return block, rows_ref[block], column_place(dims, cols_ref[block])

        backward_blocks(scen, pitch, FIRST, entry, start, duals_ref, tiles_ref, acc_ref)
        zero, one = totals
        for u in range(FIRST):
            block, row, place = entry(start + u)
            part = row // quarter % PARTS
            put(part, jnp.where(part == 0, zero, one), block, row, place)
            zero, one = zero + 1 - part, one + part
        return zero, one

    totals = (jnp.int32(0), jnp.int32(0))
    for i, copy in enumerate(copies):
        copy.wait()
        totals = lax.fori_loop(i * chunk // FIRST, (i + 1) * chunk // FIRST, body, totals)
    for part in range(PARTS):
        lists_ref[list_base(count, PARTS, 0) + part] = totals[part]
        for extra in range(NARROW):
            put(part, totals[part] + extra, 0, duals_ref.shape[0], dims[3] * dims[4])
    write_messages(dims, pitch, acc_ref, out_ref)


def backward_kernel(dims, pitch, part, core_ref, lists_ref, own_ref, other_ref, tiles_ref, *refs):
    scen = dims[0] * dims[2]
    duals_ref = refs[-1] if part == 0 else refs[-2]
    acc_ref = refs[0] if part == 0 else refs[-1]
    quarter, side = own_ref.shape[0] // scen, own_ref.shape[1]
    core = core_ref[0]
    duals_ref[pl.ds(row_part(core, part, quarter), quarter)] = own_ref[...].reshape(quarter, scen, side)
    duals_ref[pl.ds(row_part(1 - core, part, quarter), quarter)] = other_ref[...].reshape(quarter, scen, side)
    duals_ref[duals_ref.shape[0] - 1] = jnp.zeros((scen, side), jnp.bfloat16)
    acc_ref[...] = jnp.zeros_like(acc_ref) if part == 0 else refs[0][...]

    def body(entry, start, width):
        def fields(index):
            return entry(0, index), entry(1, index), entry(2, index)

        backward_blocks(scen, pitch, width, fields, start, duals_ref, tiles_ref, acc_ref)

    over_list(tiles_ref.shape[0], part, lists_ref, body)
    if part == PARTS - 1:
        write_messages(dims, pitch, acc_ref, refs[1])


def forward_kernel(dims, pitch, part, core_ref, lists_ref, probe_ref, tiles_ref, own_ref, away_ref, *refs):
    n_row, n_col, scen_local, time_block, _, own_tiles = dims
    scen = n_row * scen_local
    piece = own_tiles * time_block
    core = core_ref[0]
    acc_ref = refs[-1]
    acc_ref[...] = jnp.zeros_like(acc_ref)
    if part == 0:
        flat_ref = refs[0]
        for group in range(n_row):
            for column in range(n_col):
                for j in range(scen_local):
                    base = column * own_tiles * time_block * pitch + group * scen_local + j
                    block = probe_ref[group * n_col + column, pl.ds(j * piece, piece), :].astype(jnp.float32)
                    for f in range(own_tiles):
                        flat_ref[pl.ds(base + f * time_block * pitch, time_block, stride=pitch), :] = block[
                            f * time_block : (f + 1) * time_block
                        ]
        null = flat_ref.shape[0] - pitch
        flat_ref[pl.ds(null, pitch), :] = jnp.zeros((pitch, flat_ref.shape[1]), jnp.float32)
    else:
        flat_ref = probe_ref

    def body(entry, start, width):
        def picked(index):
            return flat_ref[pl.ds(pl.multiple_of(entry(2, index) * pitch, 8), scen), :].astype(jnp.bfloat16)

        products = []
        for u in [start + v for v in range(0, width, 2)]:
            both = jnp.concatenate([tiles_ref[entry(0, u)], tiles_ref[entry(0, u + 1)]], axis=1)
            result = lax.dot_general(
                stacked_pair(picked(u), picked(u + 1)), both, TRANSPOSED, preferred_element_type=jnp.float32
            )
            products += [result[:scen], result[scen:]]
        for u in range(width):
            place = pl.multiple_of(entry(1, start + u) * scen, scen)
            acc_ref[pl.ds(place, scen), :] += products[u]

    over_list(tiles_ref.shape[0], part, lists_ref, body)
    size = own_ref.shape[0]
    own_ref[...] = acc_ref[pl.ds(pl.multiple_of(row_part(core, part, size), scen), size), :]
    away_ref[...] = acc_ref[pl.ds(pl.multiple_of(row_part(1 - core, part, size), scen), size), :]


def running(values, trailing, terms):
    length = values.shape[0]
    row_iota = lax.broadcasted_iota(jnp.int32, (length, length), 0)
    col_iota = lax.broadcasted_iota(jnp.int32, (length, length), 1)
    keep = ((col_iota >= row_iota) if trailing else (row_iota >= col_iota)).astype(jnp.float32).astype(jnp.bfloat16)
    total = None
    for _ in range(terms):
        term = values.astype(jnp.bfloat16)
        values = values - term.astype(jnp.float32)
        part = jnp.dot(keep, term, preferred_element_type=jnp.float32)
        total = part if total is None else total + part
    return total


def primal_kernel(dims, first, last, *refs):
    n_row, n_col, scen_local, time_block, _, own_tiles = dims
    refs = list(refs)
    recv_ref, inc_ref = refs[:2]
    cum_ref = None if first else refs[2]
    cost_ref, start_ref, len_ref, inc_out, send_ref = refs[2 + (not first) :][:5]
    cum_out = None if last else refs[-1]
    window, flight_local = cost_ref.shape
    side = flight_local // own_tiles
    piece = own_tiles * time_block
    tau_step = 0.6 / math.sqrt(window)
    minutes = lax.broadcasted_iota(jnp.int32, (window, flight_local), 0)
    begin = start_ref[...]
    upper = ((minutes >= begin) & (minutes < begin + len_ref[...])).astype(jnp.float32)
    slopes = []
    for j in range(scen_local):
        bands = []
        for h in range(n_col):
            total = recv_ref[h, pl.ds(j * piece, piece), :].astype(jnp.float32)
            for g in range(1, n_row):
                total = total + recv_ref[g * n_col + h, pl.ds(j * piece, piece), :].astype(jnp.float32)
            bands.append(
                jnp.concatenate([total[f * time_block : (f + 1) * time_block] for f in range(own_tiles)], axis=1)
            )
        slopes.append(jnp.concatenate(bands, axis=0) + cost_ref[...])
    gradient = running(jnp.concatenate(slopes, axis=1), True, 2)
    old = jnp.concatenate([inc_ref[j] for j in range(scen_local)], axis=1)
    if first:
        old_sum = running(old, False, 3)
    else:
        old_sum = jnp.concatenate([cum_ref[j] for j in range(scen_local)], axis=1)
    fresh = jnp.clip(old - tau_step * gradient, 0.0, jnp.concatenate([upper] * scen_local, axis=1))
    fresh_sum = running(fresh, False, 3)
    probe = (2.0 * fresh_sum - old_sum).astype(jnp.bfloat16)
    for j in range(scen_local):
        lanes = slice(j * flight_local, (j + 1) * flight_local)
        inc_out[j] = fresh[:, lanes]
        if not last:
            cum_out[j] = fresh_sum[:, lanes]
        for h in range(n_col):
            band = probe[h * time_block : (h + 1) * time_block, lanes]
            block = jnp.concatenate([band[:, f * side : (f + 1) * side] for f in range(own_tiles)], axis=0)
            for g in range(n_row):
                send_ref[g * n_col + h, pl.ds(j * piece, piece), :] = block


def sum_kernel(first_ref, second_ref, out_ref):
    out_ref[...] = (first_ref[...].astype(jnp.float32) + second_ref[...].astype(jnp.float32)).astype(jnp.bfloat16)


def dual_kernel(remote, part, first, last, core_ref, own_ref, other_ref, *refs):
    parts, (dual_ref, cap_ref, dual_out) = refs[:remote], refs[remote : remote + 3]
    total = own_ref[...] + other_ref[...]
    for received in parts:
        total = total + received[...].astype(jnp.float32)
    bands, row_tiles, band, side = cap_ref.shape
    quarter = row_tiles // (2 * PARTS)
    begin = row_part(core_ref[0], part, quarter)

    def own_rows(ref):
        return jnp.concatenate([ref[a, pl.ds(begin, quarter)] for a in range(bands)], axis=1).reshape(-1, side)

    old = own_rows(dual_ref) if first else dual_ref[...]
    fresh = jnp.maximum(old + SIGMA_STEP * (total - own_rows(cap_ref).astype(jnp.float32)), 0.0)
    dual_out[...] = fresh
    if not last:
        refs[-1][...] = fresh.astype(jnp.bfloat16)


def assemble_kernel(core_ref, *refs):
    out_ref = refs[-1]
    bands, row_tiles, band, side = out_ref.shape
    quarter = row_tiles // (2 * PARTS)
    for i, ref in enumerate(refs[:-1]):
        core = core_ref[0] if i < PARTS else 1 - core_ref[0]
        value = ref[...].reshape(quarter, bands * band, side)
        for a in range(bands):
            out_ref[a, pl.ds(row_part(core, i % PARTS, quarter), quarter)] = value[:, a * band : (a + 1) * band]


def per_device(
    tile_values, tile_rows, tile_cols, increments, dual_vars, flight_cost, win_start, win_len, capacity
):
    n_row, n_col = lax.axis_size("row"), lax.axis_size("col")
    count, side = tile_values.shape[2], tile_values.shape[3]
    scen_local, window, flight_local = increments.shape
    scen, row_length = dual_vars.shape
    row_tiles = row_length // side
    time_block = window // n_col
    flight_tiles = flight_local * n_col // side
    own_tiles = flight_local // side
    col_tiles = time_block * flight_tiles
    dims = (n_row, n_col, scen_local, time_block, flight_tiles, own_tiles)
    message = (n_row * n_col, scen_local * own_tiles * time_block, side)
    part_rows = row_tiles * scen // (2 * PARTS)
    pitch = scen + PITCH_PAD
    band = 8

    rows, cols = tile_rows.reshape(count), tile_cols.reshape(count)
    core = (lax.axis_index("col") % 2).reshape(1)
    cost = pl.CostEstimate(flops=2 * count * scen * side * side, bytes_accessed=count * side * side, transcendentals=0)
    acc_cols = pltpu.VMEM(((col_tiles + 1) * pitch, side), jnp.float32)
    picked_duals = pltpu.VMEM((row_tiles + 1, scen, side), jnp.bfloat16)
    messages = jax.ShapeDtypeStruct(message, jnp.bfloat16)
    part_f32 = jax.ShapeDtypeStruct((part_rows, side), jnp.float32)
    part_bf16 = jax.ShapeDtypeStruct((part_rows, side), jnp.bfloat16)

    def banded(array):
        return array.reshape(scen // band, band, row_tiles, side).transpose(0, 2, 1, 3)

    def in_hbm(array):
        return pltpu.with_memory_space_constraint(array, pltpu.HBM)

    def first_backward(duals):
        return pl.pallas_call(
            functools.partial(first_backward_kernel, dims, pitch),
            in_specs=[scalars()] + [pl.BlockSpec(memory_space=pltpu.HBM)] * 4,
            out_specs=[whole(), whole(), scalars()],
            out_shape=[
                messages,
                pltpu.VMEM((count, side, side), jnp.bfloat16),
                jax.ShapeDtypeStruct((list_size(count),), jnp.int32),
            ],
            scratch_shapes=[
                pltpu.SMEM((count,), jnp.int32),
                pltpu.SMEM((count,), jnp.int32),
                pltpu.VMEM(duals.shape, jnp.float32),
                pltpu.VMEM((row_tiles, scen, side), jnp.bfloat16),
                acc_cols,
                pltpu.SemaphoreType.DMA((count // FIRST + 3,)),
            ],
            compiler_params=params(),
            cost_estimate=cost,
            name="first_backward_products",
        )(core, in_hbm(rows), in_hbm(cols), in_hbm(duals), in_hbm(tile_values.reshape(count, side, side)))

    def in_vmem(array):
        return pltpu.with_memory_space_constraint(array, pltpu.VMEM)

    def backward(part, own, other, tiles, lists, *sums):
        first = part == 0
        return pl.pallas_call(
            functools.partial(backward_kernel, dims, pitch, part),
            in_specs=[scalars()] * 2 + [whole()] * (3 if first else 4),
            out_specs=whole(),
            out_shape=acc_cols if first else messages,
            scratch_shapes=[picked_duals] if first else [picked_duals, acc_cols],
            compiler_params=params(),
            cost_estimate=cost,
            name="backward_products",
        )(core, lists, own, other, in_vmem(tiles), *map(in_vmem, sums))

    def forward(part, probe, tiles, lists):
        first = part == 0
        return pl.pallas_call(
            functools.partial(forward_kernel, dims, pitch, part),
            in_specs=[scalars()] * 2 + [whole()] * 2,
            out_specs=[whole()] * (3 if first else 2),
            out_shape=[part_f32] * 2 + ([acc_cols] if first else []),
            scratch_shapes=[pltpu.VMEM(((row_tiles + 1) * scen, side), jnp.float32)],
            compiler_params=params(),
            cost_estimate=cost,
            name="forward_products",
        )(core, lists, probe if first else in_vmem(probe), in_vmem(tiles))

    def primal_step(recv, primal, cumulative, last):
        first = cumulative is None
        state = (primal,) if first else (primal, cumulative)
        shape = jax.ShapeDtypeStruct(primal.shape, jnp.float32)
        out_shape = [shape, messages] if last else [shape, messages, shape]
        return pl.pallas_call(
            functools.partial(primal_kernel, dims, first, last),
            in_specs=[whole()] * (4 + len(state)),
            out_specs=[whole()] * len(out_shape),
            out_shape=out_shape,
            compiler_params=params(),
            name="primal_update",
        )(recv, *state, flight_cost, win_start.reshape(1, -1), win_len.reshape(1, -1))

    def swap_core(value):
        return lax.ppermute(value, "col", [(i, i ^ 1) for i in range(n_col)])

    bits = (n_col // 2).bit_length() - 1

    def swap_chip(value, step):
        return lax.ppermute(value, "col", [(i, i ^ (2 << (step + i % 2) % bits)) for i in range(n_col)])

    def bf16_sum(first, second, name):
        return pl.pallas_call(
            sum_kernel,
            in_specs=[whole()] * 2,
            out_specs=whole(),
            out_shape=part_bf16,
            compiler_params=params(),
            name=name,
        )(first, second)

    def dual_step(part, own, away, dual, first, last):
        other = swap_core(away)
        partial = bf16_sum(own, other, "core_pair_sum")
        parts = []
        for step in range(bits):
            parts.append(swap_chip(partial, step))
            if step + 1 < bits:
                partial = bf16_sum(partial, parts[-1], "chip_sum")
        out_shape = [part_f32] if last else [part_f32, part_bf16]
        return pl.pallas_call(
            functools.partial(dual_kernel, bits, part, first, last),
            in_specs=[scalars()] + [whole()] * (bits + 4),
            out_specs=[whole()] * len(out_shape),
            out_shape=out_shape,
            compiler_params=params(),
            name="dual_update",
        )(core, own, other, *parts, dual, banded(capacity))

    def assemble(owned):
        pieces = [*owned, *map(swap_core, owned)]
        return pl.pallas_call(
            assemble_kernel,
            in_specs=[scalars()] + [whole()] * len(pieces),
            out_specs=whole(),
            out_shape=jax.ShapeDtypeStruct((scen // band, row_tiles, band, side), jnp.float32),
            compiler_params=params(),
            name="assemble_duals",
        )(core, *pieces)

    send, tiles, lists = first_backward(banded(dual_vars))
    duals, primal, cumulative = [banded(dual_vars)] * PARTS, increments, None
    for sweep in range(ITERS):
        last = sweep + 1 == ITERS
        if sweep:
            sums = backward(0, rounded[0], swap_core(rounded[0]), tiles, lists)
            send = backward(1, rounded[1], swap_core(rounded[1]), tiles, lists, sums)
        recv = lax.all_to_all(send, ("row", "col"), 0, 0, tiled=True)
        primal, send, *cumulative = primal_step(recv, primal, cumulative, last)
        cumulative = None if last else cumulative[0]
        probe = lax.all_to_all(send, ("row", "col"), 0, 0, tiled=True)
        own, away, flat = forward(0, probe, tiles, lists)
        images = [(own, away), forward(1, flat, tiles, lists)]
        results = [dual_step(part, *images[part], duals[part], sweep == 0, last) for part in range(PARTS)]
        duals = [result[0] for result in results]
        rounded = None if last else [result[1] for result in results]
    duals_out = assemble(duals).transpose(0, 2, 1, 3).reshape(scen, row_length)
    return (primal, duals_out)


def solution(mesh):
    placed = (
        P("row", "col", None, None, None),
        P("row", "col", None),
        P("row", "col", None),
        P("row", None, "col"),
        P(None, "row"),
        P(None, "col"),
        P("col"),
        P("col"),
        P(None, "row"),
    )
    return jax.shard_map(
        per_device,
        mesh=mesh,
        in_specs=placed,
        out_specs=(P("row", None, "col"), P(None, "row")),
        check_vma=False,
    )
```

```python
import functools
import math

import jax
import jax.numpy as jnp
from jax import lax
from jax.experimental import pallas as pl
from jax.experimental.pallas import tpu as pltpu
from jax.sharding import PartitionSpec as P

ITERS = 2
SIGMA_STEP = 0.2
PARTS = 2
UNROLL = 64
FIRST_UNROLL = 32
PITCH_PAD = 8
VMEM_BYTES = 24 * 1024 * 1024
TRANSPOSED = (((1,), (1,)), ((), ()))


def params():
    return pltpu.CompilerParams(vmem_limit_bytes=VMEM_BYTES)


def whole():
    return pl.BlockSpec(memory_space=pltpu.VMEM)


def scalars():
    return pl.BlockSpec(memory_space=pltpu.SMEM)


def stacked_pair(first, second):
    zero = jnp.zeros_like(first)
    return jnp.concatenate(
        [jnp.concatenate([first, zero], axis=1), jnp.concatenate([zero, second], axis=1)], axis=0
    )


def column_place(dims, column, pitch):
    time_block, flight_tiles = dims[3], dims[4]
    return pl.multiple_of((column % flight_tiles * time_block + column // flight_tiles) * pitch, 8)


def backward_blocks(dims, pitch, width, rows_ref, cols_ref, duals_ref, tiles_ref, acc_ref, start):
    scen = dims[0] * dims[2]
    products = []
    for u in range(0, width, 2):
        pair = stacked_pair(duals_ref[rows_ref[start + u]], duals_ref[rows_ref[start + u + 1]])
        both = tiles_ref[pl.ds(start + u, 2)]
        result = jnp.dot(pair, both.reshape(-1, both.shape[2]), preferred_element_type=jnp.float32)
        products += [result[:scen], result[scen:]]
    for u in range(width):
        place = column_place(dims, cols_ref[start + u], pitch)
        acc_ref[pl.ds(place, scen), :] += products[u]


def write_messages(dims, pitch, acc_ref, out_ref):
    n_row, n_col, scen_local, time_block, _, own_tiles = dims
    piece = own_tiles * time_block
    for group in range(n_row):
        for column in range(n_col):
            for j in range(scen_local):
                base = column * own_tiles * time_block * pitch + group * scen_local + j
                parts = [
                    acc_ref[pl.ds(base + f * time_block * pitch, time_block, stride=pitch), :]
                    for f in range(own_tiles)
                ]
                out_ref[group * n_col + column, pl.ds(j * piece, piece), :] = jnp.concatenate(
                    parts, axis=0
                ).astype(jnp.bfloat16)


def first_backward_kernel(
    dims, pitch, core_ref, row_source, col_source, dual_source, source_ref, out_ref, tiles_ref,
    rows_ref, cols_ref, bands_ref, duals_ref, acc_ref, sems
):
    count, pieces = tiles_ref.shape[0], sems.shape[0] - 3
    chunk = count // pieces
    lists = [
        pltpu.make_async_copy(row_source, rows_ref, sems.at[pieces]),
        pltpu.make_async_copy(col_source, cols_ref, sems.at[pieces + 1]),
        pltpu.make_async_copy(dual_source, bands_ref, sems.at[pieces + 2]),
    ]
    copies = [
        pltpu.make_async_copy(source_ref.at[pl.ds(i * chunk, chunk)], tiles_ref.at[pl.ds(i * chunk, chunk)], sems.at[i])
        for i in range(pieces)
    ]
    for copy in lists + copies:
        copy.start()
    acc_ref[...] = jnp.zeros_like(acc_ref)
    for copy in lists:
        copy.wait()
    bands = [bands_ref[a].astype(jnp.bfloat16) for a in range(bands_ref.shape[0])]
    duals_ref[...] = jnp.concatenate(bands, axis=1)

    def body(index, _):
        backward_blocks(
            dims, pitch, FIRST_UNROLL, rows_ref, cols_ref, duals_ref, tiles_ref, acc_ref, index * FIRST_UNROLL
        )
        return 0

    for i, copy in enumerate(copies):
        copy.wait()
        lax.fori_loop(i * chunk // FIRST_UNROLL, (i + 1) * chunk // FIRST_UNROLL, body, 0)
    write_messages(dims, pitch, acc_ref, out_ref)


def row_part(core, part, rows):
    return (core * PARTS + part) * rows


def backward_kernel(dims, pitch, core_ref, rows_ref, cols_ref, tiles_ref, *refs):
    pieces, (out_ref, duals_ref, acc_ref) = refs[: 2 * PARTS], refs[2 * PARTS :]
    for i, piece in enumerate(pieces):
        core = core_ref[0] if i < PARTS else 1 - core_ref[0]
        scen, side = duals_ref.shape[1:]
        rows = piece.shape[0] // scen
        duals_ref[pl.ds(row_part(core, i % PARTS, rows), rows)] = piece[...].reshape(rows, scen, side)
    acc_ref[...] = jnp.zeros_like(acc_ref)

    def body(index, _):
        backward_blocks(dims, pitch, UNROLL, rows_ref, cols_ref, duals_ref, tiles_ref, acc_ref, index * UNROLL)
        return 0

    lax.fori_loop(0, tiles_ref.shape[0] // UNROLL, body, 0)
    write_messages(dims, pitch, acc_ref, out_ref)


def forward_kernel(dims, pitch, core_ref, rows_ref, cols_ref, probe_ref, tiles_ref, *refs):
    n_row, n_col, scen_local, time_block, _, own_tiles = dims
    scen = n_row * scen_local
    piece = own_tiles * time_block
    outs, (flat_ref, acc_ref) = refs[: 2 * PARTS], refs[2 * PARTS :]
    acc_ref[...] = jnp.zeros_like(acc_ref)
    for group in range(n_row):
        for column in range(n_col):
            for j in range(scen_local):
                base = column * own_tiles * time_block * pitch + group * scen_local + j
                block = probe_ref[group * n_col + column, pl.ds(j * piece, piece), :].astype(jnp.float32)
                for f in range(own_tiles):
                    flat_ref[pl.ds(base + f * time_block * pitch, time_block, stride=pitch), :] = block[
                        f * time_block : (f + 1) * time_block
                    ]

    def picked(index):
        return flat_ref[pl.ds(column_place(dims, cols_ref[index], pitch), scen), :].astype(jnp.bfloat16)

    def body(index, _):
        start = index * UNROLL
        products = []
        for u in range(0, UNROLL, 2):
            both = jnp.concatenate([tiles_ref[start + u], tiles_ref[start + u + 1]], axis=1)
            result = lax.dot_general(
                stacked_pair(picked(start + u), picked(start + u + 1)),
                both,
                TRANSPOSED,
                preferred_element_type=jnp.float32,
            )
            products += [result[:scen], result[scen:]]
        for u in range(UNROLL):
            place = pl.multiple_of(rows_ref[start + u] * scen, scen)
            acc_ref[pl.ds(place, scen), :] += products[u]
        return 0

    lax.fori_loop(0, tiles_ref.shape[0] // UNROLL, body, 0)
    for i, out_ref in enumerate(outs):
        core = core_ref[0] if i < PARTS else 1 - core_ref[0]
        size = out_ref.shape[0]
        out_ref[...] = acc_ref[pl.ds(pl.multiple_of(row_part(core, i % PARTS, size), size), size), :]


def running(values, trailing, terms):
    length = values.shape[0]
    row_iota = lax.broadcasted_iota(jnp.int32, (length, length), 0)
    col_iota = lax.broadcasted_iota(jnp.int32, (length, length), 1)
    keep = ((col_iota >= row_iota) if trailing else (row_iota >= col_iota)).astype(jnp.float32).astype(jnp.bfloat16)
    total = None
    for _ in range(terms):
        term = values.astype(jnp.bfloat16)
        values = values - term.astype(jnp.float32)
        part = jnp.dot(keep, term, preferred_element_type=jnp.float32)
        total = part if total is None else total + part
    return total


def primal_kernel(dims, first, last, *refs):
    n_row, n_col, scen_local, time_block, _, own_tiles = dims
    refs = list(refs)
    recv_ref, inc_ref = refs[:2]
    cum_ref = None if first else refs[2]
    cost_ref, start_ref, len_ref, inc_out, send_ref = refs[2 + (not first) :][:5]
    cum_out = None if last else refs[-1]
    window, flight_local = cost_ref.shape
    side = flight_local // own_tiles
    piece = own_tiles * time_block
    tau_step = 0.6 / math.sqrt(window)
    minutes = lax.broadcasted_iota(jnp.int32, (window, flight_local), 0)
    begin = start_ref[...]
    upper = ((minutes >= begin) & (minutes < begin + len_ref[...])).astype(jnp.float32)
    slopes = []
    for j in range(scen_local):
        bands = []
        for h in range(n_col):
            total = recv_ref[h, pl.ds(j * piece, piece), :].astype(jnp.float32)
            for g in range(1, n_row):
                total = total + recv_ref[g * n_col + h, pl.ds(j * piece, piece), :].astype(jnp.float32)
            bands.append(
                jnp.concatenate([total[f * time_block : (f + 1) * time_block] for f in range(own_tiles)], axis=1)
            )
        slopes.append(jnp.concatenate(bands, axis=0) + cost_ref[...])
    gradient = running(jnp.concatenate(slopes, axis=1), True, 2)
    old = jnp.concatenate([inc_ref[j] for j in range(scen_local)], axis=1)
    if first:
        old_sum = running(old, False, 3)
    else:
        old_sum = jnp.concatenate([cum_ref[j] for j in range(scen_local)], axis=1)
    fresh = jnp.clip(old - tau_step * gradient, 0.0, jnp.concatenate([upper] * scen_local, axis=1))
    fresh_sum = running(fresh, False, 3)
    probe = (2.0 * fresh_sum - old_sum).astype(jnp.bfloat16)
    for j in range(scen_local):
        lanes = slice(j * flight_local, (j + 1) * flight_local)
        inc_out[j] = fresh[:, lanes]
        if not last:
            cum_out[j] = fresh_sum[:, lanes]
        for h in range(n_col):
            band = probe[h * time_block : (h + 1) * time_block, lanes]
            block = jnp.concatenate([band[:, f * side : (f + 1) * side] for f in range(own_tiles)], axis=0)
            for g in range(n_row):
                send_ref[g * n_col + h, pl.ds(j * piece, piece), :] = block


def sum_kernel(first_ref, second_ref, out_ref):
    out_ref[...] = (first_ref[...].astype(jnp.float32) + second_ref[...].astype(jnp.float32)).astype(jnp.bfloat16)


def dual_kernel(remote, part, first, last, core_ref, own_ref, other_ref, *refs):
    parts, (dual_ref, cap_ref, dual_out) = refs[:remote], refs[remote : remote + 3]
    total = own_ref[...] + other_ref[...]
    for received in parts:
        total = total + received[...].astype(jnp.float32)
    bands, row_tiles, band, side = cap_ref.shape
    rows = row_tiles // (2 * PARTS)
    begin = row_part(core_ref[0], part, rows)

    def own_rows(ref):
        return jnp.concatenate([ref[a, pl.ds(begin, rows)] for a in range(bands)], axis=1).reshape(-1, side)

    old = own_rows(dual_ref) if first else dual_ref[...]
    fresh = jnp.maximum(old + SIGMA_STEP * (total - own_rows(cap_ref).astype(jnp.float32)), 0.0)
    dual_out[...] = fresh
    if not last:
        refs[-1][...] = fresh.astype(jnp.bfloat16)


def assemble_kernel(core_ref, *refs):
    out_ref = refs[-1]
    bands, row_tiles, band, side = out_ref.shape
    rows = row_tiles // (2 * PARTS)
    for i, ref in enumerate(refs[:-1]):
        core = core_ref[0] if i < PARTS else 1 - core_ref[0]
        value = ref[...].reshape(rows, bands * band, side)
        for a in range(bands):
            out_ref[a, pl.ds(row_part(core, i % PARTS, rows), rows)] = value[:, a * band : (a + 1) * band]


def per_device(
    tile_values, tile_rows, tile_cols, increments, dual_vars, flight_cost, win_start, win_len, capacity
):
    n_row, n_col = lax.axis_size("row"), lax.axis_size("col")
    count, side = tile_values.shape[2], tile_values.shape[3]
    scen_local, window, flight_local = increments.shape
    scen, row_length = dual_vars.shape
    row_tiles = row_length // side
    time_block = window // n_col
    flight_tiles = flight_local * n_col // side
    own_tiles = flight_local // side
    col_tiles = time_block * flight_tiles
    dims = (n_row, n_col, scen_local, time_block, flight_tiles, own_tiles)
    message = (n_row * n_col, scen_local * own_tiles * time_block, side)
    part_rows = row_tiles * scen // (2 * PARTS)
    pitch = scen + PITCH_PAD
    band = 8

    rows, cols = tile_rows.reshape(count), tile_cols.reshape(count)
    core = (lax.axis_index("col") % 2).reshape(1)
    cost = pl.CostEstimate(flops=2 * count * scen * side * side, bytes_accessed=count * side * side, transcendentals=0)
    acc_cols = pltpu.VMEM((col_tiles * pitch, side), jnp.float32)
    picked_duals = pltpu.VMEM((row_tiles, scen, side), jnp.bfloat16)
    messages = jax.ShapeDtypeStruct(message, jnp.bfloat16)
    part_f32 = jax.ShapeDtypeStruct((part_rows, side), jnp.float32)
    part_bf16 = jax.ShapeDtypeStruct((part_rows, side), jnp.bfloat16)

    def banded(array):
        return array.reshape(scen // band, band, row_tiles, side).transpose(0, 2, 1, 3)

    def in_hbm(array):
        return pltpu.with_memory_space_constraint(array, pltpu.HBM)

    def first_backward(duals):
        return pl.pallas_call(
            functools.partial(first_backward_kernel, dims, pitch),
            in_specs=[scalars()] + [pl.BlockSpec(memory_space=pltpu.HBM)] * 4,
            out_specs=[whole(), whole()],
            out_shape=[messages, pltpu.VMEM((count, side, side), jnp.bfloat16)],
            scratch_shapes=[
                pltpu.SMEM((count,), jnp.int32),
                pltpu.SMEM((count,), jnp.int32),
                pltpu.VMEM(duals.shape, jnp.float32),
                picked_duals,
                acc_cols,
                pltpu.SemaphoreType.DMA((count // FIRST_UNROLL + 3,)),
            ],
            compiler_params=params(),
            cost_estimate=cost,
            name="first_backward_products",
        )(core, in_hbm(rows), in_hbm(cols), in_hbm(duals), in_hbm(tile_values.reshape(count, side, side)))

    def in_vmem(array):
        return pltpu.with_memory_space_constraint(array, pltpu.VMEM)

    def backward(rounded, tiles):
        pieces = [*rounded, *map(swap_core, rounded)]
        return pl.pallas_call(
            functools.partial(backward_kernel, dims, pitch),
            in_specs=[scalars()] * 3 + [whole()] * (1 + len(pieces)),
            out_specs=whole(),
            out_shape=messages,
            scratch_shapes=[picked_duals, acc_cols],
            compiler_params=params(),
            cost_estimate=cost,
            name="backward_products",
        )(core, rows, cols, in_vmem(tiles), *pieces)

    def forward(probe, tiles):
        return pl.pallas_call(
            functools.partial(forward_kernel, dims, pitch),
            in_specs=[scalars()] * 3 + [whole()] * 2,
            out_specs=[whole()] * (2 * PARTS),
            out_shape=[part_f32] * (2 * PARTS),
            scratch_shapes=[acc_cols, pltpu.VMEM((row_tiles * scen, side), jnp.float32)],
            compiler_params=params(),
            cost_estimate=cost,
            name="forward_products",
        )(core, rows, cols, probe, in_vmem(tiles))

    def primal_step(recv, primal, cumulative, last):
        first = cumulative is None
        state = (primal,) if first else (primal, cumulative)
        shape = jax.ShapeDtypeStruct(primal.shape, jnp.float32)
        out_shape = [shape, messages] if last else [shape, messages, shape]
        return pl.pallas_call(
            functools.partial(primal_kernel, dims, first, last),
            in_specs=[whole()] * (4 + len(state)),
            out_specs=[whole()] * len(out_shape),
            out_shape=out_shape,
            compiler_params=params(),
            name="primal_update",
        )(recv, *state, flight_cost, win_start.reshape(1, -1), win_len.reshape(1, -1))

    def swap_core(value):
        return lax.ppermute(value, "col", [(i, i ^ 1) for i in range(n_col)])

    bits = (n_col // 2).bit_length() - 1

    def swap_chip(value, step):
        return lax.ppermute(value, "col", [(i, i ^ (2 << (step + i % 2) % bits)) for i in range(n_col)])

    def bf16_sum(first, second, name):
        return pl.pallas_call(
            sum_kernel,
            in_specs=[whole()] * 2,
            out_specs=whole(),
            out_shape=part_bf16,
            compiler_params=params(),
            name=name,
        )(first, second)

    def dual_step(part, own, away, dual, first, last):
        other = swap_core(away)
        partial = bf16_sum(own, other, "core_pair_sum")
        parts = []
        for step in range(bits):
            parts.append(swap_chip(partial, step))
            if step + 1 < bits:
                partial = bf16_sum(partial, parts[-1], "chip_sum")
        out_shape = [part_f32] if last else [part_f32, part_bf16]
        return pl.pallas_call(
            functools.partial(dual_kernel, bits, part, first, last),
            in_specs=[scalars()] + [whole()] * (bits + 4),
            out_specs=[whole()] * len(out_shape),
            out_shape=out_shape,
            compiler_params=params(),
            name="dual_update",
        )(core, own, other, *parts, dual, banded(capacity))

    def assemble(owned):
        pieces = [*owned, *map(swap_core, owned)]
        return pl.pallas_call(
            assemble_kernel,
            in_specs=[scalars()] + [whole()] * len(pieces),
            out_specs=whole(),
            out_shape=jax.ShapeDtypeStruct((scen // band, row_tiles, band, side), jnp.float32),
            compiler_params=params(),
            name="assemble_duals",
        )(core, *pieces)

    send, tiles = first_backward(banded(dual_vars))
    duals, primal, cumulative = [banded(dual_vars)] * PARTS, increments, None
    for sweep in range(ITERS):
        last = sweep + 1 == ITERS
        if sweep:
            send = backward(rounded, tiles)
        recv = lax.all_to_all(send, ("row", "col"), 0, 0, tiled=True)
        primal, send, *cumulative = primal_step(recv, primal, cumulative, last)
        cumulative = None if last else cumulative[0]
        probe = lax.all_to_all(send, ("row", "col"), 0, 0, tiled=True)
        images = forward(probe, tiles)
        results = [
            dual_step(part, images[part], images[PARTS + part], duals[part], sweep == 0, last)
            for part in range(PARTS)
        ]
        duals = [result[0] for result in results]
        rounded = None if last else [result[1] for result in results]
    duals_out = assemble(duals).transpose(0, 2, 1, 3).reshape(scen, row_length)
    return (primal, duals_out)


def solution(mesh):
    placed = (
        P("row", "col", None, None, None),
        P("row", "col", None),
        P("row", "col", None),
        P("row", None, "col"),
        P(None, "row"),
        P(None, "col"),
        P("col"),
        P("col"),
        P(None, "row"),
    )
    return jax.shard_map(
        per_device,
        mesh=mesh,
        in_specs=placed,
        out_specs=(P("row", None, "col"), P(None, "row")),
        check_vma=False,
    )
```

```python
import functools
import math

import jax
import jax.numpy as jnp
from jax import lax
from jax.experimental import pallas as pl
from jax.experimental.pallas import tpu as pltpu
from jax.sharding import PartitionSpec as P

ITERS = 2
SIGMA_STEP = 0.2
PARTS = 2
UNROLL = 256
FIRST_UNROLL = 32
TRAIL = 16
PITCH_PAD = 8
VMEM_BYTES = 24 * 1024 * 1024
TRANSPOSED = (((1,), (1,)), ((), ()))


def params():
    return pltpu.CompilerParams(vmem_limit_bytes=VMEM_BYTES)


def whole():
    return pl.BlockSpec(memory_space=pltpu.VMEM)


def scalars():
    return pl.BlockSpec(memory_space=pltpu.SMEM)


def stacked_pair(first, second):
    zero = jnp.zeros_like(first)
    return jnp.concatenate(
        [jnp.concatenate([first, zero], axis=1), jnp.concatenate([zero, second], axis=1)], axis=0
    )


def column_place(dims, column, pitch):
    time_block, flight_tiles = dims[3], dims[4]
    return pl.multiple_of((column % flight_tiles * time_block + column // flight_tiles) * pitch, 8)


def trailing_adds(width, products, add):
    waiting = []
    for u in range(0, width, 2):
        waiting += zip((u, u + 1), products(u))
        while len(waiting) > TRAIL:
            add(*waiting.pop(0))
    for item in waiting:
        add(*item)


def backward_blocks(dims, pitch, width, rows_ref, cols_ref, duals_ref, tiles_ref, acc_ref, start):
    scen = dims[0] * dims[2]

    def products(u):
        pair = stacked_pair(duals_ref[rows_ref[start + u]], duals_ref[rows_ref[start + u + 1]])
        both = tiles_ref[pl.ds(start + u, 2)]
        result = jnp.dot(pair, both.reshape(-1, both.shape[2]), preferred_element_type=jnp.float32)
        return result[:scen], result[scen:]

    def add(u, product):
        place = column_place(dims, cols_ref[start + u], pitch)
        acc_ref[pl.ds(place, scen), :] += product

    trailing_adds(width, products, add)


def write_messages(dims, pitch, acc_ref, out_ref):
    n_row, n_col, scen_local, time_block, _, own_tiles = dims
    piece = own_tiles * time_block
    for group in range(n_row):
        for column in range(n_col):
            for j in range(scen_local):
                base = column * own_tiles * time_block * pitch + group * scen_local + j
                parts = [
                    acc_ref[pl.ds(base + f * time_block * pitch, time_block, stride=pitch), :]
                    for f in range(own_tiles)
                ]
                out_ref[group * n_col + column, pl.ds(j * piece, piece), :] = jnp.concatenate(
                    parts, axis=0
                ).astype(jnp.bfloat16)


def first_backward_kernel(
    dims, pitch, core_ref, row_source, col_source, dual_source, source_ref, out_ref, tiles_ref,
    rows_ref, cols_ref, bands_ref, duals_ref, acc_ref, sems
):
    count, pieces = tiles_ref.shape[0], sems.shape[0] - 3
    chunk = count // pieces
    lists = [
        pltpu.make_async_copy(row_source, rows_ref, sems.at[pieces]),
        pltpu.make_async_copy(col_source, cols_ref, sems.at[pieces + 1]),
        pltpu.make_async_copy(dual_source, bands_ref, sems.at[pieces + 2]),
    ]
    copies = [
        pltpu.make_async_copy(source_ref.at[pl.ds(i * chunk, chunk)], tiles_ref.at[pl.ds(i * chunk, chunk)], sems.at[i])
        for i in range(pieces)
    ]
    for copy in lists + copies:
        copy.start()
    acc_ref[...] = jnp.zeros_like(acc_ref)
    for copy in lists:
        copy.wait()
    bands = [bands_ref[a].astype(jnp.bfloat16) for a in range(bands_ref.shape[0])]
    duals_ref[...] = jnp.concatenate(bands, axis=1)

    def body(index, _):
        backward_blocks(
            dims, pitch, FIRST_UNROLL, rows_ref, cols_ref, duals_ref, tiles_ref, acc_ref, index * FIRST_UNROLL
        )
        return 0

    for i, copy in enumerate(copies):
        copy.wait()
        lax.fori_loop(i * chunk // FIRST_UNROLL, (i + 1) * chunk // FIRST_UNROLL, body, 0)
    write_messages(dims, pitch, acc_ref, out_ref)


def row_part(core, part, rows):
    return (core * PARTS + part) * rows


def backward_kernel(dims, pitch, core_ref, rows_ref, cols_ref, tiles_ref, *refs):
    pieces, (out_ref, duals_ref, acc_ref) = refs[: 2 * PARTS], refs[2 * PARTS :]
    for i, piece in enumerate(pieces):
        core = core_ref[0] if i < PARTS else 1 - core_ref[0]
        scen, side = duals_ref.shape[1:]
        rows = piece.shape[0] // scen
        duals_ref[pl.ds(row_part(core, i % PARTS, rows), rows)] = piece[...].reshape(rows, scen, side)
    acc_ref[...] = jnp.zeros_like(acc_ref)

    width = min(UNROLL, tiles_ref.shape[0])

    def body(index, _):
        backward_blocks(dims, pitch, width, rows_ref, cols_ref, duals_ref, tiles_ref, acc_ref, index * width)
        return 0

    lax.fori_loop(0, tiles_ref.shape[0] // width, body, 0)
    write_messages(dims, pitch, acc_ref, out_ref)


def forward_kernel(dims, pitch, core_ref, rows_ref, cols_ref, probe_ref, tiles_ref, *refs):
    n_row, n_col, scen_local, time_block, _, own_tiles = dims
    scen = n_row * scen_local
    piece = own_tiles * time_block
    outs, (flat_ref, acc_ref) = refs[: 2 * PARTS], refs[2 * PARTS :]
    acc_ref[...] = jnp.zeros_like(acc_ref)
    for group in range(n_row):
        for column in range(n_col):
            for j in range(scen_local):
                base = column * own_tiles * time_block * pitch + group * scen_local + j
                block = probe_ref[group * n_col + column, pl.ds(j * piece, piece), :].astype(jnp.float32)
                for f in range(own_tiles):
                    flat_ref[pl.ds(base + f * time_block * pitch, time_block, stride=pitch), :] = block[
                        f * time_block : (f + 1) * time_block
                    ]

    def picked(index):
        return flat_ref[pl.ds(column_place(dims, cols_ref[index], pitch), scen), :].astype(jnp.bfloat16)

    width = min(UNROLL, tiles_ref.shape[0])

    def body(index, _):
        start = index * width

        def products(u):
            both = jnp.concatenate([tiles_ref[start + u], tiles_ref[start + u + 1]], axis=1)
            result = lax.dot_general(
                stacked_pair(picked(start + u), picked(start + u + 1)),
                both,
                TRANSPOSED,
                preferred_element_type=jnp.float32,
            )
            return result[:scen], result[scen:]

        def add(u, product):
            place = pl.multiple_of(rows_ref[start + u] * scen, scen)
            acc_ref[pl.ds(place, scen), :] += product

        trailing_adds(width, products, add)
        return 0

    lax.fori_loop(0, tiles_ref.shape[0] // width, body, 0)
    for i, out_ref in enumerate(outs):
        core = core_ref[0] if i < PARTS else 1 - core_ref[0]
        size = out_ref.shape[0]
        out_ref[...] = acc_ref[pl.ds(pl.multiple_of(row_part(core, i % PARTS, size), size), size), :]


def running(values, trailing, terms):
    length = values.shape[0]
    row_iota = lax.broadcasted_iota(jnp.int32, (length, length), 0)
    col_iota = lax.broadcasted_iota(jnp.int32, (length, length), 1)
    keep = ((col_iota >= row_iota) if trailing else (row_iota >= col_iota)).astype(jnp.float32).astype(jnp.bfloat16)
    total = None
    for _ in range(terms):
        term = values.astype(jnp.bfloat16)
        values = values - term.astype(jnp.float32)
        part = jnp.dot(keep, term, preferred_element_type=jnp.float32)
        total = part if total is None else total + part
    return total


def primal_kernel(dims, first, last, *refs):
    n_row, n_col, scen_local, time_block, _, own_tiles = dims
    refs = list(refs)
    recv_ref, inc_ref = refs[:2]
    cum_ref = None if first else refs[2]
    cost_ref, start_ref, len_ref, inc_out, send_ref = refs[2 + (not first) :][:5]
    cum_out = None if last else refs[-1]
    window, flight_local = cost_ref.shape
    side = flight_local // own_tiles
    piece = own_tiles * time_block
    tau_step = 0.6 / math.sqrt(window)
    minutes = lax.broadcasted_iota(jnp.int32, (window, flight_local), 0)
    begin = start_ref[...]
    upper = ((minutes >= begin) & (minutes < begin + len_ref[...])).astype(jnp.float32)
    slopes = []
    for j in range(scen_local):
        bands = []
        for h in range(n_col):
            total = recv_ref[h, pl.ds(j * piece, piece), :].astype(jnp.float32)
            for g in range(1, n_row):
                total = total + recv_ref[g * n_col + h, pl.ds(j * piece, piece), :].astype(jnp.float32)
            bands.append(
                jnp.concatenate([total[f * time_block : (f + 1) * time_block] for f in range(own_tiles)], axis=1)
            )
        slopes.append(jnp.concatenate(bands, axis=0) + cost_ref[...])
    gradient = running(jnp.concatenate(slopes, axis=1), True, 2)
    old = jnp.concatenate([inc_ref[j] for j in range(scen_local)], axis=1)
    if first:
        old_sum = running(old, False, 3)
    else:
        old_sum = jnp.concatenate([cum_ref[j] for j in range(scen_local)], axis=1)
    fresh = jnp.clip(old - tau_step * gradient, 0.0, jnp.concatenate([upper] * scen_local, axis=1))
    fresh_sum = running(fresh, False, 3)
    probe = (2.0 * fresh_sum - old_sum).astype(jnp.bfloat16)
    for j in range(scen_local):
        lanes = slice(j * flight_local, (j + 1) * flight_local)
        inc_out[j] = fresh[:, lanes]
        if not last:
            cum_out[j] = fresh_sum[:, lanes]
        for h in range(n_col):
            band = probe[h * time_block : (h + 1) * time_block, lanes]
            block = jnp.concatenate([band[:, f * side : (f + 1) * side] for f in range(own_tiles)], axis=0)
            for g in range(n_row):
                send_ref[g * n_col + h, pl.ds(j * piece, piece), :] = block


def sum_kernel(first_ref, second_ref, out_ref):
    out_ref[...] = (first_ref[...].astype(jnp.float32) + second_ref[...].astype(jnp.float32)).astype(jnp.bfloat16)


def dual_kernel(remote, part, first, last, core_ref, own_ref, other_ref, *refs):
    parts, (dual_ref, cap_ref, dual_out) = refs[:remote], refs[remote : remote + 3]
    total = own_ref[...] + other_ref[...]
    for received in parts:
        total = total + received[...].astype(jnp.float32)
    bands, row_tiles, band, side = cap_ref.shape
    rows = row_tiles // (2 * PARTS)
    begin = row_part(core_ref[0], part, rows)

    def own_rows(ref):
        return jnp.concatenate([ref[a, pl.ds(begin, rows)] for a in range(bands)], axis=1).reshape(-1, side)

    old = own_rows(dual_ref) if first else dual_ref[...]
    fresh = jnp.maximum(old + SIGMA_STEP * (total - own_rows(cap_ref).astype(jnp.float32)), 0.0)
    if last:
        value = fresh.reshape(rows, bands * band, side)
        for a in range(bands):
            dual_out[a] = value[:, a * band : (a + 1) * band]
    else:
        dual_out[...] = fresh
        refs[-1][...] = fresh.astype(jnp.bfloat16)


def part_copies(core, parts, out_ref, sems):
    copies = []
    for i, ref in enumerate(parts):
        bands, rows = ref.shape[:2]
        for a in range(bands):
            place = out_ref.at[a, pl.ds(row_part(core, i, rows), rows)]
            copies.append(pltpu.make_async_copy(ref.at[a], place, sems.at[len(copies)]))
    return copies


def own_results_kernel(core_ref, primal_ref, *refs):
    parts, (primal_out, duals_out, sems) = refs[:PARTS], refs[PARTS:]
    copies = part_copies(core_ref[0], parts, duals_out, sems)
    copies.append(pltpu.make_async_copy(primal_ref, primal_out, sems.at[len(copies)]))
    for copy in copies:
        copy.start()
    for copy in copies:
        copy.wait()


def other_results_kernel(core_ref, _, *refs):
    parts, (duals_out, sems) = refs[:PARTS], refs[PARTS:]
    copies = part_copies(1 - core_ref[0], parts, duals_out, sems)
    for copy in copies:
        copy.start()
    for copy in copies:
        copy.wait()


def per_device(
    tile_values, tile_rows, tile_cols, increments, dual_vars, flight_cost, win_start, win_len, capacity
):
    n_row, n_col = lax.axis_size("row"), lax.axis_size("col")
    count, side = tile_values.shape[2], tile_values.shape[3]
    scen_local, window, flight_local = increments.shape
    scen, row_length = dual_vars.shape
    row_tiles = row_length // side
    time_block = window // n_col
    flight_tiles = flight_local * n_col // side
    own_tiles = flight_local // side
    col_tiles = time_block * flight_tiles
    dims = (n_row, n_col, scen_local, time_block, flight_tiles, own_tiles)
    message = (n_row * n_col, scen_local * own_tiles * time_block, side)
    part_rows = row_tiles * scen // (2 * PARTS)
    pitch = scen + PITCH_PAD
    band = 8

    rows, cols = tile_rows.reshape(count), tile_cols.reshape(count)
    core = (lax.axis_index("col") % 2).reshape(1)
    cost = pl.CostEstimate(flops=2 * count * scen * side * side, bytes_accessed=count * side * side, transcendentals=0)
    acc_cols = pltpu.VMEM((col_tiles * pitch, side), jnp.float32)
    picked_duals = pltpu.VMEM((row_tiles, scen, side), jnp.bfloat16)
    messages = jax.ShapeDtypeStruct(message, jnp.bfloat16)
    part_f32 = jax.ShapeDtypeStruct((part_rows, side), jnp.float32)
    part_out = jax.ShapeDtypeStruct((scen // band, row_tiles // (2 * PARTS), band, side), jnp.float32)
    part_bf16 = jax.ShapeDtypeStruct((part_rows, side), jnp.bfloat16)

    def banded(array):
        return array.reshape(scen // band, band, row_tiles, side).transpose(0, 2, 1, 3)

    def in_hbm(array):
        return pltpu.with_memory_space_constraint(array, pltpu.HBM)

    def first_backward(duals):
        return pl.pallas_call(
            functools.partial(first_backward_kernel, dims, pitch),
            in_specs=[scalars()] + [pl.BlockSpec(memory_space=pltpu.HBM)] * 4,
            out_specs=[whole(), whole()],
            out_shape=[messages, pltpu.VMEM((count, side, side), jnp.bfloat16)],
            scratch_shapes=[
                pltpu.SMEM((count,), jnp.int32),
                pltpu.SMEM((count,), jnp.int32),
                pltpu.VMEM(duals.shape, jnp.float32),
                picked_duals,
                acc_cols,
                pltpu.SemaphoreType.DMA((count // FIRST_UNROLL + 3,)),
            ],
            compiler_params=params(),
            cost_estimate=cost,
            name="first_backward_products",
        )(core, in_hbm(rows), in_hbm(cols), in_hbm(duals), in_hbm(tile_values.reshape(count, side, side)))

    def in_vmem(array):
        return pltpu.with_memory_space_constraint(array, pltpu.VMEM)

    def backward(rounded, tiles):
        pieces = [*rounded, *map(swap_core, rounded)]
        return pl.pallas_call(
            functools.partial(backward_kernel, dims, pitch),
            in_specs=[scalars()] * 3 + [whole()] * (1 + len(pieces)),
            out_specs=whole(),
            out_shape=messages,
            scratch_shapes=[picked_duals, acc_cols],
            compiler_params=params(),
            cost_estimate=cost,
            name="backward_products",
        )(core, rows, cols, in_vmem(tiles), *pieces)

    def forward(probe, tiles):
        return pl.pallas_call(
            functools.partial(forward_kernel, dims, pitch),
            in_specs=[scalars()] * 3 + [whole()] * 2,
            out_specs=[whole()] * (2 * PARTS),
            out_shape=[part_f32] * (2 * PARTS),
            scratch_shapes=[acc_cols, pltpu.VMEM((row_tiles * scen, side), jnp.float32)],
            compiler_params=params(),
            cost_estimate=cost,
            name="forward_products",
        )(core, rows, cols, probe, in_vmem(tiles))

    def primal_step(recv, primal, cumulative, last):
        first = cumulative is None
        state = (primal,) if first else (primal, cumulative)
        shape = jax.ShapeDtypeStruct(primal.shape, jnp.float32)
        out_shape = [pltpu.VMEM(primal.shape, jnp.float32), messages] if last else [shape, messages, shape]
        return pl.pallas_call(
            functools.partial(primal_kernel, dims, first, last),
            in_specs=[whole()] * (4 + len(state)),
            out_specs=[whole()] * len(out_shape),
            out_shape=out_shape,
            compiler_params=params(),
            name="primal_update",
        )(recv, *state, flight_cost, win_start.reshape(1, -1), win_len.reshape(1, -1))

    def swap_core(value):
        return lax.ppermute(value, "col", [(i, i ^ 1) for i in range(n_col)])

    bits = (n_col // 2).bit_length() - 1

    def swap_chip(value, step):
        return lax.ppermute(value, "col", [(i, i ^ (2 << (step + i % 2) % bits)) for i in range(n_col)])

    def bf16_sum(first, second, name):
        return pl.pallas_call(
            sum_kernel,
            in_specs=[whole()] * 2,
            out_specs=whole(),
            out_shape=part_bf16,
            compiler_params=params(),
            name=name,
        )(first, second)

    def dual_step(part, own, away, dual, first, last):
        other = swap_core(away)
        partial = bf16_sum(own, other, "core_pair_sum")
        parts = []
        for step in range(bits):
            parts.append(swap_chip(partial, step))
            if step + 1 < bits:
                partial = bf16_sum(partial, parts[-1], "chip_sum")
        out_shape = [part_out] if last else [part_f32, part_bf16]
        return pl.pallas_call(
            functools.partial(dual_kernel, bits, part, first, last),
            in_specs=[scalars()] + [whole()] * (bits + 4),
            out_specs=[whole()] * len(out_shape),
            out_shape=out_shape,
            compiler_params=params(),
            name="dual_update",
        )(core, own, other, *parts, dual, banded(capacity))

    def results(primal, owned):
        duals_shape = jax.ShapeDtypeStruct((scen // band, row_tiles, band, side), jnp.float32)
        hbm = pl.BlockSpec(memory_space=pltpu.HBM)
        copies = PARTS * (scen // band)
        primal_out, duals_out = pl.pallas_call(
            own_results_kernel,
            in_specs=[scalars()] + [whole()] * (1 + PARTS),
            out_specs=[hbm, hbm],
            out_shape=[jax.ShapeDtypeStruct(primal.shape, jnp.float32), duals_shape],
            scratch_shapes=[pltpu.SemaphoreType.DMA((copies + 1,))],
            compiler_params=params(),
            name="own_results",
        )(core, in_vmem(primal), *owned)
        duals_out = pl.pallas_call(
            other_results_kernel,
            in_specs=[scalars(), hbm] + [whole()] * PARTS,
            out_specs=hbm,
            out_shape=duals_shape,
            input_output_aliases={1: 0},
            scratch_shapes=[pltpu.SemaphoreType.DMA((copies,))],
            compiler_params=params(),
            name="other_results",
        )(core, duals_out, *map(swap_core, owned))
        return primal_out, duals_out.transpose(0, 2, 1, 3).reshape(scen, row_length)

    send, tiles = first_backward(banded(dual_vars))
    duals, primal, cumulative = [banded(dual_vars)] * PARTS, increments, None
    for sweep in range(ITERS):
        last = sweep + 1 == ITERS
        if sweep:
            send = backward(rounded, tiles)
        recv = lax.all_to_all(send, ("row", "col"), 0, 0, tiled=True)
        primal, send, *cumulative = primal_step(recv, primal, cumulative, last)
        cumulative = None if last else cumulative[0]
        probe = lax.all_to_all(send, ("row", "col"), 0, 0, tiled=True)
        images = forward(probe, tiles)
        updates = [
            dual_step(part, images[part], images[PARTS + part], duals[part], sweep == 0, last)
            for part in range(PARTS)
        ]
        duals = [update[0] for update in updates]
        rounded = None if last else [update[1] for update in updates]
    return results(primal, duals)


def solution(mesh):
    placed = (
        P("row", "col", None, None, None),
        P("row", "col", None),
        P("row", "col", None),
        P("row", None, "col"),
        P(None, "row"),
        P(None, "col"),
        P("col"),
        P("col"),
        P(None, "row"),
    )
    return jax.shard_map(
        per_device,
        mesh=mesh,
        in_specs=placed,
        out_specs=(P("row", None, "col"), P(None, "row")),
        check_vma=False,
    )
```

```python
import functools
import math

import jax
import jax.numpy as jnp
from jax import lax
from jax.experimental import pallas as pl
from jax.experimental.pallas import tpu as pltpu
from jax.sharding import PartitionSpec as P

ITERS = 2
SIGMA_STEP = 0.2
PARTS = 2
CHUNKS = 4
UNROLL = 256
FIRST_UNROLL = 32
TRAIL = 16
PITCH_PAD = 8
VMEM_BYTES = 24 * 1024 * 1024
TRANSPOSED = (((1,), (1,)), ((), ()))


def params():
    return pltpu.CompilerParams(vmem_limit_bytes=VMEM_BYTES)


def whole():
    return pl.BlockSpec(memory_space=pltpu.VMEM)


def scalars():
    return pl.BlockSpec(memory_space=pltpu.SMEM)


def stacked_pair(first, second):
    zero = jnp.zeros_like(first)
    return jnp.concatenate(
        [jnp.concatenate([first, zero], axis=1), jnp.concatenate([zero, second], axis=1)], axis=0
    )


def column_place(dims, column, pitch):
    time_block, flight_tiles = dims[3], dims[4]
    return pl.multiple_of((column % flight_tiles * time_block + column // flight_tiles) * pitch, 8)


def chunk_sizes(dims):
    n_row, _, scen_local, time_block, flight_tiles, _ = dims
    return n_row * scen_local // 2, flight_tiles // CHUNKS, time_block


def scenario_offset(dims, index):
    scen_local = dims[2]
    return index // scen_local * 2 * scen_local + index % scen_local


def split_dot(matrix, values, terms):
    total = None
    for _ in range(terms):
        term = values.astype(jnp.bfloat16)
        values = values - term.astype(jnp.float32)
        part = jnp.dot(matrix, term, preferred_element_type=jnp.float32)
        total = part if total is None else total + part
    return total


def zero_one(condition):
    return condition.astype(jnp.float32).astype(jnp.bfloat16)


def block_ones(rows, block):
    row_iota = lax.broadcasted_iota(jnp.int32, (rows, rows * block), 0)
    col_iota = lax.broadcasted_iota(jnp.int32, (rows, rows * block), 1)
    return zero_one((col_iota >= row_iota * block) & (col_iota < (row_iota + 1) * block))


def running(values, block, trailing, terms):
    rows, side = values.shape
    shape = (side, side)
    row_iota, col_iota = lax.broadcasted_iota(jnp.int32, shape, 0), lax.broadcasted_iota(jnp.int32, shape, 1)
    ordered = (col_iota >= row_iota) if trailing else (row_iota >= col_iota)
    keep = zero_one(ordered & (row_iota // block == col_iota // block))
    wide = jnp.concatenate([values[i : i + side] for i in range(0, rows, side)], axis=1)
    sums = split_dot(keep, wide, terms)
    return jnp.concatenate([sums[:, i : i + side] for i in range(0, rows, side)], axis=0)


def spread(values, block):
    rows, side = values.shape
    return jnp.broadcast_to(values[:, None, :], (rows, block, side)).reshape(rows * block, side)


def trailing_adds(width, products, add):
    waiting = []
    for u in range(0, width, 2):
        waiting += zip((u, u + 1), products(u))
        while len(waiting) > TRAIL:
            add(*waiting.pop(0))
    for item in waiting:
        add(*item)


def backward_blocks(dims, pitch, width, rows_ref, cols_ref, duals_ref, tiles_ref, acc_ref, start):
    scen = dims[0] * dims[2]

    def products(u):
        pair = stacked_pair(duals_ref[rows_ref[start + u]], duals_ref[rows_ref[start + u + 1]])
        both = tiles_ref[pl.ds(start + u, 2)]
        result = jnp.dot(pair, both.reshape(-1, both.shape[2]), preferred_element_type=jnp.float32)
        return result[:scen], result[scen:]

    def add(u, product):
        place = column_place(dims, cols_ref[start + u], pitch)
        acc_ref[pl.ds(place, scen), :] += product

    trailing_adds(width, products, add)


def write_sums(dims, pitch, row, acc_ref, outs):
    half, tiles, block = chunk_sizes(dims)
    keeps, sends, (keep_totals, send_totals) = outs[:CHUNKS], outs[CHUNKS : 2 * CHUNKS], outs[2 * CHUNKS :]
    ones = block_ones(half * tiles, block)
    for refs, totals, parity, terms in ((sends, send_totals, 1 - row % 2, 1), (keeps, keep_totals, row % 2, 2)):
        for c, ref in enumerate(refs):
            for i in range(half):
                start = scenario_offset(dims, i) + parity * dims[2]
                parts = [
                    acc_ref[pl.ds((c * tiles + t) * block * pitch + start, block, stride=pitch), :]
                    for t in range(tiles)
                ]
                ref[pl.ds(i * tiles * block, tiles * block), :] = jnp.concatenate(parts, axis=0).astype(ref.dtype)
            totals[pl.ds(c * half * tiles, half * tiles), :] = split_dot(
                ones, ref[...].astype(jnp.float32), terms
            )


def first_backward_kernel(
    dims, pitch, where_ref, row_source, col_source, dual_source, source_ref, tiles_ref, *refs
):
    outs, (rows_ref, cols_ref, bands_ref, duals_ref, acc_ref, sems) = refs[: 2 * CHUNKS + 2], refs[2 * CHUNKS + 2 :]
    count, pieces = tiles_ref.shape[0], sems.shape[0] - 3
    chunk = count // pieces
    lists = [
        pltpu.make_async_copy(row_source, rows_ref, sems.at[pieces]),
        pltpu.make_async_copy(col_source, cols_ref, sems.at[pieces + 1]),
        pltpu.make_async_copy(dual_source, bands_ref, sems.at[pieces + 2]),
    ]
    copies = [
        pltpu.make_async_copy(source_ref.at[pl.ds(i * chunk, chunk)], tiles_ref.at[pl.ds(i * chunk, chunk)], sems.at[i])
        for i in range(pieces)
    ]
    for copy in lists + copies:
        copy.start()
    acc_ref[...] = jnp.zeros_like(acc_ref)
    for copy in lists:
        copy.wait()
    bands = [bands_ref[a].astype(jnp.bfloat16) for a in range(bands_ref.shape[0])]
    duals_ref[...] = jnp.concatenate(bands, axis=1)

    def body(index, _):
        backward_blocks(
            dims, pitch, FIRST_UNROLL, rows_ref, cols_ref, duals_ref, tiles_ref, acc_ref, index * FIRST_UNROLL
        )
        return 0

    for i, copy in enumerate(copies):
        copy.wait()
        lax.fori_loop(i * chunk // FIRST_UNROLL, (i + 1) * chunk // FIRST_UNROLL, body, 0)
    write_sums(dims, pitch, where_ref[1], acc_ref, outs)


def row_part(core, part, rows):
    return (core * PARTS + part) * rows


def backward_kernel(dims, pitch, where_ref, rows_ref, cols_ref, tiles_ref, *refs):
    pieces, outs, (duals_ref, acc_ref) = refs[: 2 * PARTS], refs[2 * PARTS : -2], refs[-2:]
    for i, piece in enumerate(pieces):
        core = where_ref[0] if i < PARTS else 1 - where_ref[0]
        scen, side = duals_ref.shape[1:]
        rows = piece.shape[0] // scen
        duals_ref[pl.ds(row_part(core, i % PARTS, rows), rows)] = piece[...].reshape(rows, scen, side)
    acc_ref[...] = jnp.zeros_like(acc_ref)

    width = min(UNROLL, tiles_ref.shape[0])

    def body(index, _):
        backward_blocks(dims, pitch, width, rows_ref, cols_ref, duals_ref, tiles_ref, acc_ref, index * width)
        return 0

    lax.fori_loop(0, tiles_ref.shape[0] // width, body, 0)
    write_sums(dims, pitch, where_ref[1], acc_ref, outs)


def forward_kernel(dims, pitch, where_ref, rows_ref, cols_ref, tiles_ref, *refs):
    scen = dims[0] * dims[2]
    half, tiles, block = chunk_sizes(dims)
    local, offsets, refs = refs[: 2 * CHUNKS], refs[2 * CHUNKS : 2 * CHUNKS + 2], refs[2 * CHUNKS + 2 :]
    outs, (flat_ref, acc_ref) = refs[: 2 * PARTS], refs[2 * PARTS :]
    acc_ref[...] = jnp.zeros_like(acc_ref)
    for parts, offset_ref, parity in (
        (local[:CHUNKS], offsets[0], where_ref[1] % 2),
        (local[CHUNKS:], offsets[1], 1 - where_ref[1] % 2),
    ):
        for c, ref in enumerate(parts):
            offset = offset_ref[pl.ds(c * half * tiles, half * tiles), :]
            value = ref[...].astype(jnp.float32) + spread(offset, block)
            for i in range(half):
                start = scenario_offset(dims, i) + parity * dims[2]
                for t in range(tiles):
                    row = (i * tiles + t) * block
                    flat_ref[pl.ds((c * tiles + t) * block * pitch + start, block, stride=pitch), :] = value[
                        row : row + block
                    ]

    def picked(index):
        return flat_ref[pl.ds(column_place(dims, cols_ref[index], pitch), scen), :].astype(jnp.bfloat16)

    width = min(UNROLL, tiles_ref.shape[0])

    def body(index, _):
        start = index * width

        def products(u):
            both = jnp.concatenate([tiles_ref[start + u], tiles_ref[start + u + 1]], axis=1)
            result = lax.dot_general(
                stacked_pair(picked(start + u), picked(start + u + 1)),
                both,
                TRANSPOSED,
                preferred_element_type=jnp.float32,
            )
            return result[:scen], result[scen:]

        def add(u, product):
            place = pl.multiple_of(rows_ref[start + u] * scen, scen)
            acc_ref[pl.ds(place, scen), :] += product

        trailing_adds(width, products, add)
        return 0

    lax.fori_loop(0, tiles_ref.shape[0] // width, body, 0)
    for i, out_ref in enumerate(outs):
        core = where_ref[0] if i < PARTS else 1 - where_ref[0]
        size = out_ref.shape[0]
        out_ref[...] = acc_ref[pl.ds(pl.multiple_of(row_part(core, i % PARTS, size), size), size), :]


def add_kernel(*refs):
    total = refs[0][...].astype(jnp.float32)
    for ref in refs[1:-1]:
        total = total + ref[...].astype(jnp.float32)
    refs[-1][...] = total.astype(refs[-1].dtype)


def pair_kernel(first_ref, second_ref, sum_ref, rounded_ref):
    total = first_ref[...] + second_ref[...].astype(jnp.float32)
    sum_ref[...] = total
    rounded_ref[...] = total.astype(jnp.bfloat16)


def scan_kernel(bit, trailing, begin, where_ref, total_ref, other_ref, *refs):
    later = (where_ref[2] >> bit) & 1
    part = other_ref[...] * ((1 - later) if trailing else later).astype(jnp.float32)
    scan_out, total_out = refs[-2:]
    scan_out[...] = part if begin else refs[0][...] + part
    total_out[...] = total_ref[...] + other_ref[...]


def primal_kernel(dims, chunk, first, where_ref, pair_ref, far_ref, tail_ref, inc_ref, *refs):
    half, tiles, block = chunk_sizes(dims)
    if not first:
        cum_ref, refs = refs[0], refs[1:]
    cost_ref, start_ref, len_ref, inc_out, cum_out, local_out, send_out, total_out = refs
    tau_step = 0.6 / math.sqrt(block * dims[1])
    slope = pair_ref[...] + far_ref[...].astype(jnp.float32) + jnp.concatenate([cost_ref[...]] * half, axis=0)
    tail = tail_ref[pl.ds(chunk * half * tiles, half * tiles), :]
    gradient = running(slope, block, True, 2) + spread(tail, block)
    begin = spread(start_ref[...][chunk * tiles : (chunk + 1) * tiles], block)
    end = begin + spread(len_ref[...][chunk * tiles : (chunk + 1) * tiles], block)
    side = begin.shape[1]
    minute = lax.broadcasted_iota(jnp.int32, (tiles, block, side), 1).reshape(tiles * block, side)
    minute = (minute + where_ref[2] * block).astype(jnp.float32)
    upper = ((minute >= begin) & (minute < end)).astype(jnp.float32)
    old = inc_ref[...]
    old_sum = running(old, block, False, 3) if first else cum_ref[...]
    fresh = jnp.clip(old - tau_step * gradient, 0.0, jnp.concatenate([upper] * half, axis=0))
    inc_out[...] = fresh
    fresh_sum = running(fresh, block, False, 3)
    cum_out[...] = fresh_sum
    local = 2.0 * fresh_sum - old_sum
    local_out[...] = local
    send_out[...] = local.astype(jnp.bfloat16)
    total_out[...] = local_out[pl.ds(block - 1, half * tiles, stride=block), :]


def join_kernel(*refs):
    refs[-1][...] = jnp.concatenate([ref[...] for ref in refs[:-1]], axis=0)


def outward_kernel(dims, inc_ref, cost_ref, start_ref, len_ref, out_ref):
    _, n_col, scen_local, block, _, own_tiles = dims
    side = inc_ref.shape[2] // own_tiles
    piece = own_tiles * block

    def lanes(value):
        return jnp.concatenate([value[:, f * side : (f + 1) * side] for f in range(own_tiles)], axis=0)

    window = jnp.concatenate([lanes(start_ref[...]), lanes(len_ref[...])], axis=0).astype(jnp.float32)
    window = jnp.concatenate([window, jnp.zeros((16 - window.shape[0], side), jnp.float32)], axis=0)
    for h in range(n_col):
        minutes = pl.ds(h * block, block)
        cost = lanes(cost_ref[minutes, :])
        high = cost.astype(jnp.bfloat16)
        bands = [lanes(inc_ref[j, minutes, :]).astype(jnp.bfloat16) for j in range(scen_local)]
        bands += [high, (cost - high.astype(jnp.float32)).astype(jnp.bfloat16)]
        for i, band in enumerate(bands):
            out_ref[h, pl.ds(i * piece, piece), :] = band
        out_ref[h, pl.ds(len(bands) * piece, 16), :] = window.astype(jnp.bfloat16)


def arrive_kernel(dims, groups, where_ref, *refs):
    _, n_col, scen_local, block, _, own_tiles = dims
    half, tiles, _ = chunk_sizes(dims)
    piece = own_tiles * block
    sources, refs = refs[:groups], refs[groups:]
    incs, costs, (start_out, len_out, total_out) = refs[:CHUNKS], refs[CHUNKS : 2 * CHUNKS], refs[2 * CHUNKS :]
    for h in range(n_col):
        bands = []
        for x, ref in enumerate(sources):
            group = (where_ref[1] >> 1) ^ x
            for j in range(scen_local):
                band = ref[h, pl.ds(j * piece, piece), :].astype(jnp.float32)
                for f in range(own_tiles):
                    c, t = divmod(h * own_tiles + f, tiles)
                    row = ((group * scen_local + j) * tiles + t) * block
                    incs[c][pl.ds(pl.multiple_of(row, 8), block), :] = band[f * block : (f + 1) * block]
        own = sources[0]
        cost = own[h, pl.ds(scen_local * piece, piece), :].astype(jnp.float32)
        cost = cost + own[h, pl.ds((scen_local + 1) * piece, piece), :].astype(jnp.float32)
        window = own[h, pl.ds((scen_local + 2) * piece, 16), :].astype(jnp.float32)
        for f in range(own_tiles):
            tile = h * own_tiles + f
            c, t = divmod(tile, tiles)
            costs[c][pl.ds(t * block, block), :] = cost[f * block : (f + 1) * block]
            start_out[pl.ds(tile, 1), :] = window[f : f + 1]
            len_out[pl.ds(tile, 1), :] = window[own_tiles + f : own_tiles + f + 1]
    ones = block_ones(tiles, block)
    for c in range(CHUNKS):
        total = split_dot(ones, costs[c][...], 3)
        total_out[pl.ds(c * half * tiles, half * tiles), :] = jnp.concatenate([total] * half, axis=0)


def homeward_kernel(dims, where_ref, *refs):
    _, n_col, scen_local, block, _, own_tiles = dims
    half, tiles, _ = chunk_sizes(dims)
    chunks, outs, flat_ref = refs[:CHUNKS], refs[CHUNKS:-1], refs[-1]
    rows = half * tiles * block
    for c, ref in enumerate(chunks):
        flat_ref[pl.ds(c * rows, rows), :] = ref[...]
    first = (where_ref[1] >> 1) * scen_local
    for d, out_ref in enumerate(outs):
        bands = []
        for j in range(scen_local):
            for f in range(own_tiles):
                tile = (where_ref[2] ^ d) * own_tiles + f
                row = tile // tiles * rows + ((first + j) * tiles + tile % tiles) * block
                bands.append(flat_ref[pl.ds(pl.multiple_of(row, 8), block), :])
        out_ref[...] = jnp.concatenate(bands, axis=0).astype(jnp.bfloat16)


def home_kernel(dims, where_ref, *refs):
    _, _, scen_local, block, _, own_tiles = dims
    out_ref = refs[-1]
    side = out_ref.shape[2] // own_tiles
    for d, ref in enumerate(refs[:-1]):
        minutes = pl.ds(pl.multiple_of((where_ref[2] ^ d) * block, 8), block)
        for j in range(scen_local):
            band = ref[pl.ds(j * own_tiles * block, own_tiles * block), :].astype(jnp.float32)
            for f in range(own_tiles):
                out_ref[j, minutes, f * side : (f + 1) * side] = band[f * block : (f + 1) * block]


def dual_kernel(remote, part, first, last, core_ref, own_ref, other_ref, *refs):
    parts, (dual_ref, cap_ref, dual_out) = refs[:remote], refs[remote : remote + 3]
    total = own_ref[...] + other_ref[...]
    for received in parts:
        total = total + received[...].astype(jnp.float32)
    bands, row_tiles, band, side = cap_ref.shape
    rows = row_tiles // (2 * PARTS)
    begin = row_part(core_ref[0], part, rows)

    def own_rows(ref):
        return jnp.concatenate([ref[a, pl.ds(begin, rows)] for a in range(bands)], axis=1).reshape(-1, side)

    old = own_rows(dual_ref) if first else dual_ref[...]
    fresh = jnp.maximum(old + SIGMA_STEP * (total - own_rows(cap_ref).astype(jnp.float32)), 0.0)
    if last:
        value = fresh.reshape(rows, bands * band, side)
        for a in range(bands):
            dual_out[a] = value[:, a * band : (a + 1) * band]
    else:
        dual_out[...] = fresh
        refs[-1][...] = fresh.astype(jnp.bfloat16)


def part_copies(core, parts, out_ref, sems):
    copies = []
    for i, ref in enumerate(parts):
        bands, rows = ref.shape[:2]
        for a in range(bands):
            place = out_ref.at[a, pl.ds(row_part(core, i, rows), rows)]
            copies.append(pltpu.make_async_copy(ref.at[a], place, sems.at[len(copies)]))
    return copies


def own_results_kernel(core_ref, primal_ref, *refs):
    parts, (primal_out, duals_out, sems) = refs[:PARTS], refs[PARTS:]
    copies = part_copies(core_ref[0], parts, duals_out, sems)
    copies.append(pltpu.make_async_copy(primal_ref, primal_out, sems.at[len(copies)]))
    for copy in copies:
        copy.start()
    for copy in copies:
        copy.wait()


def other_results_kernel(core_ref, _, *refs):
    parts, (duals_out, sems) = refs[:PARTS], refs[PARTS:]
    copies = part_copies(1 - core_ref[0], parts, duals_out, sems)
    for copy in copies:
        copy.start()
    for copy in copies:
        copy.wait()


def per_device(
    tile_values, tile_rows, tile_cols, increments, dual_vars, flight_cost, win_start, win_len, capacity
):
    n_row, n_col = lax.axis_size("row"), lax.axis_size("col")
    count, side = tile_values.shape[2], tile_values.shape[3]
    scen_local, window, flight_local = increments.shape
    scen, row_length = dual_vars.shape
    row_tiles = row_length // side
    time_block = window // n_col
    flight_tiles = flight_local * n_col // side
    own_tiles = flight_local // side
    col_tiles = time_block * flight_tiles
    dims = (n_row, n_col, scen_local, time_block, flight_tiles, own_tiles)
    part_rows = row_tiles * scen // (2 * PARTS)
    pitch = scen + PITCH_PAD
    band = 8

    rows, cols = tile_rows.reshape(count), tile_cols.reshape(count)
    column = lax.axis_index("col")
    where = jnp.stack([column % 2, lax.axis_index("row"), column]).astype(jnp.int32)
    cost = pl.CostEstimate(flops=2 * count * scen * side * side, bytes_accessed=count * side * side, transcendentals=0)
    acc_cols = pltpu.VMEM((col_tiles * pitch, side), jnp.float32)
    picked_duals = pltpu.VMEM((row_tiles, scen, side), jnp.bfloat16)
    half, tiles_each, _ = chunk_sizes(dims)

    def f32(*shape):
        return jax.ShapeDtypeStruct(shape, jnp.float32)

    def bf16(*shape):
        return jax.ShapeDtypeStruct(shape, jnp.bfloat16)

    chunk_shape = (half * tiles_each * time_block, side)
    totals_shape = (half * flight_tiles, side)
    home_rows = scen_local * own_tiles * time_block
    out_rows = (scen_local + 2) * own_tiles * time_block + 16
    sums_shape = [f32(*chunk_shape)] * CHUNKS + [bf16(*chunk_shape)] * CHUNKS + [f32(*totals_shape)] * 2

    def call(kernel, name, out_shape, *args, scalar=0, scratch=()):
        return pl.pallas_call(
            kernel,
            in_specs=[scalars()] * scalar + [whole()] * (len(args) - scalar),
            out_specs=jax.tree.map(lambda _: whole(), out_shape),
            out_shape=out_shape,
            scratch_shapes=list(scratch),
            compiler_params=params(),
            name=name,
        )(*args)

    part_f32 = jax.ShapeDtypeStruct((part_rows, side), jnp.float32)
    part_out = jax.ShapeDtypeStruct((scen // band, row_tiles // (2 * PARTS), band, side), jnp.float32)
    part_bf16 = jax.ShapeDtypeStruct((part_rows, side), jnp.bfloat16)

    def banded(array):
        return array.reshape(scen // band, band, row_tiles, side).transpose(0, 2, 1, 3)

    def in_hbm(array):
        return pltpu.with_memory_space_constraint(array, pltpu.HBM)

    def first_backward(duals):
        return pl.pallas_call(
            functools.partial(first_backward_kernel, dims, pitch),
            in_specs=[scalars()] + [pl.BlockSpec(memory_space=pltpu.HBM)] * 4,
            out_specs=[whole()] * (1 + len(sums_shape)),
            out_shape=[pltpu.VMEM((count, side, side), jnp.bfloat16), *sums_shape],
            scratch_shapes=[
                pltpu.SMEM((count,), jnp.int32),
                pltpu.SMEM((count,), jnp.int32),
                pltpu.VMEM(duals.shape, jnp.float32),
                picked_duals,
                acc_cols,
                pltpu.SemaphoreType.DMA((count // FIRST_UNROLL + 3,)),
            ],
            compiler_params=params(),
            cost_estimate=cost,
            name="first_backward_products",
        )(where, in_hbm(rows), in_hbm(cols), in_hbm(duals), in_hbm(tile_values.reshape(count, side, side)))

    def in_vmem(array):
        return pltpu.with_memory_space_constraint(array, pltpu.VMEM)

    def backward(rounded, tiles):
        pieces = [*rounded, *map(swap_core, rounded)]
        return pl.pallas_call(
            functools.partial(backward_kernel, dims, pitch),
            in_specs=[scalars()] * 3 + [whole()] * (1 + len(pieces)),
            out_specs=[whole()] * len(sums_shape),
            out_shape=sums_shape,
            scratch_shapes=[picked_duals, acc_cols],
            compiler_params=params(),
            cost_estimate=cost,
            name="backward_products",
        )(where, rows, cols, in_vmem(tiles), *pieces)

    def forward(tiles, *probes):
        return pl.pallas_call(
            functools.partial(forward_kernel, dims, pitch),
            in_specs=[scalars()] * 3 + [whole()] * (1 + len(probes)),
            out_specs=[whole()] * (2 * PARTS),
            out_shape=[part_f32] * (2 * PARTS),
            scratch_shapes=[acc_cols, pltpu.VMEM((row_tiles * scen, side), jnp.float32)],
            compiler_params=params(),
            cost_estimate=cost,
            name="forward_products",
        )(where, rows, cols, in_vmem(tiles), *probes)

    def swap_row(value, bit):
        return lax.ppermute(value, "row", [(i, i ^ (1 << bit)) for i in range(n_row)])

    row_bits, col_bits = n_row.bit_length() - 1, n_col.bit_length() - 1

    def scan_blocks(total, trailing, name):
        scanned = []
        for bit in range(col_bits):
            other = lax.ppermute(total, "col", [(i, i ^ (1 << bit)) for i in range(n_col)])
            kernel = functools.partial(scan_kernel, bit, trailing, bit == 0)
            *scanned, total = call(
                kernel, name, [f32(*totals_shape)] * 2, where, total, other, *scanned, scalar=1
            )
        return scanned[0]

    def arrive():
        message = call(
            functools.partial(outward_kernel, dims),
            "primal_outward",
            bf16(n_col, out_rows, side),
            increments,
            flight_cost,
            win_start.reshape(1, -1),
            win_len.reshape(1, -1),
        )
        own = lax.all_to_all(message, "col", 0, 0, tiled=True)
        groups = [own[:, :home_rows]]
        for bit in range(1, row_bits):
            groups += [swap_row(group, bit) for group in groups]
        groups[0] = own
        got = call(
            functools.partial(arrive_kernel, dims, len(groups)),
            "primal_arrive",
            [f32(*chunk_shape)] * CHUNKS
            + [f32(tiles_each * time_block, side)] * CHUNKS
            + [f32(flight_tiles, side)] * 2
            + [f32(*totals_shape)],
            where,
            *groups,
            scalar=1,
        )
        return got[:CHUNKS], got[CHUNKS : 2 * CHUNKS], *got[2 * CHUNKS :]

    def go_home(chunks):
        pieces = call(
            functools.partial(homeward_kernel, dims),
            "primal_homeward",
            [bf16(home_rows, side)] * n_col,
            where,
            *chunks,
            scalar=1,
            scratch=[pltpu.VMEM((CHUNKS * chunk_shape[0], side), jnp.float32)],
        )
        got = [
            lax.ppermute(piece, "col", [(i, i ^ d) for i in range(n_col)]) if d else piece
            for d, piece in enumerate(pieces)
        ]
        return call(
            functools.partial(home_kernel, dims),
            "primal_home",
            pltpu.VMEM(increments.shape, jnp.float32),
            where,
            *got,
            scalar=1,
        )

    def swap_core(value):
        return lax.ppermute(value, "col", [(i, i ^ 1) for i in range(n_col)])

    bits = (n_col // 2).bit_length() - 1

    def swap_chip(value, step):
        return lax.ppermute(value, "col", [(i, i ^ (2 << (step + i % 2) % bits)) for i in range(n_col)])

    def bf16_sum(first, second, name):
        return pl.pallas_call(
            add_kernel,
            in_specs=[whole()] * 2,
            out_specs=whole(),
            out_shape=part_bf16,
            compiler_params=params(),
            name=name,
        )(first, second)

    def dual_step(part, own, away, dual, first, last):
        other = swap_core(away)
        partial = bf16_sum(own, other, "core_pair_sum")
        parts = []
        for step in range(bits):
            parts.append(swap_chip(partial, step))
            if step + 1 < bits:
                partial = bf16_sum(partial, parts[-1], "chip_sum")
        out_shape = [part_out] if last else [part_f32, part_bf16]
        return pl.pallas_call(
            functools.partial(dual_kernel, bits, part, first, last),
            in_specs=[scalars()] + [whole()] * (bits + 4),
            out_specs=[whole()] * len(out_shape),
            out_shape=out_shape,
            compiler_params=params(),
            name="dual_update",
        )(where, own, other, *parts, dual, banded(capacity))

    def results(primal, owned):
        duals_shape = jax.ShapeDtypeStruct((scen // band, row_tiles, band, side), jnp.float32)
        hbm = pl.BlockSpec(memory_space=pltpu.HBM)
        copies = PARTS * (scen // band)
        primal_out, duals_out = pl.pallas_call(
            own_results_kernel,
            in_specs=[scalars()] + [whole()] * (1 + PARTS),
            out_specs=[hbm, hbm],
            out_shape=[jax.ShapeDtypeStruct(primal.shape, jnp.float32), duals_shape],
            scratch_shapes=[pltpu.SemaphoreType.DMA((copies + 1,))],
            compiler_params=params(),
            name="own_results",
        )(where, in_vmem(primal), *owned)
        duals_out = pl.pallas_call(
            other_results_kernel,
            in_specs=[scalars(), hbm] + [whole()] * PARTS,
            out_specs=hbm,
            out_shape=duals_shape,
            input_output_aliases={1: 0},
            scratch_shapes=[pltpu.SemaphoreType.DMA((copies,))],
            compiler_params=params(),
            name="other_results",
        )(where, duals_out, *map(swap_core, owned))
        return primal_out, duals_out.transpose(0, 2, 1, 3).reshape(scen, row_length)

    incs, costs, starts, lengths, cost_totals = arrive()
    tiles, *sums = first_backward(banded(dual_vars))
    duals, cums = [banded(dual_vars)] * PARTS, [()] * CHUNKS
    for sweep in range(ITERS):
        last = sweep + 1 == ITERS
        if sweep:
            sums = backward(rounded, tiles)
        keeps, sends, (keep_total, send_total) = sums[:CHUNKS], sums[CHUNKS : 2 * CHUNKS], sums[2 * CHUNKS :]
        near = [swap_row(send, 0) for send in sends]
        total = call(add_kernel, "totals", f32(*totals_shape), keep_total, swap_row(send_total, 0))
        pairs = [call(pair_kernel, "row_pair_sum", [f32(*chunk_shape), bf16(*chunk_shape)], *x) for x in zip(keeps, near)]
        for bit in range(1, row_bits):
            ends = bit + 1 == row_bits
            far = [swap_row(pair[1], bit) for pair in pairs]
            more = [cost_totals] if ends else []
            total = call(add_kernel, "totals", f32(*totals_shape), total, swap_row(total, bit), *more)
            if not ends:
                pairs = [
                    call(pair_kernel, "row_pair_sum", [f32(*chunk_shape), bf16(*chunk_shape)], pair[0], x)
                    for pair, x in zip(pairs, far)
                ]
        tail = scan_blocks(total, True, "later_blocks")
        steps = [
            call(
                functools.partial(primal_kernel, dims, c, sweep == 0),
                "primal_update",
                [f32(*chunk_shape)] * 3 + [bf16(*chunk_shape), f32(half * tiles_each, side)],
                where,
                pairs[c][0],
                far[c],
                tail,
                incs[c],
                *cums[c],
                costs[c],
                starts,
                lengths,
                scalar=1,
            )
            for c in range(CHUNKS)
        ]
        incs, cums = [step[0] for step in steps], [(step[1],) for step in steps]
        returned = [swap_row(step[3], 0) for step in steps]
        block_total = call(join_kernel, "block_totals", f32(*totals_shape), *(step[4] for step in steps))
        offset = scan_blocks(block_total, False, "earlier_blocks")
        images = forward(tiles, *(step[2] for step in steps), *returned, offset, swap_row(offset, 0))
        updates = [
            dual_step(part, images[part], images[PARTS + part], duals[part], sweep == 0, last)
            for part in range(PARTS)
        ]
        duals = [update[0] for update in updates]
        rounded = None if last else [update[1] for update in updates]
    return results(go_home(incs), duals)


def solution(mesh):
    placed = (
        P("row", "col", None, None, None),
        P("row", "col", None),
        P("row", "col", None),
        P("row", None, "col"),
        P(None, "row"),
        P(None, "col"),
        P("col"),
        P("col"),
        P(None, "row"),
    )
    return jax.shard_map(
        per_device,
        mesh=mesh,
        in_specs=placed,
        out_specs=(P("row", None, "col"), P(None, "row")),
        check_vma=False,
    )
```

```python
import functools
import math

import jax
import jax.numpy as jnp
from jax import lax
from jax.experimental import pallas as pl
from jax.experimental.pallas import tpu as pltpu
from jax.sharding import PartitionSpec as P

ITERS = 2
SIGMA_STEP = 0.2
PARTS = 2
UNROLL = 256
FIRST_UNROLL = 32
TRAIL = 16
PITCH_PAD = 8
VMEM_BYTES = 24 * 1024 * 1024
TRANSPOSED = (((1,), (1,)), ((), ()))


def params():
    return pltpu.CompilerParams(vmem_limit_bytes=VMEM_BYTES)


def whole():
    return pl.BlockSpec(memory_space=pltpu.VMEM)


def scalars():
    return pl.BlockSpec(memory_space=pltpu.SMEM)


def stacked_pair(first, second):
    zero = jnp.zeros_like(first)
    return jnp.concatenate(
        [jnp.concatenate([first, zero], axis=1), jnp.concatenate([zero, second], axis=1)], axis=0
    )


def column_place(dims, column, pitch):
    time_block, flight_tiles = dims[3], dims[4]
    return pl.multiple_of((column % flight_tiles * time_block + column // flight_tiles) * pitch, 8)


def trailing_adds(width, products, add):
    waiting = []
    for u in range(0, width, 2):
        waiting += zip((u, u + 1), products(u))
        while len(waiting) > TRAIL:
            add(*waiting.pop(0))
    for item in waiting:
        add(*item)


def backward_blocks(dims, pitch, width, rows_ref, cols_ref, duals_ref, tiles_ref, acc_ref, start):
    scen = dims[0] * dims[2]

    def products(u):
        pair = stacked_pair(duals_ref[rows_ref[start + u]], duals_ref[rows_ref[start + u + 1]])
        both = tiles_ref[pl.ds(start + u, 2)]
        result = jnp.dot(pair, both.reshape(-1, both.shape[2]), preferred_element_type=jnp.float32)
        return result[:scen], result[scen:]

    def add(u, product):
        place = column_place(dims, cols_ref[start + u], pitch)
        acc_ref[pl.ds(place, scen), :] += product

    trailing_adds(width, products, add)


def write_messages(dims, pitch, acc_ref, out_ref):
    n_row, n_col, scen_local, time_block, _, own_tiles = dims
    piece = own_tiles * time_block
    for group in range(n_row):
        for column in range(n_col):
            for j in range(scen_local):
                base = column * own_tiles * time_block * pitch + group * scen_local + j
                parts = [
                    acc_ref[pl.ds(base + f * time_block * pitch, time_block, stride=pitch), :]
                    for f in range(own_tiles)
                ]
                out_ref[group * n_col + column, pl.ds(j * piece, piece), :] = jnp.concatenate(
                    parts, axis=0
                ).astype(jnp.bfloat16)


def first_backward_kernel(
    dims, pitch, core_ref, row_source, col_source, dual_source, source_ref, out_ref, tiles_ref,
    rows_ref, cols_ref, bands_ref, duals_ref, acc_ref, sems
):
    count, pieces = tiles_ref.shape[0], sems.shape[0] - 3
    chunk = count // pieces
    lists = [
        pltpu.make_async_copy(row_source, rows_ref, sems.at[pieces]),
        pltpu.make_async_copy(col_source, cols_ref, sems.at[pieces + 1]),
        pltpu.make_async_copy(dual_source, bands_ref, sems.at[pieces + 2]),
    ]
    copies = [
        pltpu.make_async_copy(source_ref.at[pl.ds(i * chunk, chunk)], tiles_ref.at[pl.ds(i * chunk, chunk)], sems.at[i])
        for i in range(pieces)
    ]
    for copy in lists + copies:
        copy.start()
    acc_ref[...] = jnp.zeros_like(acc_ref)
    for copy in lists:
        copy.wait()
    bands = [bands_ref[a].astype(jnp.bfloat16) for a in range(bands_ref.shape[0])]
    duals_ref[...] = jnp.concatenate(bands, axis=1)

    def body(index, _):
        backward_blocks(
            dims, pitch, FIRST_UNROLL, rows_ref, cols_ref, duals_ref, tiles_ref, acc_ref, index * FIRST_UNROLL
        )
        return 0

    for i, copy in enumerate(copies):
        copy.wait()
        lax.fori_loop(i * chunk // FIRST_UNROLL, (i + 1) * chunk // FIRST_UNROLL, body, 0)
    write_messages(dims, pitch, acc_ref, out_ref)


def row_part(core, part, rows):
    return (core * PARTS + part) * rows


def part_rows_of(ref, core, part, size):
    return ref[pl.ds(pl.multiple_of(row_part(core, part, size), size), size), :]


def backward_kernel(dims, pitch, core_ref, rows_ref, cols_ref, tiles_ref, *refs):
    pieces, (out_ref, duals_ref, acc_ref) = refs[: 2 * PARTS], refs[2 * PARTS :]
    for i, piece in enumerate(pieces):
        core = core_ref[0] if i < PARTS else 1 - core_ref[0]
        scen, side = duals_ref.shape[1:]
        rows = piece.shape[0] // scen
        duals_ref[pl.ds(row_part(core, i % PARTS, rows), rows)] = piece[...].reshape(rows, scen, side)
    scen = duals_ref.shape[1]
    for row in range(0, acc_ref.shape[0], pitch):
        acc_ref[pl.ds(row, scen), :] = jnp.zeros((scen, acc_ref.shape[1]), jnp.float32)

    width = min(UNROLL, tiles_ref.shape[0])

    def body(index, _):
        backward_blocks(dims, pitch, width, rows_ref, cols_ref, duals_ref, tiles_ref, acc_ref, index * width)
        return 0

    lax.fori_loop(0, tiles_ref.shape[0] // width, body, 0)
    write_messages(dims, pitch, acc_ref, out_ref)


def forward_kernel(dims, pitch, core_ref, rows_ref, cols_ref, probe_ref, tiles_ref, *refs):
    n_row, n_col, scen_local, time_block, _, own_tiles = dims
    scen = n_row * scen_local
    piece = own_tiles * time_block
    (acc_ref, *outs), flat_ref = refs[:-1], refs[-1]
    acc_ref[...] = jnp.zeros_like(acc_ref)
    for group in range(n_row):
        for column in range(n_col):
            for j in range(scen_local):
                base = column * own_tiles * time_block * pitch + group * scen_local + j
                block = probe_ref[group * n_col + column, pl.ds(j * piece, piece), :].astype(jnp.float32)
                for f in range(own_tiles):
                    flat_ref[pl.ds(base + f * time_block * pitch, time_block, stride=pitch), :] = block[
                        f * time_block : (f + 1) * time_block
                    ]

    def picked(index):
        return flat_ref[pl.ds(column_place(dims, cols_ref[index], pitch), scen), :].astype(jnp.bfloat16)

    width = min(UNROLL, tiles_ref.shape[0])

    def body(index, _):
        start = index * width

        def products(u):
            both = jnp.concatenate([tiles_ref[start + u], tiles_ref[start + u + 1]], axis=1)
            result = lax.dot_general(
                stacked_pair(picked(start + u), picked(start + u + 1)),
                both,
                TRANSPOSED,
                preferred_element_type=jnp.float32,
            )
            return result[:scen], result[scen:]

        def add(u, product):
            place = pl.multiple_of(rows_ref[start + u] * scen, scen)
            acc_ref[pl.ds(place, scen), :] += product

        trailing_adds(width, products, add)
        return 0

    lax.fori_loop(0, tiles_ref.shape[0] // width, body, 0)
    for part, out_ref in enumerate(outs):
        out_ref[...] = part_rows_of(acc_ref, 1 - core_ref[0], part, out_ref.shape[0]).astype(jnp.bfloat16)


def running(values, trailing, terms):
    length = values.shape[0]
    row_iota = lax.broadcasted_iota(jnp.int32, (length, length), 0)
    col_iota = lax.broadcasted_iota(jnp.int32, (length, length), 1)
    keep = ((col_iota >= row_iota) if trailing else (row_iota >= col_iota)).astype(jnp.float32).astype(jnp.bfloat16)
    total = None
    for _ in range(terms):
        term = values.astype(jnp.bfloat16)
        values = values - term.astype(jnp.float32)
        part = jnp.dot(keep, term, preferred_element_type=jnp.float32)
        total = part if total is None else total + part
    return total


def primal_kernel(dims, first, last, *refs):
    n_row, n_col, scen_local, time_block, _, own_tiles = dims
    refs = list(refs)
    recv_ref, inc_ref = refs[:2]
    cum_ref = None if first else refs[2]
    cost_ref, start_ref, len_ref, inc_out, send_ref = refs[2 + (not first) :][:5]
    cum_out = None if last else refs[-1]
    window, flight_local = cost_ref.shape
    side = flight_local // own_tiles
    piece = own_tiles * time_block
    tau_step = 0.6 / math.sqrt(window)
    minutes = lax.broadcasted_iota(jnp.int32, (window, flight_local), 0)
    begin = start_ref[...]
    upper = ((minutes >= begin) & (minutes < begin + len_ref[...])).astype(jnp.float32)
    slopes = []
    for j in range(scen_local):
        bands = []
        for h in range(n_col):
            total = recv_ref[h, pl.ds(j * piece, piece), :].astype(jnp.float32)
            for g in range(1, n_row):
                total = total + recv_ref[g * n_col + h, pl.ds(j * piece, piece), :].astype(jnp.float32)
            bands.append(
                jnp.concatenate([total[f * time_block : (f + 1) * time_block] for f in range(own_tiles)], axis=1)
            )
        slopes.append(jnp.concatenate(bands, axis=0) + cost_ref[...])
    gradient = running(jnp.concatenate(slopes, axis=1), True, 2)
    old = jnp.concatenate([inc_ref[j] for j in range(scen_local)], axis=1)
    if first:
        old_sum = running(old, False, 3)
    else:
        old_sum = jnp.concatenate([cum_ref[j] for j in range(scen_local)], axis=1)
    fresh = jnp.clip(old - tau_step * gradient, 0.0, jnp.concatenate([upper] * scen_local, axis=1))
    fresh_sum = running(fresh, False, 3)
    probe = (2.0 * fresh_sum - old_sum).astype(jnp.bfloat16)
    for j in range(scen_local):
        lanes = slice(j * flight_local, (j + 1) * flight_local)
        inc_out[j] = fresh[:, lanes]
        if not last:
            cum_out[j] = fresh_sum[:, lanes]
        for h in range(n_col):
            band = probe[h * time_block : (h + 1) * time_block, lanes]
            block = jnp.concatenate([band[:, f * side : (f + 1) * side] for f in range(own_tiles)], axis=0)
            for g in range(n_row):
                send_ref[g * n_col + h, pl.ds(j * piece, piece), :] = block


def own_sum(part, core_ref, image_ref, other_ref):
    own = part_rows_of(image_ref, core_ref[0], part, other_ref.shape[0])
    return own + other_ref[...].astype(jnp.float32)


def pair_kernel(part, core_ref, image_ref, other_ref, out_ref):
    out_ref[...] = own_sum(part, core_ref, image_ref, other_ref).astype(jnp.bfloat16)


def sum_kernel(first_ref, second_ref, out_ref):
    out_ref[...] = (first_ref[...].astype(jnp.float32) + second_ref[...].astype(jnp.float32)).astype(jnp.bfloat16)


def dual_kernel(remote, part, first, last, core_ref, image_ref, other_ref, *refs):
    parts, (dual_ref, cap_ref, dual_out) = refs[:remote], refs[remote : remote + 3]
    total = own_sum(part, core_ref, image_ref, other_ref)
    for received in parts:
        total = total + received[...].astype(jnp.float32)
    bands, row_tiles, band, side = cap_ref.shape
    rows = row_tiles // (2 * PARTS)
    begin = row_part(core_ref[0], part, rows)

    def own_rows(ref):
        return jnp.concatenate([ref[a, pl.ds(begin, rows)] for a in range(bands)], axis=1).reshape(-1, side)

    old = own_rows(dual_ref) if first else dual_ref[...]
    fresh = jnp.maximum(old + SIGMA_STEP * (total - own_rows(cap_ref).astype(jnp.float32)), 0.0)
    if last:
        value = fresh.reshape(rows, bands * band, side)
        for a in range(bands):
            dual_out[a] = value[:, a * band : (a + 1) * band]
    else:
        dual_out[...] = fresh
        refs[-1][...] = fresh.astype(jnp.bfloat16)


def part_copies(core, parts, out_ref, sems):
    copies = []
    for i, ref in enumerate(parts):
        bands, rows = ref.shape[:2]
        for a in range(bands):
            place = out_ref.at[a, pl.ds(row_part(core, i, rows), rows)]
            copies.append(pltpu.make_async_copy(ref.at[a], place, sems.at[len(copies)]))
    return copies


def own_results_kernel(core_ref, primal_ref, *refs):
    parts, (primal_out, duals_out, sems) = refs[:PARTS], refs[PARTS:]
    copies = part_copies(core_ref[0], parts, duals_out, sems)
    copies.append(pltpu.make_async_copy(primal_ref, primal_out, sems.at[len(copies)]))
    for copy in copies:
        copy.start()
    for copy in copies:
        copy.wait()


def other_results_kernel(core_ref, _, *refs):
    parts, (duals_out, sems) = refs[:PARTS], refs[PARTS:]
    copies = part_copies(1 - core_ref[0], parts, duals_out, sems)
    for copy in copies:
        copy.start()
    for copy in copies:
        copy.wait()


def per_device(
    tile_values, tile_rows, tile_cols, increments, dual_vars, flight_cost, win_start, win_len, capacity
):
    n_row, n_col = lax.axis_size("row"), lax.axis_size("col")
    count, side = tile_values.shape[2], tile_values.shape[3]
    scen_local, window, flight_local = increments.shape
    scen, row_length = dual_vars.shape
    row_tiles = row_length // side
    time_block = window // n_col
    flight_tiles = flight_local * n_col // side
    own_tiles = flight_local // side
    col_tiles = time_block * flight_tiles
    dims = (n_row, n_col, scen_local, time_block, flight_tiles, own_tiles)
    message = (n_row * n_col, scen_local * own_tiles * time_block, side)
    part_rows = row_tiles * scen // (2 * PARTS)
    pitch = scen + PITCH_PAD
    band = 8

    rows, cols = tile_rows.reshape(count), tile_cols.reshape(count)
    core = (lax.axis_index("col") % 2).reshape(1)
    cost = pl.CostEstimate(flops=2 * count * scen * side * side, bytes_accessed=count * side * side, transcendentals=0)
    acc_cols = pltpu.VMEM((col_tiles * pitch, side), jnp.float32)
    picked_duals = pltpu.VMEM((row_tiles, scen, side), jnp.bfloat16)
    messages = jax.ShapeDtypeStruct(message, jnp.bfloat16)
    part_f32 = jax.ShapeDtypeStruct((part_rows, side), jnp.float32)
    part_out = jax.ShapeDtypeStruct((scen // band, row_tiles // (2 * PARTS), band, side), jnp.float32)
    part_bf16 = jax.ShapeDtypeStruct((part_rows, side), jnp.bfloat16)

    def banded(array):
        return array.reshape(scen // band, band, row_tiles, side).transpose(0, 2, 1, 3)

    def in_hbm(array):
        return pltpu.with_memory_space_constraint(array, pltpu.HBM)

    def first_backward(duals):
        return pl.pallas_call(
            functools.partial(first_backward_kernel, dims, pitch),
            in_specs=[scalars()] + [pl.BlockSpec(memory_space=pltpu.HBM)] * 4,
            out_specs=[whole(), whole()],
            out_shape=[messages, pltpu.VMEM((count, side, side), jnp.bfloat16)],
            scratch_shapes=[
                pltpu.SMEM((count,), jnp.int32),
                pltpu.SMEM((count,), jnp.int32),
                pltpu.VMEM(duals.shape, jnp.float32),
                picked_duals,
                acc_cols,
                pltpu.SemaphoreType.DMA((count // FIRST_UNROLL + 3,)),
            ],
            compiler_params=params(),
            cost_estimate=cost,
            name="first_backward_products",
        )(core, in_hbm(rows), in_hbm(cols), in_hbm(duals), in_hbm(tile_values.reshape(count, side, side)))

    def in_vmem(array):
        return pltpu.with_memory_space_constraint(array, pltpu.VMEM)

    def backward(rounded, tiles):
        pieces = [*rounded, *map(swap_core, rounded)]
        return pl.pallas_call(
            functools.partial(backward_kernel, dims, pitch),
            in_specs=[scalars()] * 3 + [whole()] * (1 + len(pieces)),
            out_specs=whole(),
            out_shape=messages,
            scratch_shapes=[picked_duals, acc_cols],
            compiler_params=params(),
            cost_estimate=cost,
            name="backward_products",
        )(core, rows, cols, in_vmem(tiles), *pieces)

    def forward(probe, tiles):
        return pl.pallas_call(
            functools.partial(forward_kernel, dims, pitch),
            in_specs=[scalars()] * 3 + [whole()] * 2,
            out_specs=[whole()] * (1 + PARTS),
            out_shape=[jax.ShapeDtypeStruct((row_tiles * scen, side), jnp.float32)] + [part_bf16] * PARTS,
            scratch_shapes=[acc_cols],
            compiler_params=params(),
            cost_estimate=cost,
            name="forward_products",
        )(core, rows, cols, probe, in_vmem(tiles))

    def primal_step(recv, primal, cumulative, last):
        first = cumulative is None
        state = (primal,) if first else (primal, cumulative)
        shape = jax.ShapeDtypeStruct(primal.shape, jnp.float32)
        out_shape = [pltpu.VMEM(primal.shape, jnp.float32), messages] if last else [shape, messages, shape]
        return pl.pallas_call(
            functools.partial(primal_kernel, dims, first, last),
            in_specs=[whole()] * (4 + len(state)),
            out_specs=[whole()] * len(out_shape),
            out_shape=out_shape,
            compiler_params=params(),
            name="primal_update",
        )(recv, *state, flight_cost, win_start.reshape(1, -1), win_len.reshape(1, -1))

    def swap_core(value):
        return lax.ppermute(value, "col", [(i, i ^ 1) for i in range(n_col)])

    bits = (n_col // 2).bit_length() - 1

    def swap_chip(value, step):
        return lax.ppermute(value, "col", [(i, i ^ (2 << (step + i % 2) % bits)) for i in range(n_col)])

    def bf16_sum(first, second, name):
        return pl.pallas_call(
            sum_kernel,
            in_specs=[whole()] * 2,
            out_specs=whole(),
            out_shape=part_bf16,
            compiler_params=params(),
            name=name,
        )(first, second)

    def dual_step(part, image, away, dual, first, last):
        other = swap_core(away)
        partial = pl.pallas_call(
            functools.partial(pair_kernel, part),
            in_specs=[scalars()] + [whole()] * 2,
            out_specs=whole(),
            out_shape=part_bf16,
            compiler_params=params(),
            name="core_pair_sum",
        )(core, image, other)
        parts = []
        for step in range(bits):
            parts.append(swap_chip(partial, step))
            if step + 1 < bits:
                partial = bf16_sum(partial, parts[-1], "chip_sum")
        out_shape = [part_out] if last else [part_f32, part_bf16]
        return pl.pallas_call(
            functools.partial(dual_kernel, bits, part, first, last),
            in_specs=[scalars()] + [whole()] * (bits + 4),
            out_specs=[whole()] * len(out_shape),
            out_shape=out_shape,
            compiler_params=params(),
            name="dual_update",
        )(core, image, other, *parts, dual, banded(capacity))

    def results(primal, owned):
        duals_shape = jax.ShapeDtypeStruct((scen // band, row_tiles, band, side), jnp.float32)
        hbm = pl.BlockSpec(memory_space=pltpu.HBM)
        copies = PARTS * (scen // band)
        primal_out, duals_out = pl.pallas_call(
            own_results_kernel,
            in_specs=[scalars()] + [whole()] * (1 + PARTS),
            out_specs=[hbm, hbm],
            out_shape=[jax.ShapeDtypeStruct(primal.shape, jnp.float32), duals_shape],
            scratch_shapes=[pltpu.SemaphoreType.DMA((copies + 1,))],
            compiler_params=params(),
            name="own_results",
        )(core, in_vmem(primal), *owned)
        duals_out = pl.pallas_call(
            other_results_kernel,
            in_specs=[scalars(), hbm] + [whole()] * PARTS,
            out_specs=hbm,
            out_shape=duals_shape,
            input_output_aliases={1: 0},
            scratch_shapes=[pltpu.SemaphoreType.DMA((copies,))],
            compiler_params=params(),
            name="other_results",
        )(core, duals_out, *map(swap_core, owned))
        return primal_out, duals_out.transpose(0, 2, 1, 3).reshape(scen, row_length)

    send, tiles = first_backward(banded(dual_vars))
    duals, primal, cumulative = [banded(dual_vars)] * PARTS, increments, None
    for sweep in range(ITERS):
        last = sweep + 1 == ITERS
        if sweep:
            send = backward(rounded, tiles)
        recv = lax.all_to_all(send, ("row", "col"), 0, 0, tiled=True)
        primal, send, *cumulative = primal_step(recv, primal, cumulative, last)
        cumulative = None if last else cumulative[0]
        probe = lax.all_to_all(send, ("row", "col"), 0, 0, tiled=True)
        image, *aways = forward(probe, tiles)
        updates = [
            dual_step(part, image, aways[part], duals[part], sweep == 0, last)
            for part in range(PARTS)
        ]
        duals = [update[0] for update in updates]
        rounded = None if last else [update[1] for update in updates]
    return results(primal, duals)


def solution(mesh):
    placed = (
        P("row", "col", None, None, None),
        P("row", "col", None),
        P("row", "col", None),
        P("row", None, "col"),
        P(None, "row"),
        P(None, "col"),
        P("col"),
        P("col"),
        P(None, "row"),
    )
    return jax.shard_map(
        per_device,
        mesh=mesh,
        in_specs=placed,
        out_specs=(P("row", None, "col"), P(None, "row")),
        check_vma=False,
    )
```

```python
import functools
import math

import jax
import jax.numpy as jnp
from jax import lax
from jax.experimental import pallas as pl
from jax.experimental.pallas import tpu as pltpu
from jax.sharding import PartitionSpec as P

ITERS = 2
SIGMA_STEP = 0.2
PARTS = 2
UNROLL = 256
FIRST_UNROLL = 32
TRAIL = 16
PITCH_PAD = 8
VMEM_BYTES = 24 * 1024 * 1024
TRANSPOSED = (((1,), (1,)), ((), ()))


def params():
    return pltpu.CompilerParams(vmem_limit_bytes=VMEM_BYTES)


def whole():
    return pl.BlockSpec(memory_space=pltpu.VMEM)


def scalars():
    return pl.BlockSpec(memory_space=pltpu.SMEM)


def stacked_pair(first, second):
    zero = jnp.zeros_like(first)
    return jnp.concatenate(
        [jnp.concatenate([first, zero], axis=1), jnp.concatenate([zero, second], axis=1)], axis=0
    )


def column_place(dims, column, pitch):
    time_block, flight_tiles = dims[3], dims[4]
    return pl.multiple_of((column % flight_tiles * time_block + column // flight_tiles) * pitch, 8)


def trailing_adds(width, products, add):
    waiting = []
    for u in range(0, width, 2):
        waiting += zip((u, u + 1), products(u))
        while len(waiting) > TRAIL:
            add(*waiting.pop(0))
    for item in waiting:
        add(*item)


def backward_blocks(dims, pitch, width, rows_ref, cols_ref, duals_ref, tiles_ref, acc_ref, start):
    scen = dims[0] * dims[2]

    def products(u):
        pair = stacked_pair(duals_ref[rows_ref[start + u]], duals_ref[rows_ref[start + u + 1]])
        both = tiles_ref[pl.ds(start + u, 2)]
        result = jnp.dot(pair, both.reshape(-1, both.shape[2]), preferred_element_type=jnp.float32)
        return result[:scen], result[scen:]

    def add(u, product):
        place = column_place(dims, cols_ref[start + u], pitch)
        acc_ref[pl.ds(place, scen), :] += product

    trailing_adds(width, products, add)


def round_sums(dims, pitch, acc_ref):
    scen, time_block, flight_tiles = dims[0] * dims[2], dims[3], dims[4]
    lost = [jnp.zeros((scen, acc_ref.shape[1]), jnp.float32)] * flight_tiles
    for minute in reversed(range(time_block)):
        for f in range(flight_tiles):
            place = pl.ds((f * time_block + minute) * pitch, scen)
            value = acc_ref[place, :] + lost[f]
            rounded = value.astype(jnp.bfloat16).astype(jnp.float32)
            lost[f] = value - rounded
            acc_ref[place, :] = rounded


def write_messages(dims, pitch, acc_ref, out_ref):
    n_row, n_col, scen_local, time_block, _, own_tiles = dims
    piece = own_tiles * time_block
    round_sums(dims, pitch, acc_ref)
    for group in range(n_row):
        for column in range(n_col):
            for j in range(scen_local):
                base = column * own_tiles * time_block * pitch + group * scen_local + j
                parts = [
                    acc_ref[pl.ds(base + f * time_block * pitch, time_block, stride=pitch), :]
                    for f in range(own_tiles)
                ]
                out_ref[group * n_col + column, pl.ds(j * piece, piece), :] = jnp.concatenate(
                    parts, axis=0
                ).astype(jnp.bfloat16)


def first_backward_kernel(
    dims, pitch, core_ref, row_source, col_source, dual_source, source_ref, out_ref, tiles_ref,
    rows_ref, cols_ref, bands_ref, duals_ref, acc_ref, sems
):
    count, pieces = tiles_ref.shape[0], sems.shape[0] - 3
    chunk = count // pieces
    lists = [
        pltpu.make_async_copy(row_source, rows_ref, sems.at[pieces]),
        pltpu.make_async_copy(col_source, cols_ref, sems.at[pieces + 1]),
        pltpu.make_async_copy(dual_source, bands_ref, sems.at[pieces + 2]),
    ]
    copies = [
        pltpu.make_async_copy(source_ref.at[pl.ds(i * chunk, chunk)], tiles_ref.at[pl.ds(i * chunk, chunk)], sems.at[i])
        for i in range(pieces)
    ]
    for copy in lists + copies:
        copy.start()
    acc_ref[...] = jnp.zeros_like(acc_ref)
    for copy in lists:
        copy.wait()
    bands = [bands_ref[a].astype(jnp.bfloat16) for a in range(bands_ref.shape[0])]
    duals_ref[...] = jnp.concatenate(bands, axis=1)

    def body(index, _):
        backward_blocks(
            dims, pitch, FIRST_UNROLL, rows_ref, cols_ref, duals_ref, tiles_ref, acc_ref, index * FIRST_UNROLL
        )
        return 0

    for i, copy in enumerate(copies):
        copy.wait()
        lax.fori_loop(i * chunk // FIRST_UNROLL, (i + 1) * chunk // FIRST_UNROLL, body, 0)
    write_messages(dims, pitch, acc_ref, out_ref)


def row_part(core, part, rows):
    return (core * PARTS + part) * rows


def part_rows_of(ref, core, part, size):
    return ref[pl.ds(pl.multiple_of(row_part(core, part, size), size), size), :]


def backward_kernel(dims, pitch, core_ref, rows_ref, cols_ref, tiles_ref, *refs):
    pieces, (out_ref, duals_ref, acc_ref) = refs[: 2 * PARTS], refs[2 * PARTS :]
    for i, piece in enumerate(pieces):
        core = core_ref[0] if i < PARTS else 1 - core_ref[0]
        scen, side = duals_ref.shape[1:]
        rows = piece.shape[0] // scen
        duals_ref[pl.ds(row_part(core, i % PARTS, rows), rows)] = piece[...].reshape(rows, scen, side)
    scen = duals_ref.shape[1]
    for row in range(0, acc_ref.shape[0], pitch):
        acc_ref[pl.ds(row, scen), :] = jnp.zeros((scen, acc_ref.shape[1]), jnp.float32)

    width = min(UNROLL, tiles_ref.shape[0])

    def body(index, _):
        backward_blocks(dims, pitch, width, rows_ref, cols_ref, duals_ref, tiles_ref, acc_ref, index * width)
        return 0

    lax.fori_loop(0, tiles_ref.shape[0] // width, body, 0)
    write_messages(dims, pitch, acc_ref, out_ref)


def forward_kernel(dims, pitch, core_ref, rows_ref, cols_ref, probe_ref, tiles_ref, *refs):
    n_row, n_col, scen_local, time_block, _, own_tiles = dims
    scen = n_row * scen_local
    piece = own_tiles * time_block
    (acc_ref, *outs), flat_ref = refs[:-1], refs[-1]
    acc_ref[...] = jnp.zeros_like(acc_ref)
    for group in range(n_row):
        for column in range(n_col):
            for j in range(scen_local):
                base = column * own_tiles * time_block * pitch + group * scen_local + j
                block = probe_ref[group * n_col + column, pl.ds(j * piece, piece), :].astype(jnp.float32)
                for f in range(own_tiles):
                    flat_ref[pl.ds(base + f * time_block * pitch, time_block, stride=pitch), :] = block[
                        f * time_block : (f + 1) * time_block
                    ]

    def picked(index):
        return flat_ref[pl.ds(column_place(dims, cols_ref[index], pitch), scen), :].astype(jnp.bfloat16)

    width = min(UNROLL, tiles_ref.shape[0])

    def body(index, _):
        start = index * width

        def products(u):
            both = jnp.concatenate([tiles_ref[start + u], tiles_ref[start + u + 1]], axis=1)
            result = lax.dot_general(
                stacked_pair(picked(start + u), picked(start + u + 1)),
                both,
                TRANSPOSED,
                preferred_element_type=jnp.float32,
            )
            return result[:scen], result[scen:]

        def add(u, product):
            place = pl.multiple_of(rows_ref[start + u] * scen, scen)
            acc_ref[pl.ds(place, scen), :] += product

        trailing_adds(width, products, add)
        return 0

    lax.fori_loop(0, tiles_ref.shape[0] // width, body, 0)
    for part, out_ref in enumerate(outs):
        out_ref[...] = part_rows_of(acc_ref, 1 - core_ref[0], part, out_ref.shape[0]).astype(jnp.bfloat16)


def running(values, trailing, terms):
    length = values.shape[0]
    row_iota = lax.broadcasted_iota(jnp.int32, (length, length), 0)
    col_iota = lax.broadcasted_iota(jnp.int32, (length, length), 1)
    keep = ((col_iota >= row_iota) if trailing else (row_iota >= col_iota)).astype(jnp.float32).astype(jnp.bfloat16)
    total = None
    for _ in range(terms):
        term = values.astype(jnp.bfloat16)
        values = values - term.astype(jnp.float32)
        part = jnp.dot(keep, term, preferred_element_type=jnp.float32)
        total = part if total is None else total + part
    return total


def primal_kernel(dims, first, last, *refs):
    n_row, n_col, scen_local, time_block, _, own_tiles = dims
    refs = list(refs)
    recv_ref, inc_ref = refs[:2]
    cum_ref = None if first else refs[2]
    cost_ref, start_ref, len_ref, inc_out, send_ref = refs[2 + (not first) :][:5]
    cum_out = None if last else refs[-1]
    window, flight_local = cost_ref.shape
    side = flight_local // own_tiles
    piece = own_tiles * time_block
    tau_step = 0.6 / math.sqrt(window)
    minutes = lax.broadcasted_iota(jnp.int32, (window, flight_local), 0)
    begin = start_ref[...]
    upper = ((minutes >= begin) & (minutes < begin + len_ref[...])).astype(jnp.float32)
    slopes = []
    for j in range(scen_local):
        bands = []
        for h in range(n_col):
            total = recv_ref[h, pl.ds(j * piece, piece), :].astype(jnp.float32)
            for g in range(1, n_row):
                total = total + recv_ref[g * n_col + h, pl.ds(j * piece, piece), :].astype(jnp.float32)
            bands.append(
                jnp.concatenate([total[f * time_block : (f + 1) * time_block] for f in range(own_tiles)], axis=1)
            )
        slopes.append(jnp.concatenate(bands, axis=0) + cost_ref[...])
    gradient = running(jnp.concatenate(slopes, axis=1), True, 2)
    old = jnp.concatenate([inc_ref[j] for j in range(scen_local)], axis=1)
    if first:
        old_sum = running(old, False, 3)
    else:
        old_sum = jnp.concatenate([cum_ref[j] for j in range(scen_local)], axis=1)
    fresh = jnp.clip(old - tau_step * gradient, 0.0, jnp.concatenate([upper] * scen_local, axis=1))
    fresh_sum = running(fresh, False, 3)
    probe = (2.0 * fresh_sum - old_sum).astype(jnp.bfloat16)
    for j in range(scen_local):
        lanes = slice(j * flight_local, (j + 1) * flight_local)
        inc_out[j] = fresh[:, lanes]
        if not last:
            cum_out[j] = fresh_sum[:, lanes]
        for h in range(n_col):
            band = probe[h * time_block : (h + 1) * time_block, lanes]
            block = jnp.concatenate([band[:, f * side : (f + 1) * side] for f in range(own_tiles)], axis=0)
            for g in range(n_row):
                send_ref[g * n_col + h, pl.ds(j * piece, piece), :] = block


def own_sum(part, core_ref, image_ref, other_ref):
    own = part_rows_of(image_ref, core_ref[0], part, other_ref.shape[0])
    return own + other_ref[...].astype(jnp.float32)


def pair_kernel(part, core_ref, image_ref, other_ref, out_ref):
    out_ref[...] = own_sum(part, core_ref, image_ref, other_ref).astype(jnp.bfloat16)


def sum_kernel(first_ref, second_ref, out_ref):
    out_ref[...] = (first_ref[...].astype(jnp.float32) + second_ref[...].astype(jnp.float32)).astype(jnp.bfloat16)


def dual_kernel(remote, part, first, last, core_ref, image_ref, other_ref, *refs):
    parts, (dual_ref, cap_ref, dual_out) = refs[:remote], refs[remote : remote + 3]
    total = own_sum(part, core_ref, image_ref, other_ref)
    for received in parts:
        total = total + received[...].astype(jnp.float32)
    bands, row_tiles, band, side = cap_ref.shape
    rows = row_tiles // (2 * PARTS)
    begin = row_part(core_ref[0], part, rows)

    def own_rows(ref):
        return jnp.concatenate([ref[a, pl.ds(begin, rows)] for a in range(bands)], axis=1).reshape(-1, side)

    old = own_rows(dual_ref) if first else dual_ref[...]
    fresh = jnp.maximum(old + SIGMA_STEP * (total - own_rows(cap_ref).astype(jnp.float32)), 0.0)
    if last:
        value = fresh.reshape(rows, bands * band, side)
        for a in range(bands):
            dual_out[a] = value[:, a * band : (a + 1) * band]
    else:
        dual_out[...] = fresh
        refs[-1][...] = fresh.astype(jnp.bfloat16)


def part_copies(core, parts, out_ref, sems):
    copies = []
    for i, ref in enumerate(parts):
        bands, rows = ref.shape[:2]
        for a in range(bands):
            place = out_ref.at[a, pl.ds(row_part(core, i, rows), rows)]
            copies.append(pltpu.make_async_copy(ref.at[a], place, sems.at[len(copies)]))
    return copies


def own_results_kernel(core_ref, primal_ref, *refs):
    parts, (primal_out, duals_out, sems) = refs[:PARTS], refs[PARTS:]
    copies = part_copies(core_ref[0], parts, duals_out, sems)
    copies.append(pltpu.make_async_copy(primal_ref, primal_out, sems.at[len(copies)]))
    for copy in copies:
        copy.start()
    for copy in copies:
        copy.wait()


def other_results_kernel(core_ref, _, *refs):
    parts, (duals_out, sems) = refs[:PARTS], refs[PARTS:]
    copies = part_copies(1 - core_ref[0], parts, duals_out, sems)
    for copy in copies:
        copy.start()
    for copy in copies:
        copy.wait()


def per_device(
    tile_values, tile_rows, tile_cols, increments, dual_vars, flight_cost, win_start, win_len, capacity
):
    n_row, n_col = lax.axis_size("row"), lax.axis_size("col")
    count, side = tile_values.shape[2], tile_values.shape[3]
    scen_local, window, flight_local = increments.shape
    scen, row_length = dual_vars.shape
    row_tiles = row_length // side
    time_block = window // n_col
    flight_tiles = flight_local * n_col // side
    own_tiles = flight_local // side
    col_tiles = time_block * flight_tiles
    dims = (n_row, n_col, scen_local, time_block, flight_tiles, own_tiles)
    message = (n_row * n_col, scen_local * own_tiles * time_block, side)
    part_rows = row_tiles * scen // (2 * PARTS)
    pitch = scen + PITCH_PAD
    band = 8

    rows, cols = tile_rows.reshape(count), tile_cols.reshape(count)
    core = (lax.axis_index("col") % 2).reshape(1)
    cost = pl.CostEstimate(flops=2 * count * scen * side * side, bytes_accessed=count * side * side, transcendentals=0)
    acc_cols = pltpu.VMEM((col_tiles * pitch, side), jnp.float32)
    picked_duals = pltpu.VMEM((row_tiles, scen, side), jnp.bfloat16)
    messages = jax.ShapeDtypeStruct(message, jnp.bfloat16)
    part_f32 = jax.ShapeDtypeStruct((part_rows, side), jnp.float32)
    part_out = jax.ShapeDtypeStruct((scen // band, row_tiles // (2 * PARTS), band, side), jnp.float32)
    part_bf16 = jax.ShapeDtypeStruct((part_rows, side), jnp.bfloat16)

    def banded(array):
        return array.reshape(scen // band, band, row_tiles, side).transpose(0, 2, 1, 3)

    def in_hbm(array):
        return pltpu.with_memory_space_constraint(array, pltpu.HBM)

    def first_backward(duals):
        return pl.pallas_call(
            functools.partial(first_backward_kernel, dims, pitch),
            in_specs=[scalars()] + [pl.BlockSpec(memory_space=pltpu.HBM)] * 4,
            out_specs=[whole(), whole()],
            out_shape=[messages, pltpu.VMEM((count, side, side), jnp.bfloat16)],
            scratch_shapes=[
                pltpu.SMEM((count,), jnp.int32),
                pltpu.SMEM((count,), jnp.int32),
                pltpu.VMEM(duals.shape, jnp.float32),
                picked_duals,
                acc_cols,
                pltpu.SemaphoreType.DMA((count // FIRST_UNROLL + 3,)),
            ],
            compiler_params=params(),
            cost_estimate=cost,
            name="first_backward_products",
        )(core, in_hbm(rows), in_hbm(cols), in_hbm(duals), in_hbm(tile_values.reshape(count, side, side)))

    def in_vmem(array):
        return pltpu.with_memory_space_constraint(array, pltpu.VMEM)

    def backward(rounded, tiles):
        pieces = [*rounded, *map(swap_core, rounded)]
        return pl.pallas_call(
            functools.partial(backward_kernel, dims, pitch),
            in_specs=[scalars()] * 3 + [whole()] * (1 + len(pieces)),
            out_specs=whole(),
            out_shape=messages,
            scratch_shapes=[picked_duals, acc_cols],
            compiler_params=params(),
            cost_estimate=cost,
            name="backward_products",
        )(core, rows, cols, in_vmem(tiles), *pieces)

    def forward(probe, tiles):
        return pl.pallas_call(
            functools.partial(forward_kernel, dims, pitch),
            in_specs=[scalars()] * 3 + [whole()] * 2,
            out_specs=[whole()] * (1 + PARTS),
            out_shape=[jax.ShapeDtypeStruct((row_tiles * scen, side), jnp.float32)] + [part_bf16] * PARTS,
            scratch_shapes=[acc_cols],
            compiler_params=params(),
            cost_estimate=cost,
            name="forward_products",
        )(core, rows, cols, probe, in_vmem(tiles))

    def primal_step(recv, primal, cumulative, last):
        first = cumulative is None
        state = (primal,) if first else (primal, cumulative)
        shape = jax.ShapeDtypeStruct(primal.shape, jnp.float32)
        out_shape = [pltpu.VMEM(primal.shape, jnp.float32), messages] if last else [shape, messages, shape]
        return pl.pallas_call(
            functools.partial(primal_kernel, dims, first, last),
            in_specs=[whole()] * (4 + len(state)),
            out_specs=[whole()] * len(out_shape),
            out_shape=out_shape,
            compiler_params=params(),
            name="primal_update",
        )(recv, *state, flight_cost, win_start.reshape(1, -1), win_len.reshape(1, -1))

    def swap_core(value):
        return lax.ppermute(value, "col", [(i, i ^ 1) for i in range(n_col)])

    bits = (n_col // 2).bit_length() - 1

    def swap_chip(value, step):
        return lax.ppermute(value, "col", [(i, i ^ (2 << (step + i % 2) % bits)) for i in range(n_col)])

    def bf16_sum(first, second, name):
        return pl.pallas_call(
            sum_kernel,
            in_specs=[whole()] * 2,
            out_specs=whole(),
            out_shape=part_bf16,
            compiler_params=params(),
            name=name,
        )(first, second)

    def dual_step(part, image, away, dual, first, last):
        other = swap_core(away)
        partial = pl.pallas_call(
            functools.partial(pair_kernel, part),
            in_specs=[scalars()] + [whole()] * 2,
            out_specs=whole(),
            out_shape=part_bf16,
            compiler_params=params(),
            name="core_pair_sum",
        )(core, image, other)
        parts = []
        for step in range(bits):
            parts.append(swap_chip(partial, step))
            if step + 1 < bits:
                partial = bf16_sum(partial, parts[-1], "chip_sum")
        out_shape = [part_out] if last else [part_f32, part_bf16]
        return pl.pallas_call(
            functools.partial(dual_kernel, bits, part, first, last),
            in_specs=[scalars()] + [whole()] * (bits + 4),
            out_specs=[whole()] * len(out_shape),
            out_shape=out_shape,
            compiler_params=params(),
            name="dual_update",
        )(core, image, other, *parts, dual, banded(capacity))

    def results(primal, owned):
        duals_shape = jax.ShapeDtypeStruct((scen // band, row_tiles, band, side), jnp.float32)
        hbm = pl.BlockSpec(memory_space=pltpu.HBM)
        copies = PARTS * (scen // band)
        primal_out, duals_out = pl.pallas_call(
            own_results_kernel,
            in_specs=[scalars()] + [whole()] * (1 + PARTS),
            out_specs=[hbm, hbm],
            out_shape=[jax.ShapeDtypeStruct(primal.shape, jnp.float32), duals_shape],
            scratch_shapes=[pltpu.SemaphoreType.DMA((copies + 1,))],
            compiler_params=params(),
            name="own_results",
        )(core, in_vmem(primal), *owned)
        duals_out = pl.pallas_call(
            other_results_kernel,
            in_specs=[scalars(), hbm] + [whole()] * PARTS,
            out_specs=hbm,
            out_shape=duals_shape,
            input_output_aliases={1: 0},
            scratch_shapes=[pltpu.SemaphoreType.DMA((copies,))],
            compiler_params=params(),
            name="other_results",
        )(core, duals_out, *map(swap_core, owned))
        return primal_out, duals_out.transpose(0, 2, 1, 3).reshape(scen, row_length)

    send, tiles = first_backward(banded(dual_vars))
    duals, primal, cumulative = [banded(dual_vars)] * PARTS, increments, None
    for sweep in range(ITERS):
        last = sweep + 1 == ITERS
        if sweep:
            send = backward(rounded, tiles)
        recv = lax.all_to_all(send, ("row", "col"), 0, 0, tiled=True)
        primal, send, *cumulative = primal_step(recv, primal, cumulative, last)
        cumulative = None if last else cumulative[0]
        probe = lax.all_to_all(send, ("row", "col"), 0, 0, tiled=True)
        image, *aways = forward(probe, tiles)
        updates = [
            dual_step(part, image, aways[part], duals[part], sweep == 0, last)
            for part in range(PARTS)
        ]
        duals = [update[0] for update in updates]
        rounded = None if last else [update[1] for update in updates]
    return results(primal, duals)


def solution(mesh):
    placed = (
        P("row", "col", None, None, None),
        P("row", "col", None),
        P("row", "col", None),
        P("row", None, "col"),
        P(None, "row"),
        P(None, "col"),
        P("col"),
        P("col"),
        P(None, "row"),
    )
    return jax.shard_map(
        per_device,
        mesh=mesh,
        in_specs=placed,
        out_specs=(P("row", None, "col"), P(None, "row")),
        check_vma=False,
    )
```

```python
import functools
import math

import jax
import jax.numpy as jnp
from jax import lax
from jax.experimental import pallas as pl
from jax.experimental.pallas import tpu as pltpu
from jax.sharding import PartitionSpec as P

ITERS = 2
SIGMA_STEP = 0.2
PARTS = 2
UNROLL = 256
FIRST_UNROLL = 32
TRAIL = 16
PITCH_PAD = 8
VMEM_BYTES = 24 * 1024 * 1024
TRANSPOSED = (((1,), (1,)), ((), ()))


def params():
    return pltpu.CompilerParams(vmem_limit_bytes=VMEM_BYTES)


def whole():
    return pl.BlockSpec(memory_space=pltpu.VMEM)


def scalars():
    return pl.BlockSpec(memory_space=pltpu.SMEM)


def stacked_pair(first, second):
    zero = jnp.zeros_like(first)
    return jnp.concatenate(
        [jnp.concatenate([first, zero], axis=1), jnp.concatenate([zero, second], axis=1)], axis=0
    )


def column_place(dims, column, pitch):
    time_block, flight_tiles = dims[3], dims[4]
    return pl.multiple_of((column % flight_tiles * time_block + column // flight_tiles) * pitch, 8)


def trailing_adds(width, products, add):
    waiting = []
    for u in range(0, width, 2):
        waiting += zip((u, u + 1), products(u))
        while len(waiting) > TRAIL:
            add(*waiting.pop(0))
    for item in waiting:
        add(*item)


def backward_blocks(dims, pitch, width, rows_ref, cols_ref, duals_ref, tiles_ref, acc_ref, start):
    scen = dims[0] * dims[2]

    def products(u):
        pair = stacked_pair(duals_ref[rows_ref[start + u]], duals_ref[rows_ref[start + u + 1]])
        both = tiles_ref[pl.ds(start + u, 2)]
        result = jnp.dot(pair, both.reshape(-1, both.shape[2]), preferred_element_type=jnp.float32)
        return result[:scen], result[scen:]

    def add(u, product):
        place = column_place(dims, cols_ref[start + u], pitch)
        acc_ref[pl.ds(place, scen), :] += product

    trailing_adds(width, products, add)


def round_sums(dims, pitch, acc_ref):
    scen, time_block, flight_tiles = dims[0] * dims[2], dims[3], dims[4]
    lost = [jnp.zeros((scen, acc_ref.shape[1]), jnp.float32)] * flight_tiles
    for minute in reversed(range(time_block)):
        for f in range(flight_tiles):
            place = pl.ds((f * time_block + minute) * pitch, scen)
            value = acc_ref[place, :] + lost[f]
            rounded = value.astype(jnp.bfloat16).astype(jnp.float32)
            lost[f] = value - rounded
            acc_ref[place, :] = rounded


def write_messages(dims, pitch, acc_ref, out_ref):
    n_row, n_col, scen_local, time_block, _, own_tiles = dims
    piece = own_tiles * time_block
    round_sums(dims, pitch, acc_ref)
    for group in range(n_row):
        for column in range(n_col):
            for j in range(scen_local):
                base = column * own_tiles * time_block * pitch + group * scen_local + j
                parts = [
                    acc_ref[pl.ds(base + f * time_block * pitch, time_block, stride=pitch), :]
                    for f in range(own_tiles)
                ]
                out_ref[group * n_col + column, pl.ds(j * piece, piece), :] = jnp.concatenate(
                    parts, axis=0
                ).astype(jnp.bfloat16)


def first_backward_kernel(
    dims, pitch, core_ref, row_source, col_source, dual_source, source_ref, out_ref, tiles_ref,
    rows_ref, cols_ref, bands_ref, duals_ref, acc_ref, sems
):
    count, pieces = tiles_ref.shape[0], sems.shape[0] - 3
    chunk = count // pieces
    lists = [
        pltpu.make_async_copy(row_source, rows_ref, sems.at[pieces]),
        pltpu.make_async_copy(col_source, cols_ref, sems.at[pieces + 1]),
        pltpu.make_async_copy(dual_source, bands_ref, sems.at[pieces + 2]),
    ]
    copies = [
        pltpu.make_async_copy(source_ref.at[pl.ds(i * chunk, chunk)], tiles_ref.at[pl.ds(i * chunk, chunk)], sems.at[i])
        for i in range(pieces)
    ]
    for copy in lists + copies:
        copy.start()
    acc_ref[...] = jnp.zeros_like(acc_ref)
    for copy in lists:
        copy.wait()
    bands = [bands_ref[a].astype(jnp.bfloat16) for a in range(bands_ref.shape[0])]
    duals_ref[...] = jnp.concatenate(bands, axis=1)

    def body(index, _):
        backward_blocks(
            dims, pitch, FIRST_UNROLL, rows_ref, cols_ref, duals_ref, tiles_ref, acc_ref, index * FIRST_UNROLL
        )
        return 0

    for i, copy in enumerate(copies):
        copy.wait()
        lax.fori_loop(i * chunk // FIRST_UNROLL, (i + 1) * chunk // FIRST_UNROLL, body, 0)
    write_messages(dims, pitch, acc_ref, out_ref)


def row_part(core, part, rows):
    return (core * PARTS + part) * rows


def part_rows_of(ref, core, part, size):
    return ref[pl.ds(pl.multiple_of(row_part(core, part, size), size), size), :]


def clear_kernel(scen, pitch, acc_ref):
    for row in range(0, acc_ref.shape[0], pitch):
        acc_ref[pl.ds(row, scen), :] = jnp.zeros((scen, acc_ref.shape[1]), jnp.float32)


def backward_kernel(dims, pitch, core_ref, rows_ref, cols_ref, tiles_ref, _, *refs):
    pieces, (out_ref, acc_ref, duals_ref) = refs[: 2 * PARTS], refs[2 * PARTS :]
    for i, piece in enumerate(pieces):
        core = core_ref[0] if i < PARTS else 1 - core_ref[0]
        scen, side = duals_ref.shape[1:]
        rows = piece.shape[0] // scen
        duals_ref[pl.ds(row_part(core, i % PARTS, rows), rows)] = piece[...].reshape(rows, scen, side)
    width = min(UNROLL, tiles_ref.shape[0])

    def body(index, _):
        backward_blocks(dims, pitch, width, rows_ref, cols_ref, duals_ref, tiles_ref, acc_ref, index * width)
        return 0

    lax.fori_loop(0, tiles_ref.shape[0] // width, body, 0)
    write_messages(dims, pitch, acc_ref, out_ref)


def forward_kernel(dims, pitch, core_ref, rows_ref, cols_ref, probe_ref, tiles_ref, *refs):
    n_row, n_col, scen_local, time_block, _, own_tiles = dims
    scen = n_row * scen_local
    piece = own_tiles * time_block
    (acc_ref, *outs), flat_ref = refs[:-1], refs[-1]
    acc_ref[...] = jnp.zeros_like(acc_ref)
    for group in range(n_row):
        for column in range(n_col):
            for j in range(scen_local):
                base = column * own_tiles * time_block * pitch + group * scen_local + j
                block = probe_ref[group * n_col + column, pl.ds(j * piece, piece), :].astype(jnp.float32)
                for f in range(own_tiles):
                    flat_ref[pl.ds(base + f * time_block * pitch, time_block, stride=pitch), :] = block[
                        f * time_block : (f + 1) * time_block
                    ]

    def picked(index):
        return flat_ref[pl.ds(column_place(dims, cols_ref[index], pitch), scen), :].astype(jnp.bfloat16)

    width = min(UNROLL, tiles_ref.shape[0])

    def body(index, _):
        start = index * width

        def products(u):
            both = jnp.concatenate([tiles_ref[start + u], tiles_ref[start + u + 1]], axis=1)
            result = lax.dot_general(
                stacked_pair(picked(start + u), picked(start + u + 1)),
                both,
                TRANSPOSED,
                preferred_element_type=jnp.float32,
            )
            return result[:scen], result[scen:]

        def add(u, product):
            place = pl.multiple_of(rows_ref[start + u] * scen, scen)
            acc_ref[pl.ds(place, scen), :] += product

        trailing_adds(width, products, add)
        return 0

    lax.fori_loop(0, tiles_ref.shape[0] // width, body, 0)
    for part, out_ref in enumerate(outs):
        out_ref[...] = part_rows_of(acc_ref, 1 - core_ref[0], part, out_ref.shape[0]).astype(jnp.bfloat16)


def running(values, trailing, terms):
    length = values.shape[0]
    row_iota = lax.broadcasted_iota(jnp.int32, (length, length), 0)
    col_iota = lax.broadcasted_iota(jnp.int32, (length, length), 1)
    keep = ((col_iota >= row_iota) if trailing else (row_iota >= col_iota)).astype(jnp.float32).astype(jnp.bfloat16)
    total = None
    for _ in range(terms):
        term = values.astype(jnp.bfloat16)
        values = values - term.astype(jnp.float32)
        part = jnp.dot(keep, term, preferred_element_type=jnp.float32)
        total = part if total is None else total + part
    return total


def primal_kernel(dims, first, last, *refs):
    n_row, n_col, scen_local, time_block, _, own_tiles = dims
    refs = list(refs)
    recv_ref, inc_ref = refs[:2]
    cum_ref = None if first else refs[2]
    cost_ref, start_ref, len_ref, inc_out, send_ref = refs[2 + (not first) :][:5]
    cum_out = None if last else refs[-1]
    window, flight_local = cost_ref.shape
    side = flight_local // own_tiles
    piece = own_tiles * time_block
    tau_step = 0.6 / math.sqrt(window)
    minutes = lax.broadcasted_iota(jnp.int32, (window, flight_local), 0)
    begin = start_ref[...]
    upper = ((minutes >= begin) & (minutes < begin + len_ref[...])).astype(jnp.float32)
    slopes = []
    for j in range(scen_local):
        bands = []
        for h in range(n_col):
            total = recv_ref[h, pl.ds(j * piece, piece), :].astype(jnp.float32)
            for g in range(1, n_row):
                total = total + recv_ref[g * n_col + h, pl.ds(j * piece, piece), :].astype(jnp.float32)
            bands.append(
                jnp.concatenate([total[f * time_block : (f + 1) * time_block] for f in range(own_tiles)], axis=1)
            )
        slopes.append(jnp.concatenate(bands, axis=0) + cost_ref[...])
    gradient = running(jnp.concatenate(slopes, axis=1), True, 2)
    old = jnp.concatenate([inc_ref[j] for j in range(scen_local)], axis=1)
    if first:
        old_sum = running(old, False, 3)
    else:
        old_sum = jnp.concatenate([cum_ref[j] for j in range(scen_local)], axis=1)
    fresh = jnp.clip(old - tau_step * gradient, 0.0, jnp.concatenate([upper] * scen_local, axis=1))
    fresh_sum = running(fresh, False, 3)
    probe = (2.0 * fresh_sum - old_sum).astype(jnp.bfloat16)
    for j in range(scen_local):
        lanes = slice(j * flight_local, (j + 1) * flight_local)
        inc_out[j] = fresh[:, lanes]
        if not last:
            cum_out[j] = fresh_sum[:, lanes]
        for h in range(n_col):
            band = probe[h * time_block : (h + 1) * time_block, lanes]
            block = jnp.concatenate([band[:, f * side : (f + 1) * side] for f in range(own_tiles)], axis=0)
            for g in range(n_row):
                send_ref[g * n_col + h, pl.ds(j * piece, piece), :] = block


def own_sum(part, core_ref, image_ref, other_ref):
    own = part_rows_of(image_ref, core_ref[0], part, other_ref.shape[0])
    return own + other_ref[...].astype(jnp.float32)


def pair_kernel(part, core_ref, image_ref, other_ref, out_ref):
    out_ref[...] = own_sum(part, core_ref, image_ref, other_ref).astype(jnp.bfloat16)


def sum_kernel(first_ref, second_ref, out_ref):
    out_ref[...] = (first_ref[...].astype(jnp.float32) + second_ref[...].astype(jnp.float32)).astype(jnp.bfloat16)


def dual_kernel(remote, part, first, last, core_ref, image_ref, other_ref, *refs):
    parts, (dual_ref, cap_ref, dual_out) = refs[:remote], refs[remote : remote + 3]
    total = own_sum(part, core_ref, image_ref, other_ref)
    for received in parts:
        total = total + received[...].astype(jnp.float32)
    bands, row_tiles, band, side = cap_ref.shape
    rows = row_tiles // (2 * PARTS)
    begin = row_part(core_ref[0], part, rows)

    def own_rows(ref):
        return jnp.concatenate([ref[a, pl.ds(begin, rows)] for a in range(bands)], axis=1).reshape(-1, side)

    old = own_rows(dual_ref) if first else dual_ref[...]
    fresh = jnp.maximum(old + SIGMA_STEP * (total - own_rows(cap_ref).astype(jnp.float32)), 0.0)
    if last:
        value = fresh.reshape(rows, bands * band, side)
        for a in range(bands):
            dual_out[a] = value[:, a * band : (a + 1) * band]
    else:
        dual_out[...] = fresh
        refs[-1][...] = fresh.astype(jnp.bfloat16)


def part_copies(core, parts, out_ref, sems, used=0):
    copies = []
    for i, ref in parts:
        bands, rows = ref.shape[:2]
        for a in range(bands):
            place = out_ref.at[a, pl.ds(row_part(core, i, rows), rows)]
            copies.append(pltpu.make_async_copy(ref.at[a], place, sems.at[used + len(copies)]))
    return copies


def finish(copies):
    for copy in copies:
        copy.start()
    for copy in copies:
        copy.wait()


def own_results_kernel(core_ref, primal_ref, *refs):
    (*own, other), (primal_out, duals_out, sems) = refs[: PARTS + 1], refs[PARTS + 1 :]
    copies = part_copies(core_ref[0], list(enumerate(own)), duals_out, sems)
    copies += part_copies(1 - core_ref[0], [(0, other)], duals_out, sems, len(copies))
    copies.append(pltpu.make_async_copy(primal_ref, primal_out, sems.at[len(copies)]))
    finish(copies)


def other_results_kernel(core_ref, _, *refs):
    parts, (duals_out, sems) = refs[: PARTS - 1], refs[PARTS - 1 :]
    finish(part_copies(1 - core_ref[0], list(enumerate(parts, 1)), duals_out, sems))


def per_device(
    tile_values, tile_rows, tile_cols, increments, dual_vars, flight_cost, win_start, win_len, capacity
):
    n_row, n_col = lax.axis_size("row"), lax.axis_size("col")
    count, side = tile_values.shape[2], tile_values.shape[3]
    scen_local, window, flight_local = increments.shape
    scen, row_length = dual_vars.shape
    row_tiles = row_length // side
    time_block = window // n_col
    flight_tiles = flight_local * n_col // side
    own_tiles = flight_local // side
    col_tiles = time_block * flight_tiles
    dims = (n_row, n_col, scen_local, time_block, flight_tiles, own_tiles)
    message = (n_row * n_col, scen_local * own_tiles * time_block, side)
    part_rows = row_tiles * scen // (2 * PARTS)
    pitch = scen + PITCH_PAD
    band = 8

    rows, cols = tile_rows.reshape(count), tile_cols.reshape(count)
    core = (lax.axis_index("col") % 2).reshape(1)
    cost = pl.CostEstimate(flops=2 * count * scen * side * side, bytes_accessed=count * side * side, transcendentals=0)
    acc_cols = pltpu.VMEM((col_tiles * pitch, side), jnp.float32)
    picked_duals = pltpu.VMEM((row_tiles, scen, side), jnp.bfloat16)
    messages = jax.ShapeDtypeStruct(message, jnp.bfloat16)
    part_f32 = jax.ShapeDtypeStruct((part_rows, side), jnp.float32)
    part_out = jax.ShapeDtypeStruct((scen // band, row_tiles // (2 * PARTS), band, side), jnp.float32)
    part_bf16 = jax.ShapeDtypeStruct((part_rows, side), jnp.bfloat16)

    def banded(array):
        return array.reshape(scen // band, band, row_tiles, side).transpose(0, 2, 1, 3)

    def in_hbm(array):
        return pltpu.with_memory_space_constraint(array, pltpu.HBM)

    def first_backward(duals):
        return pl.pallas_call(
            functools.partial(first_backward_kernel, dims, pitch),
            in_specs=[scalars()] + [pl.BlockSpec(memory_space=pltpu.HBM)] * 4,
            out_specs=[whole(), whole()],
            out_shape=[messages, pltpu.VMEM((count, side, side), jnp.bfloat16)],
            scratch_shapes=[
                pltpu.SMEM((count,), jnp.int32),
                pltpu.SMEM((count,), jnp.int32),
                pltpu.VMEM(duals.shape, jnp.float32),
                picked_duals,
                acc_cols,
                pltpu.SemaphoreType.DMA((count // FIRST_UNROLL + 3,)),
            ],
            compiler_params=params(),
            cost_estimate=cost,
            name="first_backward_products",
        )(core, in_hbm(rows), in_hbm(cols), in_hbm(duals), in_hbm(tile_values.reshape(count, side, side)))

    def in_vmem(array):
        return pltpu.with_memory_space_constraint(array, pltpu.VMEM)

    def backward(rounded, tiles):
        pieces = [*rounded, *map(swap_core, rounded)]
        cleared = pl.pallas_call(
            functools.partial(clear_kernel, scen, pitch),
            out_specs=whole(),
            out_shape=acc_cols,
            compiler_params=params(),
            name="clear_sums",
        )()
        return pl.pallas_call(
            functools.partial(backward_kernel, dims, pitch),
            in_specs=[scalars()] * 3 + [whole()] * (2 + len(pieces)),
            out_specs=[whole()] * 2,
            out_shape=[messages, acc_cols],
            input_output_aliases={4: 1},
            scratch_shapes=[picked_duals],
            compiler_params=params(),
            cost_estimate=cost,
            name="backward_products",
        )(core, rows, cols, in_vmem(tiles), in_vmem(cleared), *pieces)[0]

    def forward(probe, tiles):
        return pl.pallas_call(
            functools.partial(forward_kernel, dims, pitch),
            in_specs=[scalars()] * 3 + [whole()] * 2,
            out_specs=[whole()] * (1 + PARTS),
            out_shape=[jax.ShapeDtypeStruct((row_tiles * scen, side), jnp.float32)] + [part_bf16] * PARTS,
            scratch_shapes=[acc_cols],
            compiler_params=params(),
            cost_estimate=cost,
            name="forward_products",
        )(core, rows, cols, probe, in_vmem(tiles))

    def primal_step(recv, primal, cumulative, last):
        first = cumulative is None
        state = (primal,) if first else (primal, cumulative)
        shape = jax.ShapeDtypeStruct(primal.shape, jnp.float32)
        out_shape = [pltpu.VMEM(primal.shape, jnp.float32), messages] if last else [shape, messages, shape]
        return pl.pallas_call(
            functools.partial(primal_kernel, dims, first, last),
            in_specs=[whole()] * (4 + len(state)),
            out_specs=[whole()] * len(out_shape),
            out_shape=out_shape,
            compiler_params=params(),
            name="primal_update",
        )(recv, *state, flight_cost, win_start.reshape(1, -1), win_len.reshape(1, -1))

    def swap_core(value):
        return lax.ppermute(value, "col", [(i, i ^ 1) for i in range(n_col)])

    bits = (n_col // 2).bit_length() - 1

    def swap_chip(value, step):
        return lax.ppermute(value, "col", [(i, i ^ (2 << (step + i % 2) % bits)) for i in range(n_col)])

    def bf16_sum(first, second, name):
        return pl.pallas_call(
            sum_kernel,
            in_specs=[whole()] * 2,
            out_specs=whole(),
            out_shape=part_bf16,
            compiler_params=params(),
            name=name,
        )(first, second)

    def dual_step(part, image, away, dual, first, last):
        other = swap_core(away)
        partial = pl.pallas_call(
            functools.partial(pair_kernel, part),
            in_specs=[scalars()] + [whole()] * 2,
            out_specs=whole(),
            out_shape=part_bf16,
            compiler_params=params(),
            name="core_pair_sum",
        )(core, image, other)
        parts = []
        for step in range(bits):
            parts.append(swap_chip(partial, step))
            if step + 1 < bits:
                partial = bf16_sum(partial, parts[-1], "chip_sum")
        out_shape = [part_out] if last else [part_f32, part_bf16]
        return pl.pallas_call(
            functools.partial(dual_kernel, bits, part, first, last),
            in_specs=[scalars()] + [whole()] * (bits + 4),
            out_specs=[whole()] * len(out_shape),
            out_shape=out_shape,
            compiler_params=params(),
            name="dual_update",
        )(core, image, other, *parts, dual, banded(capacity))

    def results(primal, owned):
        duals_shape = jax.ShapeDtypeStruct((scen // band, row_tiles, band, side), jnp.float32)
        hbm = pl.BlockSpec(memory_space=pltpu.HBM)
        copies = scen // band
        others = [swap_core(part) for part in owned]
        primal_out, duals_out = pl.pallas_call(
            own_results_kernel,
            in_specs=[scalars()] + [whole()] * (2 + PARTS),
            out_specs=[hbm, hbm],
            out_shape=[jax.ShapeDtypeStruct(primal.shape, jnp.float32), duals_shape],
            scratch_shapes=[pltpu.SemaphoreType.DMA(((PARTS + 1) * copies + 1,))],
            compiler_params=params(),
            name="own_results",
        )(core, in_vmem(primal), *owned, others[0])
        duals_out = pl.pallas_call(
            other_results_kernel,
            in_specs=[scalars(), hbm] + [whole()] * (PARTS - 1),
            out_specs=hbm,
            out_shape=duals_shape,
            input_output_aliases={1: 0},
            scratch_shapes=[pltpu.SemaphoreType.DMA(((PARTS - 1) * copies,))],
            compiler_params=params(),
            name="other_results",
        )(core, duals_out, *others[1:])
        return primal_out, duals_out.transpose(0, 2, 1, 3).reshape(scen, row_length)

    send, tiles = first_backward(banded(dual_vars))
    duals, primal, cumulative = [banded(dual_vars)] * PARTS, increments, None
    for sweep in range(ITERS):
        last = sweep + 1 == ITERS
        if sweep:
            send = backward(rounded, tiles)
        recv = lax.all_to_all(send, ("row", "col"), 0, 0, tiled=True)
        primal, send, *cumulative = primal_step(recv, primal, cumulative, last)
        cumulative = None if last else cumulative[0]
        probe = lax.all_to_all(send, ("row", "col"), 0, 0, tiled=True)
        image, *aways = forward(probe, tiles)
        updates = [
            dual_step(part, image, aways[part], duals[part], sweep == 0, last)
            for part in range(PARTS)
        ]
        duals = [update[0] for update in updates]
        rounded = None if last else [update[1] for update in updates]
    return results(primal, duals)


def solution(mesh):
    placed = (
        P("row", "col", None, None, None),
        P("row", "col", None),
        P("row", "col", None),
        P("row", None, "col"),
        P(None, "row"),
        P(None, "col"),
        P("col"),
        P("col"),
        P(None, "row"),
    )
    return jax.shard_map(
        per_device,
        mesh=mesh,
        in_specs=placed,
        out_specs=(P("row", None, "col"), P(None, "row")),
        check_vma=False,
    )
```

```python
import functools
import math

import jax
import jax.numpy as jnp
from jax import lax
from jax.experimental import pallas as pl
from jax.experimental.pallas import tpu as pltpu
from jax.sharding import PartitionSpec as P

ITERS = 2
SIGMA_STEP = 0.2
PARTS = 2
UNROLL = 256
FIRST_UNROLL = 32
TRAIL = 16
PITCH_PAD = 8
VMEM_BYTES = 24 * 1024 * 1024
TRANSPOSED = (((1,), (1,)), ((), ()))


def params():
    return pltpu.CompilerParams(vmem_limit_bytes=VMEM_BYTES)


def whole():
    return pl.BlockSpec(memory_space=pltpu.VMEM)


def scalars():
    return pl.BlockSpec(memory_space=pltpu.SMEM)


def stacked_pair(first, second):
    zero = jnp.zeros_like(first)
    return jnp.concatenate(
        [jnp.concatenate([first, zero], axis=1), jnp.concatenate([zero, second], axis=1)], axis=0
    )


def column_place(dims, column, pitch):
    time_block, flight_tiles = dims[3], dims[4]
    return pl.multiple_of((column % flight_tiles * time_block + column // flight_tiles) * pitch, 8)


def trailing_adds(width, group, products, add):
    waiting = []
    for u in range(0, width, group):
        waiting += zip(range(u, u + group), products(u))
        while len(waiting) > TRAIL:
            add(*waiting.pop(0))
    for item in waiting:
        add(*item)


def backward_blocks(dims, pitch, width, rows_ref, cols_ref, duals_ref, tiles_ref, acc_ref, start):
    scen = dims[0] * dims[2]

    def products(u):
        pair = stacked_pair(duals_ref[rows_ref[start + u]], duals_ref[rows_ref[start + u + 1]])
        both = tiles_ref[pl.ds(start + u, 2)]
        result = jnp.dot(pair, both.reshape(-1, both.shape[2]), preferred_element_type=jnp.float32)
        return result[:scen], result[scen:]

    def add(u, product):
        place = column_place(dims, cols_ref[start + u], pitch)
        acc_ref[pl.ds(place, scen), :] += product

    trailing_adds(width, 2, products, add)


def round_sums(dims, pitch, acc_ref):
    scen, time_block, flight_tiles = dims[0] * dims[2], dims[3], dims[4]
    lost = [jnp.zeros((scen, acc_ref.shape[1]), jnp.float32)] * flight_tiles
    for minute in reversed(range(time_block)):
        for f in range(flight_tiles):
            place = pl.ds((f * time_block + minute) * pitch, scen)
            value = acc_ref[place, :] + lost[f]
            rounded = value.astype(jnp.bfloat16).astype(jnp.float32)
            lost[f] = value - rounded
            acc_ref[place, :] = rounded


def write_messages(dims, pitch, acc_ref, out_ref):
    n_row, n_col, scen_local, time_block, _, own_tiles = dims
    piece = own_tiles * time_block
    round_sums(dims, pitch, acc_ref)
    for group in range(n_row):
        for column in range(n_col):
            for j in range(scen_local):
                base = column * own_tiles * time_block * pitch + group * scen_local + j
                parts = [
                    acc_ref[pl.ds(base + f * time_block * pitch, time_block, stride=pitch), :]
                    for f in range(own_tiles)
                ]
                out_ref[group * n_col + column, pl.ds(j * piece, piece), :] = jnp.concatenate(
                    parts, axis=0
                ).astype(jnp.bfloat16)


def first_backward_kernel(
    dims, pitch, core_ref, row_source, col_source, dual_source, source_ref, out_ref, tiles_ref,
    rows_ref, cols_ref, bands_ref, duals_ref, acc_ref, sems
):
    count, pieces = tiles_ref.shape[0], sems.shape[0] - 3
    chunk = count // pieces
    lists = [
        pltpu.make_async_copy(row_source, rows_ref, sems.at[pieces]),
        pltpu.make_async_copy(col_source, cols_ref, sems.at[pieces + 1]),
        pltpu.make_async_copy(dual_source, bands_ref, sems.at[pieces + 2]),
    ]
    copies = [
        pltpu.make_async_copy(source_ref.at[pl.ds(i * chunk, chunk)], tiles_ref.at[pl.ds(i * chunk, chunk)], sems.at[i])
        for i in range(pieces)
    ]
    for copy in lists + copies:
        copy.start()
    acc_ref[...] = jnp.zeros_like(acc_ref)
    for copy in lists:
        copy.wait()
    bands = [bands_ref[a].astype(jnp.bfloat16) for a in range(bands_ref.shape[0])]
    duals_ref[...] = jnp.concatenate(bands, axis=1)

    def body(index, _):
        backward_blocks(
            dims, pitch, FIRST_UNROLL, rows_ref, cols_ref, duals_ref, tiles_ref, acc_ref, index * FIRST_UNROLL
        )
        return 0

    for i, copy in enumerate(copies):
        copy.wait()
        lax.fori_loop(i * chunk // FIRST_UNROLL, (i + 1) * chunk // FIRST_UNROLL, body, 0)
    write_messages(dims, pitch, acc_ref, out_ref)


def row_part(core, part, rows):
    return (core * PARTS + part) * rows


def part_rows_of(ref, core, part, size):
    return ref[pl.ds(pl.multiple_of(row_part(core, part, size), size), size), :]


def clear_kernel(scen, pitch, acc_ref):
    for row in range(0, acc_ref.shape[0], pitch):
        acc_ref[pl.ds(row, scen), :] = jnp.zeros((scen, acc_ref.shape[1]), jnp.float32)


def backward_kernel(dims, pitch, core_ref, rows_ref, cols_ref, tiles_ref, _, *refs):
    pieces, (out_ref, acc_ref, duals_ref) = refs[: 2 * PARTS], refs[2 * PARTS :]
    for i, piece in enumerate(pieces):
        core = core_ref[0] if i < PARTS else 1 - core_ref[0]
        scen, side = duals_ref.shape[1:]
        rows = piece.shape[0] // scen
        duals_ref[pl.ds(row_part(core, i % PARTS, rows), rows)] = piece[...].reshape(rows, scen, side)
    width = min(UNROLL, tiles_ref.shape[0])

    def body(index, _):
        backward_blocks(dims, pitch, width, rows_ref, cols_ref, duals_ref, tiles_ref, acc_ref, index * width)
        return 0

    lax.fori_loop(0, tiles_ref.shape[0] // width, body, 0)
    write_messages(dims, pitch, acc_ref, out_ref)


def forward_kernel(dims, pitch, core_ref, rows_ref, cols_ref, probe_ref, tiles_ref, *refs):
    n_row, n_col, scen_local, time_block, _, own_tiles = dims
    scen = n_row * scen_local
    piece = own_tiles * time_block
    (acc_ref, *outs), flat_ref = refs[:-1], refs[-1]
    acc_ref[...] = jnp.zeros_like(acc_ref)
    for group in range(n_row):
        for column in range(n_col):
            for j in range(scen_local):
                base = column * own_tiles * time_block * pitch + group * scen_local + j
                block = probe_ref[group * n_col + column, pl.ds(j * piece, piece), :].astype(jnp.float32)
                for f in range(own_tiles):
                    flat_ref[pl.ds(base + f * time_block * pitch, time_block, stride=pitch), :] = block[
                        f * time_block : (f + 1) * time_block
                    ]

    def picked(index):
        return flat_ref[pl.ds(column_place(dims, cols_ref[index], pitch), scen), :].astype(jnp.bfloat16)

    width = min(UNROLL, tiles_ref.shape[0])

    def body(index, _):
        start = index * width

        def products(u):
            first, second, third, fourth = (picked(start + u + i) for i in range(4))
            zero = jnp.zeros_like(first)
            left = jnp.concatenate([first, second, zero, zero], axis=0)
            right = jnp.concatenate([zero, zero, third, fourth], axis=0)
            sides = [tiles_ref[pl.ds(start + u + i, 2)] for i in (0, 2)]
            both = jnp.concatenate([two.reshape(-1, two.shape[2]) for two in sides], axis=1)
            result = lax.dot_general(
                jnp.concatenate([left, right], axis=1), both, TRANSPOSED, preferred_element_type=jnp.float32
            )
            side = tiles_ref.shape[1]
            return [
                result[i * scen : (i + 1) * scen, i % 2 * side : (i % 2 + 1) * side] for i in range(4)
            ]

        def add(u, product):
            place = pl.multiple_of(rows_ref[start + u] * scen, scen)
            acc_ref[pl.ds(place, scen), :] += product

        trailing_adds(width, 4, products, add)
        return 0

    lax.fori_loop(0, tiles_ref.shape[0] // width, body, 0)
    for part, out_ref in enumerate(outs):
        out_ref[...] = part_rows_of(acc_ref, 1 - core_ref[0], part, out_ref.shape[0]).astype(jnp.bfloat16)


def running(values, trailing, terms):
    length = values.shape[0]
    row_iota = lax.broadcasted_iota(jnp.int32, (length, length), 0)
    col_iota = lax.broadcasted_iota(jnp.int32, (length, length), 1)
    keep = ((col_iota >= row_iota) if trailing else (row_iota >= col_iota)).astype(jnp.float32).astype(jnp.bfloat16)
    total = None
    for _ in range(terms):
        term = values.astype(jnp.bfloat16)
        values = values - term.astype(jnp.float32)
        part = jnp.dot(keep, term, preferred_element_type=jnp.float32)
        total = part if total is None else total + part
    return total


def primal_kernel(dims, first, last, *refs):
    n_row, n_col, scen_local, time_block, _, own_tiles = dims
    refs = list(refs)
    recv_ref, inc_ref = refs[:2]
    cum_ref = None if first else refs[2]
    cost_ref, start_ref, len_ref, inc_out, send_ref = refs[2 + (not first) :][:5]
    cum_out = None if last else refs[-1]
    window, flight_local = cost_ref.shape
    side = flight_local // own_tiles
    piece = own_tiles * time_block
    tau_step = 0.6 / math.sqrt(window)
    minutes = lax.broadcasted_iota(jnp.int32, (window, flight_local), 0)
    begin = start_ref[...]
    upper = ((minutes >= begin) & (minutes < begin + len_ref[...])).astype(jnp.float32)
    slopes = []
    for j in range(scen_local):
        bands = []
        for h in range(n_col):
            total = recv_ref[h, pl.ds(j * piece, piece), :].astype(jnp.float32)
            for g in range(1, n_row):
                total = total + recv_ref[g * n_col + h, pl.ds(j * piece, piece), :].astype(jnp.float32)
            bands.append(
                jnp.concatenate([total[f * time_block : (f + 1) * time_block] for f in range(own_tiles)], axis=1)
            )
        slopes.append(jnp.concatenate(bands, axis=0) + cost_ref[...])
    gradient = running(jnp.concatenate(slopes, axis=1), True, 2)
    old = jnp.concatenate([inc_ref[j] for j in range(scen_local)], axis=1)
    if first:
        old_sum = running(old, False, 3)
    else:
        old_sum = jnp.concatenate([cum_ref[j] for j in range(scen_local)], axis=1)
    fresh = jnp.clip(old - tau_step * gradient, 0.0, jnp.concatenate([upper] * scen_local, axis=1))
    fresh_sum = running(fresh, False, 3)
    probe = (2.0 * fresh_sum - old_sum).astype(jnp.bfloat16)
    for j in range(scen_local):
        lanes = slice(j * flight_local, (j + 1) * flight_local)
        inc_out[j] = fresh[:, lanes]
        if not last:
            cum_out[j] = fresh_sum[:, lanes]
        for h in range(n_col):
            band = probe[h * time_block : (h + 1) * time_block, lanes]
            block = jnp.concatenate([band[:, f * side : (f + 1) * side] for f in range(own_tiles)], axis=0)
            for g in range(n_row):
                send_ref[g * n_col + h, pl.ds(j * piece, piece), :] = block


def own_sum(part, core_ref, image_ref, other_ref):
    own = part_rows_of(image_ref, core_ref[0], part, other_ref.shape[0])
    return own + other_ref[...].astype(jnp.float32)


def pair_kernel(part, core_ref, image_ref, other_ref, out_ref):
    out_ref[...] = own_sum(part, core_ref, image_ref, other_ref).astype(jnp.bfloat16)


def sum_kernel(first_ref, second_ref, out_ref):
    out_ref[...] = (first_ref[...].astype(jnp.float32) + second_ref[...].astype(jnp.float32)).astype(jnp.bfloat16)


def dual_kernel(remote, part, first, last, core_ref, image_ref, other_ref, *refs):
    parts, (dual_ref, cap_ref, dual_out) = refs[:remote], refs[remote : remote + 3]
    total = own_sum(part, core_ref, image_ref, other_ref)
    for received in parts:
        total = total + received[...].astype(jnp.float32)
    bands, row_tiles, band, side = cap_ref.shape
    rows = row_tiles // (2 * PARTS)
    begin = row_part(core_ref[0], part, rows)

    def own_rows(ref):
        return jnp.concatenate([ref[a, pl.ds(begin, rows)] for a in range(bands)], axis=1).reshape(-1, side)

    old = own_rows(dual_ref) if first else dual_ref[...]
    fresh = jnp.maximum(old + SIGMA_STEP * (total - own_rows(cap_ref).astype(jnp.float32)), 0.0)
    if last:
        value = fresh.reshape(rows, bands * band, side)
        for a in range(bands):
            dual_out[a] = value[:, a * band : (a + 1) * band]
    else:
        dual_out[...] = fresh
        refs[-1][...] = fresh.astype(jnp.bfloat16)


def part_copies(core, parts, out_ref, sems, used=0):
    copies = []
    for i, ref in parts:
        bands, rows = ref.shape[:2]
        for a in range(bands):
            place = out_ref.at[a, pl.ds(row_part(core, i, rows), rows)]
            copies.append(pltpu.make_async_copy(ref.at[a], place, sems.at[used + len(copies)]))
    return copies


def finish(copies):
    for copy in copies:
        copy.start()
    for copy in copies:
        copy.wait()


def own_results_kernel(core_ref, primal_ref, *refs):
    (*own, other), (primal_out, duals_out, sems) = refs[: PARTS + 1], refs[PARTS + 1 :]
    copies = part_copies(core_ref[0], list(enumerate(own)), duals_out, sems)
    copies += part_copies(1 - core_ref[0], [(0, other)], duals_out, sems, len(copies))
    copies.append(pltpu.make_async_copy(primal_ref, primal_out, sems.at[len(copies)]))
    finish(copies)


def other_results_kernel(core_ref, _, *refs):
    parts, (duals_out, sems) = refs[: PARTS - 1], refs[PARTS - 1 :]
    finish(part_copies(1 - core_ref[0], list(enumerate(parts, 1)), duals_out, sems))


def per_device(
    tile_values, tile_rows, tile_cols, increments, dual_vars, flight_cost, win_start, win_len, capacity
):
    n_row, n_col = lax.axis_size("row"), lax.axis_size("col")
    count, side = tile_values.shape[2], tile_values.shape[3]
    scen_local, window, flight_local = increments.shape
    scen, row_length = dual_vars.shape
    row_tiles = row_length // side
    time_block = window // n_col
    flight_tiles = flight_local * n_col // side
    own_tiles = flight_local // side
    col_tiles = time_block * flight_tiles
    dims = (n_row, n_col, scen_local, time_block, flight_tiles, own_tiles)
    message = (n_row * n_col, scen_local * own_tiles * time_block, side)
    part_rows = row_tiles * scen // (2 * PARTS)
    pitch = scen + PITCH_PAD
    band = 8

    rows, cols = tile_rows.reshape(count), tile_cols.reshape(count)
    core = (lax.axis_index("col") % 2).reshape(1)
    cost = pl.CostEstimate(flops=2 * count * scen * side * side, bytes_accessed=count * side * side, transcendentals=0)
    acc_cols = pltpu.VMEM((col_tiles * pitch, side), jnp.float32)
    picked_duals = pltpu.VMEM((row_tiles, scen, side), jnp.bfloat16)
    messages = jax.ShapeDtypeStruct(message, jnp.bfloat16)
    part_f32 = jax.ShapeDtypeStruct((part_rows, side), jnp.float32)
    part_out = jax.ShapeDtypeStruct((scen // band, row_tiles // (2 * PARTS), band, side), jnp.float32)
    part_bf16 = jax.ShapeDtypeStruct((part_rows, side), jnp.bfloat16)

    def banded(array):
        return array.reshape(scen // band, band, row_tiles, side).transpose(0, 2, 1, 3)

    def in_hbm(array):
        return pltpu.with_memory_space_constraint(array, pltpu.HBM)

    def first_backward(duals):
        return pl.pallas_call(
            functools.partial(first_backward_kernel, dims, pitch),
            in_specs=[scalars()] + [pl.BlockSpec(memory_space=pltpu.HBM)] * 4,
            out_specs=[whole(), whole()],
            out_shape=[messages, pltpu.VMEM((count, side, side), jnp.bfloat16)],
            scratch_shapes=[
                pltpu.SMEM((count,), jnp.int32),
                pltpu.SMEM((count,), jnp.int32),
                pltpu.VMEM(duals.shape, jnp.float32),
                picked_duals,
                acc_cols,
                pltpu.SemaphoreType.DMA((count // FIRST_UNROLL + 3,)),
            ],
            compiler_params=params(),
            cost_estimate=cost,
            name="first_backward_products",
        )(core, in_hbm(rows), in_hbm(cols), in_hbm(duals), in_hbm(tile_values.reshape(count, side, side)))

    def in_vmem(array):
        return pltpu.with_memory_space_constraint(array, pltpu.VMEM)

    def backward(rounded, tiles):
        pieces = [*rounded, *map(swap_core, rounded)]
        cleared = pl.pallas_call(
            functools.partial(clear_kernel, scen, pitch),
            out_specs=whole(),
            out_shape=acc_cols,
            compiler_params=params(),
            name="clear_sums",
        )()
        return pl.pallas_call(
            functools.partial(backward_kernel, dims, pitch),
            in_specs=[scalars()] * 3 + [whole()] * (2 + len(pieces)),
            out_specs=[whole()] * 2,
            out_shape=[messages, acc_cols],
            input_output_aliases={4: 1},
            scratch_shapes=[picked_duals],
            compiler_params=params(),
            cost_estimate=cost,
            name="backward_products",
        )(core, rows, cols, in_vmem(tiles), in_vmem(cleared), *pieces)[0]

    def forward(probe, tiles):
        return pl.pallas_call(
            functools.partial(forward_kernel, dims, pitch),
            in_specs=[scalars()] * 3 + [whole()] * 2,
            out_specs=[whole()] * (1 + PARTS),
            out_shape=[jax.ShapeDtypeStruct((row_tiles * scen, side), jnp.float32)] + [part_bf16] * PARTS,
            scratch_shapes=[acc_cols],
            compiler_params=params(),
            cost_estimate=cost,
            name="forward_products",
        )(core, rows, cols, probe, in_vmem(tiles))

    def primal_step(recv, primal, cumulative, last):
        first = cumulative is None
        state = (primal,) if first else (primal, cumulative)
        shape = jax.ShapeDtypeStruct(primal.shape, jnp.float32)
        out_shape = [pltpu.VMEM(primal.shape, jnp.float32), messages] if last else [shape, messages, shape]
        return pl.pallas_call(
            functools.partial(primal_kernel, dims, first, last),
            in_specs=[whole()] * (4 + len(state)),
            out_specs=[whole()] * len(out_shape),
            out_shape=out_shape,
            compiler_params=params(),
            name="primal_update",
        )(recv, *state, flight_cost, win_start.reshape(1, -1), win_len.reshape(1, -1))

    def swap_core(value):
        return lax.ppermute(value, "col", [(i, i ^ 1) for i in range(n_col)])

    bits = (n_col // 2).bit_length() - 1

    def swap_chip(value, step):
        return lax.ppermute(value, "col", [(i, i ^ (2 << (step + i % 2) % bits)) for i in range(n_col)])

    def bf16_sum(first, second, name):
        return pl.pallas_call(
            sum_kernel,
            in_specs=[whole()] * 2,
            out_specs=whole(),
            out_shape=part_bf16,
            compiler_params=params(),
            name=name,
        )(first, second)

    def dual_step(part, image, away, dual, first, last):
        other = swap_core(away)
        partial = pl.pallas_call(
            functools.partial(pair_kernel, part),
            in_specs=[scalars()] + [whole()] * 2,
            out_specs=whole(),
            out_shape=part_bf16,
            compiler_params=params(),
            name="core_pair_sum",
        )(core, image, other)
        parts = []
        for step in range(bits):
            parts.append(swap_chip(partial, step))
            if step + 1 < bits:
                partial = bf16_sum(partial, parts[-1], "chip_sum")
        out_shape = [part_out] if last else [part_f32, part_bf16]
        return pl.pallas_call(
            functools.partial(dual_kernel, bits, part, first, last),
            in_specs=[scalars()] + [whole()] * (bits + 4),
            out_specs=[whole()] * len(out_shape),
            out_shape=out_shape,
            compiler_params=params(),
            name="dual_update",
        )(core, image, other, *parts, dual, banded(capacity))

    def results(primal, owned):
        duals_shape = jax.ShapeDtypeStruct((scen // band, row_tiles, band, side), jnp.float32)
        hbm = pl.BlockSpec(memory_space=pltpu.HBM)
        copies = scen // band
        others = [swap_core(part) for part in owned]
        primal_out, duals_out = pl.pallas_call(
            own_results_kernel,
            in_specs=[scalars()] + [whole()] * (2 + PARTS),
            out_specs=[hbm, hbm],
            out_shape=[jax.ShapeDtypeStruct(primal.shape, jnp.float32), duals_shape],
            scratch_shapes=[pltpu.SemaphoreType.DMA(((PARTS + 1) * copies + 1,))],
            compiler_params=params(),
            name="own_results",
        )(core, in_vmem(primal), *owned, others[0])
        duals_out = pl.pallas_call(
            other_results_kernel,
            in_specs=[scalars(), hbm] + [whole()] * (PARTS - 1),
            out_specs=hbm,
            out_shape=duals_shape,
            input_output_aliases={1: 0},
            scratch_shapes=[pltpu.SemaphoreType.DMA(((PARTS - 1) * copies,))],
            compiler_params=params(),
            name="other_results",
        )(core, duals_out, *others[1:])
        return primal_out, duals_out.transpose(0, 2, 1, 3).reshape(scen, row_length)

    send, tiles = first_backward(banded(dual_vars))
    duals, primal, cumulative = [banded(dual_vars)] * PARTS, increments, None
    for sweep in range(ITERS):
        last = sweep + 1 == ITERS
        if sweep:
            send = backward(rounded, tiles)
        recv = lax.all_to_all(send, ("row", "col"), 0, 0, tiled=True)
        primal, send, *cumulative = primal_step(recv, primal, cumulative, last)
        cumulative = None if last else cumulative[0]
        probe = lax.all_to_all(send, ("row", "col"), 0, 0, tiled=True)
        image, *aways = forward(probe, tiles)
        updates = [
            dual_step(part, image, aways[part], duals[part], sweep == 0, last)
            for part in range(PARTS)
        ]
        duals = [update[0] for update in updates]
        rounded = None if last else [update[1] for update in updates]
    return results(primal, duals)


def solution(mesh):
    placed = (
        P("row", "col", None, None, None),
        P("row", "col", None),
        P("row", "col", None),
        P("row", None, "col"),
        P(None, "row"),
        P(None, "col"),
        P("col"),
        P("col"),
        P(None, "row"),
    )
    return jax.shard_map(
        per_device,
        mesh=mesh,
        in_specs=placed,
        out_specs=(P("row", None, "col"), P(None, "row")),
        check_vma=False,
    )
```

```python
import functools
import math

import jax
import jax.numpy as jnp
from jax import lax
from jax.experimental import pallas as pl
from jax.experimental.pallas import tpu as pltpu
from jax.sharding import PartitionSpec as P

ITERS = 2
SIGMA_STEP = 0.2
PARTS = 2
UNROLL = 256
FIRST_LOAD = 16
TRAIL = 16
PITCH_PAD = 8
VMEM_BYTES = 24 * 1024 * 1024
TRANSPOSED = (((1,), (1,)), ((), ()))


def params():
    return pltpu.CompilerParams(vmem_limit_bytes=VMEM_BYTES)


def whole():
    return pl.BlockSpec(memory_space=pltpu.VMEM)


def scalars():
    return pl.BlockSpec(memory_space=pltpu.SMEM)


def stacked_pair(first, second):
    zero = jnp.zeros_like(first)
    return jnp.concatenate(
        [jnp.concatenate([first, zero], axis=1), jnp.concatenate([zero, second], axis=1)], axis=0
    )


def column_place(dims, column, pitch):
    time_block, flight_tiles = dims[3], dims[4]
    return pl.multiple_of((column % flight_tiles * time_block + column // flight_tiles) * pitch, 8)


def trailing_adds(width, group, products, add):
    waiting = []
    for u in range(0, width, group):
        waiting += zip(range(u, u + group), products(u))
        while len(waiting) > TRAIL:
            add(*waiting.pop(0))
    for item in waiting:
        add(*item)


def backward_blocks(dims, pitch, width, rows_ref, cols_ref, duals_ref, tiles_ref, acc_ref, start, ready=None):
    scen = dims[0] * dims[2]

    def products(u):
        if ready is not None:
            ready(u)
        pair = stacked_pair(duals_ref[rows_ref[start + u]], duals_ref[rows_ref[start + u + 1]])
        both = tiles_ref[pl.ds(start + u, 2)]
        result = jnp.dot(pair, both.reshape(-1, both.shape[2]), preferred_element_type=jnp.float32)
        return result[:scen], result[scen:]

    def add(u, product):
        place = column_place(dims, cols_ref[start + u], pitch)
        acc_ref[pl.ds(place, scen), :] += product

    trailing_adds(width, 2, products, add)


def round_sums(dims, pitch, acc_ref):
    scen, time_block, flight_tiles = dims[0] * dims[2], dims[3], dims[4]
    lost = [jnp.zeros((scen, acc_ref.shape[1]), jnp.float32)] * flight_tiles
    for minute in reversed(range(time_block)):
        for f in range(flight_tiles):
            place = pl.ds((f * time_block + minute) * pitch, scen)
            value = acc_ref[place, :] + lost[f]
            rounded = value.astype(jnp.bfloat16).astype(jnp.float32)
            lost[f] = value - rounded
            acc_ref[place, :] = rounded


def write_messages(dims, pitch, acc_ref, out_ref):
    n_row, n_col, scen_local, time_block, _, own_tiles = dims
    piece = own_tiles * time_block
    round_sums(dims, pitch, acc_ref)
    for group in range(n_row):
        for column in range(n_col):
            for j in range(scen_local):
                base = column * own_tiles * time_block * pitch + group * scen_local + j
                parts = [
                    acc_ref[pl.ds(base + f * time_block * pitch, time_block, stride=pitch), :]
                    for f in range(own_tiles)
                ]
                out_ref[group * n_col + column, pl.ds(j * piece, piece), :] = jnp.concatenate(
                    parts, axis=0
                ).astype(jnp.bfloat16)


def first_backward_kernel(
    dims, pitch, core_ref, row_source, col_source, dual_source, source_ref, out_ref, tiles_ref,
    rows_ref, cols_ref, bands_ref, duals_ref, acc_ref, sems
):
    count, pieces = tiles_ref.shape[0], sems.shape[0] - 3
    chunk = count // pieces
    lists = [
        pltpu.make_async_copy(row_source, rows_ref, sems.at[pieces]),
        pltpu.make_async_copy(col_source, cols_ref, sems.at[pieces + 1]),
        pltpu.make_async_copy(dual_source, bands_ref, sems.at[pieces + 2]),
    ]
    copies = [
        pltpu.make_async_copy(source_ref.at[pl.ds(i * chunk, chunk)], tiles_ref.at[pl.ds(i * chunk, chunk)], sems.at[i])
        for i in range(pieces)
    ]
    for copy in lists + copies:
        copy.start()
    acc_ref[...] = jnp.zeros_like(acc_ref)
    for copy in lists:
        copy.wait()
    bands = [bands_ref[a].astype(jnp.bfloat16) for a in range(bands_ref.shape[0])]
    duals_ref[...] = jnp.concatenate(bands, axis=1)

    def ready(u):
        if u % chunk == 0:
            copies[u // chunk].wait()

    backward_blocks(dims, pitch, count, rows_ref, cols_ref, duals_ref, tiles_ref, acc_ref, 0, ready)
    write_messages(dims, pitch, acc_ref, out_ref)


def row_part(core, part, rows):
    return (core * PARTS + part) * rows


def part_rows_of(ref, core, part, size):
    return ref[pl.ds(pl.multiple_of(row_part(core, part, size), size), size), :]


def clear_kernel(scen, pitch, acc_ref):
    for row in range(0, acc_ref.shape[0], pitch):
        acc_ref[pl.ds(row, scen), :] = jnp.zeros((scen, acc_ref.shape[1]), jnp.float32)


def backward_kernel(dims, pitch, core_ref, rows_ref, cols_ref, tiles_ref, _, *refs):
    pieces, (out_ref, acc_ref, duals_ref) = refs[: 2 * PARTS], refs[2 * PARTS :]
    for i, piece in enumerate(pieces):
        core = core_ref[0] if i < PARTS else 1 - core_ref[0]
        scen, side = duals_ref.shape[1:]
        rows = piece.shape[0] // scen
        duals_ref[pl.ds(row_part(core, i % PARTS, rows), rows)] = piece[...].reshape(rows, scen, side)
    width = min(UNROLL, tiles_ref.shape[0])

    def body(index, _):
        backward_blocks(dims, pitch, width, rows_ref, cols_ref, duals_ref, tiles_ref, acc_ref, index * width)
        return 0

    lax.fori_loop(0, tiles_ref.shape[0] // width, body, 0)
    write_messages(dims, pitch, acc_ref, out_ref)


def forward_kernel(dims, pitch, core_ref, rows_ref, cols_ref, probe_ref, tiles_ref, *refs):
    n_row, n_col, scen_local, time_block, _, own_tiles = dims
    scen = n_row * scen_local
    piece = own_tiles * time_block
    (acc_ref, *outs), flat_ref = refs[:-1], refs[-1]
    acc_ref[...] = jnp.zeros_like(acc_ref)
    for group in range(n_row):
        for column in range(n_col):
            for j in range(scen_local):
                base = column * own_tiles * time_block * pitch + group * scen_local + j
                block = probe_ref[group * n_col + column, pl.ds(j * piece, piece), :].astype(jnp.float32)
                for f in range(own_tiles):
                    flat_ref[pl.ds(base + f * time_block * pitch, time_block, stride=pitch), :] = block[
                        f * time_block : (f + 1) * time_block
                    ]

    def picked(index):
        return flat_ref[pl.ds(column_place(dims, cols_ref[index], pitch), scen), :].astype(jnp.bfloat16)

    width = min(UNROLL, tiles_ref.shape[0])

    def body(index, _):
        start = index * width

        def products(u):
            first, second, third, fourth = (picked(start + u + i) for i in range(4))
            zero = jnp.zeros_like(first)
            left = jnp.concatenate([first, second, zero, zero], axis=0)
            right = jnp.concatenate([zero, zero, third, fourth], axis=0)
            sides = [tiles_ref[pl.ds(start + u + i, 2)] for i in (0, 2)]
            both = jnp.concatenate([two.reshape(-1, two.shape[2]) for two in sides], axis=1)
            result = lax.dot_general(
                jnp.concatenate([left, right], axis=1), both, TRANSPOSED, preferred_element_type=jnp.float32
            )
            side = tiles_ref.shape[1]
            return [
                result[i * scen : (i + 1) * scen, i % 2 * side : (i % 2 + 1) * side] for i in range(4)
            ]

        def add(u, product):
            place = pl.multiple_of(rows_ref[start + u] * scen, scen)
            acc_ref[pl.ds(place, scen), :] += product

        trailing_adds(width, 4, products, add)
        return 0

    lax.fori_loop(0, tiles_ref.shape[0] // width, body, 0)
    for part, out_ref in enumerate(outs):
        out_ref[...] = part_rows_of(acc_ref, 1 - core_ref[0], part, out_ref.shape[0]).astype(jnp.bfloat16)


def running(values, trailing, terms):
    length = values.shape[0]
    row_iota = lax.broadcasted_iota(jnp.int32, (length, length), 0)
    col_iota = lax.broadcasted_iota(jnp.int32, (length, length), 1)
    keep = ((col_iota >= row_iota) if trailing else (row_iota >= col_iota)).astype(jnp.float32).astype(jnp.bfloat16)
    total = None
    for _ in range(terms):
        term = values.astype(jnp.bfloat16)
        values = values - term.astype(jnp.float32)
        part = jnp.dot(keep, term, preferred_element_type=jnp.float32)
        total = part if total is None else total + part
    return total


def primal_kernel(dims, first, last, *refs):
    n_row, n_col, scen_local, time_block, _, own_tiles = dims
    refs = list(refs)
    recv_ref, inc_ref = refs[:2]
    cum_ref = None if first else refs[2]
    cost_ref, start_ref, len_ref, inc_out, send_ref = refs[2 + (not first) :][:5]
    cum_out = None if last else refs[-1]
    window, flight_local = cost_ref.shape
    side = flight_local // own_tiles
    piece = own_tiles * time_block
    tau_step = 0.6 / math.sqrt(window)
    minutes = lax.broadcasted_iota(jnp.int32, (window, flight_local), 0)
    begin = start_ref[...]
    upper = ((minutes >= begin) & (minutes < begin + len_ref[...])).astype(jnp.float32)
    slopes = []
    for j in range(scen_local):
        bands = []
        for h in range(n_col):
            total = recv_ref[h, pl.ds(j * piece, piece), :].astype(jnp.float32)
            for g in range(1, n_row):
                total = total + recv_ref[g * n_col + h, pl.ds(j * piece, piece), :].astype(jnp.float32)
            bands.append(
                jnp.concatenate([total[f * time_block : (f + 1) * time_block] for f in range(own_tiles)], axis=1)
            )
        slopes.append(jnp.concatenate(bands, axis=0) + cost_ref[...])
    gradient = running(jnp.concatenate(slopes, axis=1), True, 2)
    old = jnp.concatenate([inc_ref[j] for j in range(scen_local)], axis=1)
    if first:
        old_sum = running(old, False, 3)
    else:
        old_sum = jnp.concatenate([cum_ref[j] for j in range(scen_local)], axis=1)
    fresh = jnp.clip(old - tau_step * gradient, 0.0, jnp.concatenate([upper] * scen_local, axis=1))
    fresh_sum = running(fresh, False, 3)
    probe = (2.0 * fresh_sum - old_sum).astype(jnp.bfloat16)
    for j in range(scen_local):
        lanes = slice(j * flight_local, (j + 1) * flight_local)
        inc_out[j] = fresh[:, lanes]
        if not last:
            cum_out[j] = fresh_sum[:, lanes]
        for h in range(n_col):
            band = probe[h * time_block : (h + 1) * time_block, lanes]
            block = jnp.concatenate([band[:, f * side : (f + 1) * side] for f in range(own_tiles)], axis=0)
            for g in range(n_row):
                send_ref[g * n_col + h, pl.ds(j * piece, piece), :] = block


def own_sum(part, core_ref, image_ref, other_ref):
    own = part_rows_of(image_ref, core_ref[0], part, other_ref.shape[0])
    return own + other_ref[...].astype(jnp.float32)


def pair_kernel(part, core_ref, image_ref, other_ref, out_ref):
    out_ref[...] = own_sum(part, core_ref, image_ref, other_ref).astype(jnp.bfloat16)


def sum_kernel(first_ref, second_ref, out_ref):
    out_ref[...] = (first_ref[...].astype(jnp.float32) + second_ref[...].astype(jnp.float32)).astype(jnp.bfloat16)


def dual_kernel(remote, part, first, last, core_ref, image_ref, other_ref, *refs):
    parts, (dual_ref, cap_ref, dual_out) = refs[:remote], refs[remote : remote + 3]
    total = own_sum(part, core_ref, image_ref, other_ref)
    for received in parts:
        total = total + received[...].astype(jnp.float32)
    bands, row_tiles, band, side = cap_ref.shape
    rows = row_tiles // (2 * PARTS)
    begin = row_part(core_ref[0], part, rows)

    def own_rows(ref):
        return jnp.concatenate([ref[a, pl.ds(begin, rows)] for a in range(bands)], axis=1).reshape(-1, side)

    old = own_rows(dual_ref) if first else dual_ref[...]
    fresh = jnp.maximum(old + SIGMA_STEP * (total - own_rows(cap_ref).astype(jnp.float32)), 0.0)
    if last:
        value = fresh.reshape(rows, bands * band, side)
        for a in range(bands):
            dual_out[a] = value[:, a * band : (a + 1) * band]
    else:
        dual_out[...] = fresh
        refs[-1][...] = fresh.astype(jnp.bfloat16)


def part_copies(core, parts, out_ref, sems, used=0):
    copies = []
    for i, ref in parts:
        bands, rows = ref.shape[:2]
        for a in range(bands):
            place = out_ref.at[a, pl.ds(row_part(core, i, rows), rows)]
            copies.append(pltpu.make_async_copy(ref.at[a], place, sems.at[used + len(copies)]))
    return copies


def finish(copies):
    for copy in copies:
        copy.start()
    for copy in copies:
        copy.wait()


def own_results_kernel(core_ref, primal_ref, *refs):
    (*own, other), (primal_out, duals_out, sems) = refs[: PARTS + 1], refs[PARTS + 1 :]
    copies = part_copies(core_ref[0], list(enumerate(own)), duals_out, sems)
    copies += part_copies(1 - core_ref[0], [(0, other)], duals_out, sems, len(copies))
    copies.append(pltpu.make_async_copy(primal_ref, primal_out, sems.at[len(copies)]))
    finish(copies)


def other_results_kernel(core_ref, _, *refs):
    parts, (duals_out, sems) = refs[: PARTS - 1], refs[PARTS - 1 :]
    finish(part_copies(1 - core_ref[0], list(enumerate(parts, 1)), duals_out, sems))


def per_device(
    tile_values, tile_rows, tile_cols, increments, dual_vars, flight_cost, win_start, win_len, capacity
):
    n_row, n_col = lax.axis_size("row"), lax.axis_size("col")
    count, side = tile_values.shape[2], tile_values.shape[3]
    scen_local, window, flight_local = increments.shape
    scen, row_length = dual_vars.shape
    row_tiles = row_length // side
    time_block = window // n_col
    flight_tiles = flight_local * n_col // side
    own_tiles = flight_local // side
    col_tiles = time_block * flight_tiles
    dims = (n_row, n_col, scen_local, time_block, flight_tiles, own_tiles)
    message = (n_row * n_col, scen_local * own_tiles * time_block, side)
    part_rows = row_tiles * scen // (2 * PARTS)
    pitch = scen + PITCH_PAD
    band = 8

    rows, cols = tile_rows.reshape(count), tile_cols.reshape(count)
    core = (lax.axis_index("col") % 2).reshape(1)
    cost = pl.CostEstimate(flops=2 * count * scen * side * side, bytes_accessed=count * side * side, transcendentals=0)
    acc_cols = pltpu.VMEM((col_tiles * pitch, side), jnp.float32)
    picked_duals = pltpu.VMEM((row_tiles, scen, side), jnp.bfloat16)
    messages = jax.ShapeDtypeStruct(message, jnp.bfloat16)
    part_f32 = jax.ShapeDtypeStruct((part_rows, side), jnp.float32)
    part_out = jax.ShapeDtypeStruct((scen // band, row_tiles // (2 * PARTS), band, side), jnp.float32)
    part_bf16 = jax.ShapeDtypeStruct((part_rows, side), jnp.bfloat16)

    def banded(array):
        return array.reshape(scen // band, band, row_tiles, side).transpose(0, 2, 1, 3)

    def in_hbm(array):
        return pltpu.with_memory_space_constraint(array, pltpu.HBM)

    def first_backward(duals):
        return pl.pallas_call(
            functools.partial(first_backward_kernel, dims, pitch),
            in_specs=[scalars()] + [pl.BlockSpec(memory_space=pltpu.HBM)] * 4,
            out_specs=[whole(), whole()],
            out_shape=[messages, pltpu.VMEM((count, side, side), jnp.bfloat16)],
            scratch_shapes=[
                pltpu.SMEM((count,), jnp.int32),
                pltpu.SMEM((count,), jnp.int32),
                pltpu.VMEM(duals.shape, jnp.float32),
                picked_duals,
                acc_cols,
                pltpu.SemaphoreType.DMA((count // FIRST_LOAD + 3,)),
            ],
            compiler_params=params(),
            cost_estimate=cost,
            name="first_backward_products",
        )(core, in_hbm(rows), in_hbm(cols), in_hbm(duals), in_hbm(tile_values.reshape(count, side, side)))

    def in_vmem(array):
        return pltpu.with_memory_space_constraint(array, pltpu.VMEM)

    def backward(rounded, tiles):
        pieces = [*rounded, *map(swap_core, rounded)]
        cleared = pl.pallas_call(
            functools.partial(clear_kernel, scen, pitch),
            out_specs=whole(),
            out_shape=acc_cols,
            compiler_params=params(),
            name="clear_sums",
        )()
        return pl.pallas_call(
            functools.partial(backward_kernel, dims, pitch),
            in_specs=[scalars()] * 3 + [whole()] * (2 + len(pieces)),
            out_specs=[whole()] * 2,
            out_shape=[messages, acc_cols],
            input_output_aliases={4: 1},
            scratch_shapes=[picked_duals],
            compiler_params=params(),
            cost_estimate=cost,
            name="backward_products",
        )(core, rows, cols, in_vmem(tiles), in_vmem(cleared), *pieces)[0]

    def forward(probe, tiles):
        return pl.pallas_call(
            functools.partial(forward_kernel, dims, pitch),
            in_specs=[scalars()] * 3 + [whole()] * 2,
            out_specs=[whole()] * (1 + PARTS),
            out_shape=[jax.ShapeDtypeStruct((row_tiles * scen, side), jnp.float32)] + [part_bf16] * PARTS,
            scratch_shapes=[acc_cols],
            compiler_params=params(),
            cost_estimate=cost,
            name="forward_products",
        )(core, rows, cols, probe, in_vmem(tiles))

    def primal_step(recv, primal, cumulative, last):
        first = cumulative is None
        state = (primal,) if first else (primal, cumulative)
        shape = jax.ShapeDtypeStruct(primal.shape, jnp.float32)
        out_shape = [pltpu.VMEM(primal.shape, jnp.float32), messages] if last else [shape, messages, shape]
        return pl.pallas_call(
            functools.partial(primal_kernel, dims, first, last),
            in_specs=[whole()] * (4 + len(state)),
            out_specs=[whole()] * len(out_shape),
            out_shape=out_shape,
            compiler_params=params(),
            name="primal_update",
        )(recv, *state, flight_cost, win_start.reshape(1, -1), win_len.reshape(1, -1))

    def swap_core(value):
        return lax.ppermute(value, "col", [(i, i ^ 1) for i in range(n_col)])

    bits = (n_col // 2).bit_length() - 1

    def swap_chip(value, step):
        return lax.ppermute(value, "col", [(i, i ^ (2 << (step + i % 2) % bits)) for i in range(n_col)])

    def bf16_sum(first, second, name):
        return pl.pallas_call(
            sum_kernel,
            in_specs=[whole()] * 2,
            out_specs=whole(),
            out_shape=part_bf16,
            compiler_params=params(),
            name=name,
        )(first, second)

    def dual_step(part, image, away, dual, first, last):
        other = swap_core(away)
        partial = pl.pallas_call(
            functools.partial(pair_kernel, part),
            in_specs=[scalars()] + [whole()] * 2,
            out_specs=whole(),
            out_shape=part_bf16,
            compiler_params=params(),
            name="core_pair_sum",
        )(core, image, other)
        parts = []
        for step in range(bits):
            parts.append(swap_chip(partial, step))
            if step + 1 < bits:
                partial = bf16_sum(partial, parts[-1], "chip_sum")
        out_shape = [part_out] if last else [part_f32, part_bf16]
        return pl.pallas_call(
            functools.partial(dual_kernel, bits, part, first, last),
            in_specs=[scalars()] + [whole()] * (bits + 4),
            out_specs=[whole()] * len(out_shape),
            out_shape=out_shape,
            compiler_params=params(),
            name="dual_update",
        )(core, image, other, *parts, dual, banded(capacity))

    def results(primal, owned):
        duals_shape = jax.ShapeDtypeStruct((scen // band, row_tiles, band, side), jnp.float32)
        hbm = pl.BlockSpec(memory_space=pltpu.HBM)
        copies = scen // band
        others = [swap_core(part) for part in owned]
        primal_out, duals_out = pl.pallas_call(
            own_results_kernel,
            in_specs=[scalars()] + [whole()] * (2 + PARTS),
            out_specs=[hbm, hbm],
            out_shape=[jax.ShapeDtypeStruct(primal.shape, jnp.float32), duals_shape],
            scratch_shapes=[pltpu.SemaphoreType.DMA(((PARTS + 1) * copies + 1,))],
            compiler_params=params(),
            name="own_results",
        )(core, in_vmem(primal), *owned, others[0])
        duals_out = pl.pallas_call(
            other_results_kernel,
            in_specs=[scalars(), hbm] + [whole()] * (PARTS - 1),
            out_specs=hbm,
            out_shape=duals_shape,
            input_output_aliases={1: 0},
            scratch_shapes=[pltpu.SemaphoreType.DMA(((PARTS - 1) * copies,))],
            compiler_params=params(),
            name="other_results",
        )(core, duals_out, *others[1:])
        return primal_out, duals_out.transpose(0, 2, 1, 3).reshape(scen, row_length)

    send, tiles = first_backward(banded(dual_vars))
    duals, primal, cumulative = [banded(dual_vars)] * PARTS, increments, None
    for sweep in range(ITERS):
        last = sweep + 1 == ITERS
        if sweep:
            send = backward(rounded, tiles)
        recv = lax.all_to_all(send, ("row", "col"), 0, 0, tiled=True)
        primal, send, *cumulative = primal_step(recv, primal, cumulative, last)
        cumulative = None if last else cumulative[0]
        probe = lax.all_to_all(send, ("row", "col"), 0, 0, tiled=True)
        image, *aways = forward(probe, tiles)
        updates = [
            dual_step(part, image, aways[part], duals[part], sweep == 0, last)
            for part in range(PARTS)
        ]
        duals = [update[0] for update in updates]
        rounded = None if last else [update[1] for update in updates]
    return results(primal, duals)


def solution(mesh):
    placed = (
        P("row", "col", None, None, None),
        P("row", "col", None),
        P("row", "col", None),
        P("row", None, "col"),
        P(None, "row"),
        P(None, "col"),
        P("col"),
        P("col"),
        P(None, "row"),
    )
    return jax.shard_map(
        per_device,
        mesh=mesh,
        in_specs=placed,
        out_specs=(P("row", None, "col"), P(None, "row")),
        check_vma=False,
    )
```

```python
import functools
import math

import jax
import jax.numpy as jnp
from jax import lax
from jax.experimental import pallas as pl
from jax.experimental.pallas import tpu as pltpu
from jax.sharding import PartitionSpec as P

ITERS = 2
SIGMA_STEP = 0.2
PARTS = 2
UNROLL = 256
FIRST_UNROLL = 32
TRAIL = 16
PITCH_PAD = 8
VMEM_BYTES = 24 * 1024 * 1024
TRANSPOSED = (((1,), (1,)), ((), ()))


def params():
    return pltpu.CompilerParams(vmem_limit_bytes=VMEM_BYTES)


def whole():
    return pl.BlockSpec(memory_space=pltpu.VMEM)


def scalars():
    return pl.BlockSpec(memory_space=pltpu.SMEM)


def stacked_pair(first, second):
    zero = jnp.zeros_like(first)
    return jnp.concatenate(
        [jnp.concatenate([first, zero], axis=1), jnp.concatenate([zero, second], axis=1)], axis=0
    )


def column_place(dims, column, pitch):
    time_block, flight_tiles = dims[3], dims[4]
    return pl.multiple_of((column % flight_tiles * time_block + column // flight_tiles) * pitch, 8)


def trailing_adds(width, group, products, add):
    waiting = []
    for u in range(0, width, group):
        waiting += zip(range(u, u + group), products(u))
        while len(waiting) > TRAIL:
            add(*waiting.pop(0))
    for item in waiting:
        add(*item)


def backward_blocks(dims, pitch, width, rows_ref, cols_ref, duals_ref, tiles_ref, acc_ref, start):
    scen = dims[0] * dims[2]

    def products(u):
        pair = stacked_pair(duals_ref[rows_ref[start + u]], duals_ref[rows_ref[start + u + 1]])
        both = tiles_ref[pl.ds(start + u, 2)]
        result = jnp.dot(pair, both.reshape(-1, both.shape[2]), preferred_element_type=jnp.float32)
        return result[:scen], result[scen:]

    def add(u, product):
        place = column_place(dims, cols_ref[start + u], pitch)
        acc_ref[pl.ds(place, scen), :] += product

    trailing_adds(width, 2, products, add)


def round_sums(dims, pitch, acc_ref):
    scen, time_block, flight_tiles = dims[0] * dims[2], dims[3], dims[4]

    def body(index, lost):
        minute, kept = time_block - 1 - index, []
        for f in range(flight_tiles):
            place = pl.ds(pl.multiple_of((f * time_block + minute) * pitch, 8), scen)
            value = acc_ref[place, :] + lost[f]
            rounded = value.astype(jnp.bfloat16).astype(jnp.float32)
            kept.append(value - rounded)
            acc_ref[place, :] = rounded
        return tuple(kept)

    nothing = jnp.zeros((scen, acc_ref.shape[1]), jnp.float32)
    lax.fori_loop(0, time_block, body, (nothing,) * flight_tiles)


def write_messages(dims, pitch, acc_ref, out_ref):
    n_row, n_col, scen_local, time_block, _, own_tiles = dims
    piece = own_tiles * time_block
    round_sums(dims, pitch, acc_ref)

    def body(column, _):
        for group in range(n_row):
            for j in range(scen_local):
                base = column * (own_tiles * time_block * pitch) + group * scen_local + j
                parts = [
                    acc_ref[pl.ds(base + f * time_block * pitch, time_block, stride=pitch), :]
                    for f in range(own_tiles)
                ]
                out_ref[group * n_col + column, pl.ds(j * piece, piece), :] = jnp.concatenate(
                    parts, axis=0
                ).astype(jnp.bfloat16)
        return 0

    lax.fori_loop(0, n_col, body, 0)


def first_backward_kernel(
    dims, pitch, core_ref, row_source, col_source, dual_source, source_ref, out_ref, tiles_ref,
    rows_ref, cols_ref, bands_ref, duals_ref, acc_ref, sems
):
    count, pieces = tiles_ref.shape[0], sems.shape[0] - 3
    chunk = count // pieces
    lists = [
        pltpu.make_async_copy(row_source, rows_ref, sems.at[pieces]),
        pltpu.make_async_copy(col_source, cols_ref, sems.at[pieces + 1]),
        pltpu.make_async_copy(dual_source, bands_ref, sems.at[pieces + 2]),
    ]
    copies = [
        pltpu.make_async_copy(source_ref.at[pl.ds(i * chunk, chunk)], tiles_ref.at[pl.ds(i * chunk, chunk)], sems.at[i])
        for i in range(pieces)
    ]
    for copy in lists + copies:
        copy.start()
    acc_ref[...] = jnp.zeros_like(acc_ref)
    for copy in lists:
        copy.wait()
    bands = [bands_ref[a].astype(jnp.bfloat16) for a in range(bands_ref.shape[0])]
    duals_ref[...] = jnp.concatenate(bands, axis=1)

    def body(index, _):
        backward_blocks(
            dims, pitch, FIRST_UNROLL, rows_ref, cols_ref, duals_ref, tiles_ref, acc_ref, index * FIRST_UNROLL
        )
        return 0

    for i, copy in enumerate(copies):
        copy.wait()
        lax.fori_loop(i * chunk // FIRST_UNROLL, (i + 1) * chunk // FIRST_UNROLL, body, 0)
    write_messages(dims, pitch, acc_ref, out_ref)


def row_part(core, part, rows):
    return (core * PARTS + part) * rows


def part_rows_of(ref, core, part, size):
    return ref[pl.ds(pl.multiple_of(row_part(core, part, size), size), size), :]


def clear_kernel(scen, pitch, acc_ref):
    for row in range(0, acc_ref.shape[0], pitch):
        acc_ref[pl.ds(row, scen), :] = jnp.zeros((scen, acc_ref.shape[1]), jnp.float32)


def backward_kernel(dims, pitch, core_ref, rows_ref, cols_ref, tiles_ref, _, *refs):
    pieces, (out_ref, acc_ref, duals_ref) = refs[: 2 * PARTS], refs[2 * PARTS :]
    for i, piece in enumerate(pieces):
        core = core_ref[0] if i < PARTS else 1 - core_ref[0]
        scen, side = duals_ref.shape[1:]
        rows = piece.shape[0] // scen
        duals_ref[pl.ds(row_part(core, i % PARTS, rows), rows)] = piece[...].reshape(rows, scen, side)
    width = min(UNROLL, tiles_ref.shape[0])

    def body(index, _):
        backward_blocks(dims, pitch, width, rows_ref, cols_ref, duals_ref, tiles_ref, acc_ref, index * width)
        return 0

    lax.fori_loop(0, tiles_ref.shape[0] // width, body, 0)
    write_messages(dims, pitch, acc_ref, out_ref)


def forward_kernel(dims, pitch, core_ref, rows_ref, cols_ref, probe_ref, tiles_ref, *refs):
    n_row, n_col, scen_local, time_block, _, own_tiles = dims
    scen = n_row * scen_local
    piece = own_tiles * time_block
    (acc_ref, *outs), flat_ref = refs[:-1], refs[-1]
    acc_ref[...] = jnp.zeros_like(acc_ref)
    for group in range(n_row):
        for column in range(n_col):
            for j in range(scen_local):
                base = column * own_tiles * time_block * pitch + group * scen_local + j
                block = probe_ref[group * n_col + column, pl.ds(j * piece, piece), :].astype(jnp.float32)
                for f in range(own_tiles):
                    flat_ref[pl.ds(base + f * time_block * pitch, time_block, stride=pitch), :] = block[
                        f * time_block : (f + 1) * time_block
                    ]

    def picked(index):
        return flat_ref[pl.ds(column_place(dims, cols_ref[index], pitch), scen), :].astype(jnp.bfloat16)

    width = min(UNROLL, tiles_ref.shape[0])

    def body(index, _):
        start = index * width

        def products(u):
            first, second, third, fourth = (picked(start + u + i) for i in range(4))
            zero = jnp.zeros_like(first)
            left = jnp.concatenate([first, second, zero, zero], axis=0)
            right = jnp.concatenate([zero, zero, third, fourth], axis=0)
            sides = [tiles_ref[pl.ds(start + u + i, 2)] for i in (0, 2)]
            both = jnp.concatenate([two.reshape(-1, two.shape[2]) for two in sides], axis=1)
            result = lax.dot_general(
                jnp.concatenate([left, right], axis=1), both, TRANSPOSED, preferred_element_type=jnp.float32
            )
            side = tiles_ref.shape[1]
            return [
                result[i * scen : (i + 1) * scen, i % 2 * side : (i % 2 + 1) * side] for i in range(4)
            ]

        def add(u, product):
            place = pl.multiple_of(rows_ref[start + u] * scen, scen)
            acc_ref[pl.ds(place, scen), :] += product

        trailing_adds(width, 4, products, add)
        return 0

    lax.fori_loop(0, tiles_ref.shape[0] // width, body, 0)
    for part, out_ref in enumerate(outs):
        out_ref[...] = part_rows_of(acc_ref, 1 - core_ref[0], part, out_ref.shape[0]).astype(jnp.bfloat16)


def running(values, trailing, terms):
    length = values.shape[0]
    row_iota = lax.broadcasted_iota(jnp.int32, (length, length), 0)
    col_iota = lax.broadcasted_iota(jnp.int32, (length, length), 1)
    keep = ((col_iota >= row_iota) if trailing else (row_iota >= col_iota)).astype(jnp.float32).astype(jnp.bfloat16)
    total = None
    for _ in range(terms):
        term = values.astype(jnp.bfloat16)
        values = values - term.astype(jnp.float32)
        part = jnp.dot(keep, term, preferred_element_type=jnp.float32)
        total = part if total is None else total + part
    return total


def primal_kernel(dims, first, last, *refs):
    n_row, n_col, scen_local, time_block, _, own_tiles = dims
    refs = list(refs)
    recv_ref, inc_ref = refs[:2]
    cum_ref = None if first else refs[2]
    cost_ref, start_ref, len_ref, inc_out, send_ref = refs[2 + (not first) :][:5]
    cum_out = None if last else refs[-1]
    window, flight_local = cost_ref.shape
    side = flight_local // own_tiles
    piece = own_tiles * time_block
    tau_step = 0.6 / math.sqrt(window)
    minutes = lax.broadcasted_iota(jnp.int32, (window, flight_local), 0)
    begin = start_ref[...]
    upper = ((minutes >= begin) & (minutes < begin + len_ref[...])).astype(jnp.float32)
    slopes = []
    for j in range(scen_local):
        bands = []
        for h in range(n_col):
            total = recv_ref[h, pl.ds(j * piece, piece), :].astype(jnp.float32)
            for g in range(1, n_row):
                total = total + recv_ref[g * n_col + h, pl.ds(j * piece, piece), :].astype(jnp.float32)
            bands.append(
                jnp.concatenate([total[f * time_block : (f + 1) * time_block] for f in range(own_tiles)], axis=1)
            )
        slopes.append(jnp.concatenate(bands, axis=0) + cost_ref[...])
    gradient = running(jnp.concatenate(slopes, axis=1), True, 2)
    old = jnp.concatenate([inc_ref[j] for j in range(scen_local)], axis=1)
    if first:
        old_sum = running(old, False, 3)
    else:
        old_sum = jnp.concatenate([cum_ref[j] for j in range(scen_local)], axis=1)
    fresh = jnp.clip(old - tau_step * gradient, 0.0, jnp.concatenate([upper] * scen_local, axis=1))
    fresh_sum = running(fresh, False, 3)
    probe = (2.0 * fresh_sum - old_sum).astype(jnp.bfloat16)
    for j in range(scen_local):
        lanes = slice(j * flight_local, (j + 1) * flight_local)
        inc_out[j] = fresh[:, lanes]
        if not last:
            cum_out[j] = fresh_sum[:, lanes]
        for h in range(n_col):
            band = probe[h * time_block : (h + 1) * time_block, lanes]
            block = jnp.concatenate([band[:, f * side : (f + 1) * side] for f in range(own_tiles)], axis=0)
            for g in range(n_row):
                send_ref[g * n_col + h, pl.ds(j * piece, piece), :] = block


def own_sum(part, core_ref, image_ref, other_ref):
    own = part_rows_of(image_ref, core_ref[0], part, other_ref.shape[0])
    return own + other_ref[...].astype(jnp.float32)


def pair_kernel(part, core_ref, image_ref, other_ref, out_ref):
    out_ref[...] = own_sum(part, core_ref, image_ref, other_ref).astype(jnp.bfloat16)


def sum_kernel(first_ref, second_ref, out_ref):
    out_ref[...] = (first_ref[...].astype(jnp.float32) + second_ref[...].astype(jnp.float32)).astype(jnp.bfloat16)


def dual_kernel(remote, part, first, last, core_ref, image_ref, other_ref, *refs):
    parts, (dual_ref, cap_ref, dual_out) = refs[:remote], refs[remote : remote + 3]
    total = own_sum(part, core_ref, image_ref, other_ref)
    for received in parts:
        total = total + received[...].astype(jnp.float32)
    bands, row_tiles, band, side = cap_ref.shape
    rows = row_tiles // (2 * PARTS)
    begin = row_part(core_ref[0], part, rows)

    def own_rows(ref):
        return jnp.concatenate([ref[a, pl.ds(begin, rows)] for a in range(bands)], axis=1).reshape(-1, side)

    old = own_rows(dual_ref) if first else dual_ref[...]
    fresh = jnp.maximum(old + SIGMA_STEP * (total - own_rows(cap_ref).astype(jnp.float32)), 0.0)
    if last:
        value = fresh.reshape(rows, bands * band, side)
        for a in range(bands):
            dual_out[a] = value[:, a * band : (a + 1) * band]
    else:
        dual_out[...] = fresh
        refs[-1][...] = fresh.astype(jnp.bfloat16)


def part_copies(core, parts, out_ref, sems, used=0):
    copies = []
    for i, ref in parts:
        bands, rows = ref.shape[:2]
        for a in range(bands):
            place = out_ref.at[a, pl.ds(row_part(core, i, rows), rows)]
            copies.append(pltpu.make_async_copy(ref.at[a], place, sems.at[used + len(copies)]))
    return copies


def finish(copies):
    for copy in copies:
        copy.start()
    for copy in copies:
        copy.wait()


def own_results_kernel(core_ref, primal_ref, *refs):
    (*own, other), (primal_out, duals_out, sems) = refs[: PARTS + 1], refs[PARTS + 1 :]
    copies = part_copies(core_ref[0], list(enumerate(own)), duals_out, sems)
    copies += part_copies(1 - core_ref[0], [(0, other)], duals_out, sems, len(copies))
    copies.append(pltpu.make_async_copy(primal_ref, primal_out, sems.at[len(copies)]))
    finish(copies)


def other_results_kernel(core_ref, _, *refs):
    parts, (duals_out, sems) = refs[: PARTS - 1], refs[PARTS - 1 :]
    finish(part_copies(1 - core_ref[0], list(enumerate(parts, 1)), duals_out, sems))


def per_device(
    tile_values, tile_rows, tile_cols, increments, dual_vars, flight_cost, win_start, win_len, capacity
):
    n_row, n_col = lax.axis_size("row"), lax.axis_size("col")
    count, side = tile_values.shape[2], tile_values.shape[3]
    scen_local, window, flight_local = increments.shape
    scen, row_length = dual_vars.shape
    row_tiles = row_length // side
    time_block = window // n_col
    flight_tiles = flight_local * n_col // side
    own_tiles = flight_local // side
    col_tiles = time_block * flight_tiles
    dims = (n_row, n_col, scen_local, time_block, flight_tiles, own_tiles)
    message = (n_row * n_col, scen_local * own_tiles * time_block, side)
    part_rows = row_tiles * scen // (2 * PARTS)
    pitch = scen + PITCH_PAD
    band = 8

    rows, cols = tile_rows.reshape(count), tile_cols.reshape(count)
    core = (lax.axis_index("col") % 2).reshape(1)
    cost = pl.CostEstimate(flops=2 * count * scen * side * side, bytes_accessed=count * side * side, transcendentals=0)
    acc_cols = pltpu.VMEM((col_tiles * pitch, side), jnp.float32)
    picked_duals = pltpu.VMEM((row_tiles, scen, side), jnp.bfloat16)
    messages = jax.ShapeDtypeStruct(message, jnp.bfloat16)
    part_f32 = jax.ShapeDtypeStruct((part_rows, side), jnp.float32)
    part_out = jax.ShapeDtypeStruct((scen // band, row_tiles // (2 * PARTS), band, side), jnp.float32)
    part_bf16 = jax.ShapeDtypeStruct((part_rows, side), jnp.bfloat16)

    def banded(array):
        return array.reshape(scen // band, band, row_tiles, side).transpose(0, 2, 1, 3)

    def in_hbm(array):
        return pltpu.with_memory_space_constraint(array, pltpu.HBM)

    def first_backward(duals):
        return pl.pallas_call(
            functools.partial(first_backward_kernel, dims, pitch),
            in_specs=[scalars()] + [pl.BlockSpec(memory_space=pltpu.HBM)] * 4,
            out_specs=[whole(), whole()],
            out_shape=[messages, pltpu.VMEM((count, side, side), jnp.bfloat16)],
            scratch_shapes=[
                pltpu.SMEM((count,), jnp.int32),
                pltpu.SMEM((count,), jnp.int32),
                pltpu.VMEM(duals.shape, jnp.float32),
                picked_duals,
                acc_cols,
                pltpu.SemaphoreType.DMA((count // FIRST_UNROLL + 3,)),
            ],
            compiler_params=params(),
            cost_estimate=cost,
            name="first_backward_products",
        )(core, in_hbm(rows), in_hbm(cols), in_hbm(duals), in_hbm(tile_values.reshape(count, side, side)))

    def in_vmem(array):
        return pltpu.with_memory_space_constraint(array, pltpu.VMEM)

    def backward(rounded, tiles):
        pieces = [*rounded, *map(swap_core, rounded)]
        cleared = pl.pallas_call(
            functools.partial(clear_kernel, scen, pitch),
            out_specs=whole(),
            out_shape=acc_cols,
            compiler_params=params(),
            name="clear_sums",
        )()
        return pl.pallas_call(
            functools.partial(backward_kernel, dims, pitch),
            in_specs=[scalars()] * 3 + [whole()] * (2 + len(pieces)),
            out_specs=[whole()] * 2,
            out_shape=[messages, acc_cols],
            input_output_aliases={4: 1},
            scratch_shapes=[picked_duals],
            compiler_params=params(),
            cost_estimate=cost,
            name="backward_products",
        )(core, rows, cols, in_vmem(tiles), in_vmem(cleared), *pieces)[0]

    def forward(probe, tiles):
        return pl.pallas_call(
            functools.partial(forward_kernel, dims, pitch),
            in_specs=[scalars()] * 3 + [whole()] * 2,
            out_specs=[whole()] * (1 + PARTS),
            out_shape=[jax.ShapeDtypeStruct((row_tiles * scen, side), jnp.float32)] + [part_bf16] * PARTS,
            scratch_shapes=[acc_cols],
            compiler_params=params(),
            cost_estimate=cost,
            name="forward_products",
        )(core, rows, cols, probe, in_vmem(tiles))

    def primal_step(recv, primal, cumulative, last):
        first = cumulative is None
        state = (primal,) if first else (primal, cumulative)
        shape = jax.ShapeDtypeStruct(primal.shape, jnp.float32)
        out_shape = [pltpu.VMEM(primal.shape, jnp.float32), messages] if last else [shape, messages, shape]
        return pl.pallas_call(
            functools.partial(primal_kernel, dims, first, last),
            in_specs=[whole()] * (4 + len(state)),
            out_specs=[whole()] * len(out_shape),
            out_shape=out_shape,
            compiler_params=params(),
            name="primal_update",
        )(recv, *state, flight_cost, win_start.reshape(1, -1), win_len.reshape(1, -1))

    def swap_core(value):
        return lax.ppermute(value, "col", [(i, i ^ 1) for i in range(n_col)])

    bits = (n_col // 2).bit_length() - 1

    def swap_chip(value, step):
        return lax.ppermute(value, "col", [(i, i ^ (2 << (step + i % 2) % bits)) for i in range(n_col)])

    def bf16_sum(first, second, name):
        return pl.pallas_call(
            sum_kernel,
            in_specs=[whole()] * 2,
            out_specs=whole(),
            out_shape=part_bf16,
            compiler_params=params(),
            name=name,
        )(first, second)

    def dual_step(part, image, away, dual, first, last):
        other = swap_core(away)
        partial = pl.pallas_call(
            functools.partial(pair_kernel, part),
            in_specs=[scalars()] + [whole()] * 2,
            out_specs=whole(),
            out_shape=part_bf16,
            compiler_params=params(),
            name="core_pair_sum",
        )(core, image, other)
        parts = []
        for step in range(bits):
            parts.append(swap_chip(partial, step))
            if step + 1 < bits:
                partial = bf16_sum(partial, parts[-1], "chip_sum")
        out_shape = [part_out] if last else [part_f32, part_bf16]
        return pl.pallas_call(
            functools.partial(dual_kernel, bits, part, first, last),
            in_specs=[scalars()] + [whole()] * (bits + 4),
            out_specs=[whole()] * len(out_shape),
            out_shape=out_shape,
            compiler_params=params(),
            name="dual_update",
        )(core, image, other, *parts, dual, banded(capacity))

    def results(primal, owned):
        duals_shape = jax.ShapeDtypeStruct((scen // band, row_tiles, band, side), jnp.float32)
        hbm = pl.BlockSpec(memory_space=pltpu.HBM)
        copies = scen // band
        others = [swap_core(part) for part in owned]
        primal_out, duals_out = pl.pallas_call(
            own_results_kernel,
            in_specs=[scalars()] + [whole()] * (2 + PARTS),
            out_specs=[hbm, hbm],
            out_shape=[jax.ShapeDtypeStruct(primal.shape, jnp.float32), duals_shape],
            scratch_shapes=[pltpu.SemaphoreType.DMA(((PARTS + 1) * copies + 1,))],
            compiler_params=params(),
            name="own_results",
        )(core, in_vmem(primal), *owned, others[0])
        duals_out = pl.pallas_call(
            other_results_kernel,
            in_specs=[scalars(), hbm] + [whole()] * (PARTS - 1),
            out_specs=hbm,
            out_shape=duals_shape,
            input_output_aliases={1: 0},
            scratch_shapes=[pltpu.SemaphoreType.DMA(((PARTS - 1) * copies,))],
            compiler_params=params(),
            name="other_results",
        )(core, duals_out, *others[1:])
        return primal_out, duals_out.transpose(0, 2, 1, 3).reshape(scen, row_length)

    send, tiles = first_backward(banded(dual_vars))
    duals, primal, cumulative = [banded(dual_vars)] * PARTS, increments, None
    for sweep in range(ITERS):
        last = sweep + 1 == ITERS
        if sweep:
            send = backward(rounded, tiles)
        recv = lax.all_to_all(send, ("row", "col"), 0, 0, tiled=True)
        primal, send, *cumulative = primal_step(recv, primal, cumulative, last)
        cumulative = None if last else cumulative[0]
        probe = lax.all_to_all(send, ("row", "col"), 0, 0, tiled=True)
        image, *aways = forward(probe, tiles)
        updates = [
            dual_step(part, image, aways[part], duals[part], sweep == 0, last)
            for part in range(PARTS)
        ]
        duals = [update[0] for update in updates]
        rounded = None if last else [update[1] for update in updates]
    return results(primal, duals)


def solution(mesh):
    placed = (
        P("row", "col", None, None, None),
        P("row", "col", None),
        P("row", "col", None),
        P("row", None, "col"),
        P(None, "row"),
        P(None, "col"),
        P("col"),
        P("col"),
        P(None, "row"),
    )
    return jax.shard_map(
        per_device,
        mesh=mesh,
        in_specs=placed,
        out_specs=(P("row", None, "col"), P(None, "row")),
        check_vma=False,
    )
```

```python
import functools
import math

import jax
import jax.numpy as jnp
from jax import lax
from jax.experimental import pallas as pl
from jax.experimental.pallas import tpu as pltpu
from jax.sharding import PartitionSpec as P

ITERS = 2
SIGMA_STEP = 0.2
PARTS = 2
UNROLL = 256
FIRST_UNROLL = 32
TRAIL = 16
PITCH_PAD = 8
VMEM_BYTES = 24 * 1024 * 1024
TRANSPOSED = (((1,), (1,)), ((), ()))


def params():
    return pltpu.CompilerParams(vmem_limit_bytes=VMEM_BYTES)


def whole():
    return pl.BlockSpec(memory_space=pltpu.VMEM)


def scalars():
    return pl.BlockSpec(memory_space=pltpu.SMEM)


def stacked_pair(first, second):
    zero = jnp.zeros_like(first)
    return jnp.concatenate(
        [jnp.concatenate([first, zero], axis=1), jnp.concatenate([zero, second], axis=1)], axis=0
    )


def column_place(dims, column, pitch):
    time_block, flight_tiles = dims[3], dims[4]
    return pl.multiple_of((column % flight_tiles * time_block + column // flight_tiles) * pitch, 8)


def trailing_adds(width, group, products, add):
    waiting = []
    for u in range(0, width, group):
        waiting += zip(range(u, u + group), products(u))
        while len(waiting) > TRAIL:
            add(*waiting.pop(0))
    for item in waiting:
        add(*item)


def backward_blocks(dims, pitch, width, rows_ref, cols_ref, duals_ref, tiles_ref, acc_ref, start):
    scen = dims[0] * dims[2]

    def products(u):
        pair = stacked_pair(duals_ref[rows_ref[start + u]], duals_ref[rows_ref[start + u + 1]])
        both = tiles_ref[pl.ds(start + u, 2)]
        result = jnp.dot(pair, both.reshape(-1, both.shape[2]), preferred_element_type=jnp.float32)
        return result[:scen], result[scen:]

    def add(u, product):
        place = column_place(dims, cols_ref[start + u], pitch)
        acc_ref[pl.ds(place, scen), :] += product

    trailing_adds(width, 2, products, add)


def round_sums(dims, pitch, acc_ref):
    scen, time_block, flight_tiles = dims[0] * dims[2], dims[3], dims[4]
    lost = [jnp.zeros((scen, acc_ref.shape[1]), jnp.float32)] * flight_tiles
    for minute in reversed(range(time_block)):
        for f in range(flight_tiles):
            place = pl.ds((f * time_block + minute) * pitch, scen)
            value = acc_ref[place, :] + lost[f]
            rounded = value.astype(jnp.bfloat16).astype(jnp.float32)
            lost[f] = value - rounded
            acc_ref[place, :] = rounded


def write_messages(dims, pitch, acc_ref, out_ref):
    n_row, n_col, scen_local, time_block, _, own_tiles = dims
    piece = own_tiles * time_block
    round_sums(dims, pitch, acc_ref)
    for group in range(n_row):
        for column in range(n_col):
            for j in range(scen_local):
                base = column * own_tiles * time_block * pitch + group * scen_local + j
                parts = [
                    acc_ref[pl.ds(base + f * time_block * pitch, time_block, stride=pitch), :]
                    for f in range(own_tiles)
                ]
                out_ref[group * n_col + column, pl.ds(j * piece, piece), :] = jnp.concatenate(
                    parts, axis=0
                ).astype(jnp.bfloat16)


def first_backward_kernel(
    dims, pitch, core_ref, row_source, col_source, dual_source, source_ref, out_ref, tiles_ref,
    rows_ref, cols_ref, bands_ref, duals_ref, acc_ref, sems
):
    count, pieces = tiles_ref.shape[0], sems.shape[0] - 3
    chunk = count // pieces
    lists = [
        pltpu.make_async_copy(row_source, rows_ref, sems.at[pieces]),
        pltpu.make_async_copy(col_source, cols_ref, sems.at[pieces + 1]),
        pltpu.make_async_copy(dual_source, bands_ref, sems.at[pieces + 2]),
    ]
    copies = [
        pltpu.make_async_copy(source_ref.at[pl.ds(i * chunk, chunk)], tiles_ref.at[pl.ds(i * chunk, chunk)], sems.at[i])
        for i in range(pieces)
    ]
    for copy in lists + copies:
        copy.start()
    acc_ref[...] = jnp.zeros_like(acc_ref)
    for copy in lists:
        copy.wait()
    bands = [bands_ref[a].astype(jnp.bfloat16) for a in range(bands_ref.shape[0])]
    duals_ref[...] = jnp.concatenate(bands, axis=1)

    def body(index, _):
        backward_blocks(
            dims, pitch, FIRST_UNROLL, rows_ref, cols_ref, duals_ref, tiles_ref, acc_ref, index * FIRST_UNROLL
        )
        return 0

    for i, copy in enumerate(copies):
        copy.wait()
        lax.fori_loop(i * chunk // FIRST_UNROLL, (i + 1) * chunk // FIRST_UNROLL, body, 0)
    write_messages(dims, pitch, acc_ref, out_ref)


def row_part(core, part, rows):
    return (core * PARTS + part) * rows


def part_rows_of(ref, core, part, size):
    return ref[pl.ds(pl.multiple_of(row_part(core, part, size), size), size), :]


def clear_kernel(scen, pitch, acc_ref):
    for row in range(0, acc_ref.shape[0], pitch):
        acc_ref[pl.ds(row, scen), :] = jnp.zeros((scen, acc_ref.shape[1]), jnp.float32)


def backward_kernel(dims, pitch, core_ref, rows_ref, cols_ref, tiles_ref, _, *refs):
    pieces, (out_ref, acc_ref, duals_ref) = refs[: 2 * PARTS], refs[2 * PARTS :]
    for i, piece in enumerate(pieces):
        core = core_ref[0] if i < PARTS else 1 - core_ref[0]
        scen, side = duals_ref.shape[1:]
        rows = piece.shape[0] // scen
        duals_ref[pl.ds(row_part(core, i % PARTS, rows), rows)] = piece[...].reshape(rows, scen, side)
    width = min(UNROLL, tiles_ref.shape[0])

    def body(index, _):
        backward_blocks(dims, pitch, width, rows_ref, cols_ref, duals_ref, tiles_ref, acc_ref, index * width)
        return 0

    lax.fori_loop(0, tiles_ref.shape[0] // width, body, 0)
    write_messages(dims, pitch, acc_ref, out_ref)


def forward_kernel(dims, pitch, core_ref, rows_ref, cols_ref, probe_ref, tiles_ref, *refs):
    n_row, n_col, scen_local, time_block, _, own_tiles = dims
    scen = n_row * scen_local
    piece = own_tiles * time_block
    (acc_ref, *outs), flat_ref = refs[:-1], refs[-1]
    acc_ref[...] = jnp.zeros_like(acc_ref)
    for group in range(n_row):
        for column in range(n_col):
            for j in range(scen_local):
                base = column * own_tiles * time_block * pitch + group * scen_local + j
                block = probe_ref[group * n_col + column, pl.ds(j * piece, piece), :].astype(jnp.float32)
                for f in range(own_tiles):
                    flat_ref[pl.ds(base + f * time_block * pitch, time_block, stride=pitch), :] = block[
                        f * time_block : (f + 1) * time_block
                    ]

    def picked(index):
        return flat_ref[pl.ds(column_place(dims, cols_ref[index], pitch), scen), :].astype(jnp.bfloat16)

    width = min(UNROLL, tiles_ref.shape[0])

    def body(index, _):
        start = index * width

        def products(u):
            first, second, third, fourth = (picked(start + u + i) for i in range(4))
            zero = jnp.zeros_like(first)
            left = jnp.concatenate([first, second, zero, zero], axis=0)
            right = jnp.concatenate([zero, zero, third, fourth], axis=0)
            sides = [tiles_ref[pl.ds(start + u + i, 2)] for i in (0, 2)]
            both = jnp.concatenate([two.reshape(-1, two.shape[2]) for two in sides], axis=1)
            result = lax.dot_general(
                jnp.concatenate([left, right], axis=1), both, TRANSPOSED, preferred_element_type=jnp.float32
            )
            side = tiles_ref.shape[1]
            return [
                result[i * scen : (i + 1) * scen, i % 2 * side : (i % 2 + 1) * side] for i in range(4)
            ]

        def add(u, product):
            place = pl.multiple_of(rows_ref[start + u] * scen, scen)
            acc_ref[pl.ds(place, scen), :] += product

        trailing_adds(width, 4, products, add)
        return 0

    lax.fori_loop(0, tiles_ref.shape[0] // width, body, 0)
    for part, out_ref in enumerate(outs):
        out_ref[...] = part_rows_of(acc_ref, 1 - core_ref[0], part, out_ref.shape[0]).astype(jnp.bfloat16)


def running(values, trailing, terms):
    length = values.shape[0]
    row_iota = lax.broadcasted_iota(jnp.int32, (length, length), 0)
    col_iota = lax.broadcasted_iota(jnp.int32, (length, length), 1)
    keep = ((col_iota >= row_iota) if trailing else (row_iota >= col_iota)).astype(jnp.float32).astype(jnp.bfloat16)
    total = None
    for _ in range(terms):
        term = values.astype(jnp.bfloat16)
        values = values - term.astype(jnp.float32)
        part = jnp.dot(keep, term, preferred_element_type=jnp.float32)
        total = part if total is None else total + part
    return total


def primal_kernel(dims, first, last, *refs):
    n_row, n_col, scen_local, time_block, _, own_tiles = dims
    refs = list(refs)
    recv_ref, inc_ref = refs[:2]
    cum_ref = None if first else refs[2]
    cost_ref, start_ref, len_ref, inc_out, send_ref = refs[2 + (not first) :][:5]
    cum_out = None if last else refs[-1]
    window, flight_local = cost_ref.shape
    side = flight_local // own_tiles
    piece = own_tiles * time_block
    tau_step = 0.6 / math.sqrt(window)
    minutes = lax.broadcasted_iota(jnp.int32, (window, flight_local), 0)
    begin = start_ref[...]
    upper = ((minutes >= begin) & (minutes < begin + len_ref[...])).astype(jnp.float32)
    slopes = []
    for j in range(scen_local):
        bands = []
        for h in range(n_col):
            total = recv_ref[h, pl.ds(j * piece, piece), :].astype(jnp.float32)
            for g in range(1, n_row):
                total = total + recv_ref[g * n_col + h, pl.ds(j * piece, piece), :].astype(jnp.float32)
            bands.append(
                jnp.concatenate([total[f * time_block : (f + 1) * time_block] for f in range(own_tiles)], axis=1)
            )
        slopes.append(jnp.concatenate(bands, axis=0) + cost_ref[...])
    gradient = running(jnp.concatenate(slopes, axis=1), True, 2)
    old = jnp.concatenate([inc_ref[j] for j in range(scen_local)], axis=1)
    if first:
        old_sum = running(old, False, 2)
    else:
        old_sum = jnp.concatenate([cum_ref[j] for j in range(scen_local)], axis=1)
    fresh = jnp.clip(old - tau_step * gradient, 0.0, jnp.concatenate([upper] * scen_local, axis=1))
    fresh_sum = running(fresh, False, 2)
    probe = (2.0 * fresh_sum - old_sum).astype(jnp.bfloat16)
    for j in range(scen_local):
        lanes = slice(j * flight_local, (j + 1) * flight_local)
        inc_out[j] = fresh[:, lanes]
        if not last:
            cum_out[j] = fresh_sum[:, lanes]
        for h in range(n_col):
            band = probe[h * time_block : (h + 1) * time_block, lanes]
            block = jnp.concatenate([band[:, f * side : (f + 1) * side] for f in range(own_tiles)], axis=0)
            for g in range(n_row):
                send_ref[g * n_col + h, pl.ds(j * piece, piece), :] = block


def own_sum(part, core_ref, image_ref, other_ref):
    own = part_rows_of(image_ref, core_ref[0], part, other_ref.shape[0])
    return own + other_ref[...].astype(jnp.float32)


def pair_kernel(part, core_ref, image_ref, other_ref, out_ref):
    out_ref[...] = own_sum(part, core_ref, image_ref, other_ref).astype(jnp.bfloat16)


def sum_kernel(first_ref, second_ref, out_ref):
    out_ref[...] = (first_ref[...].astype(jnp.float32) + second_ref[...].astype(jnp.float32)).astype(jnp.bfloat16)


def dual_kernel(remote, part, first, last, core_ref, image_ref, other_ref, *refs):
    parts, (dual_ref, cap_ref, dual_out) = refs[:remote], refs[remote : remote + 3]
    total = own_sum(part, core_ref, image_ref, other_ref)
    for received in parts:
        total = total + received[...].astype(jnp.float32)
    bands, row_tiles, band, side = cap_ref.shape
    rows = row_tiles // (2 * PARTS)
    begin = row_part(core_ref[0], part, rows)

    def own_rows(ref):
        return jnp.concatenate([ref[a, pl.ds(begin, rows)] for a in range(bands)], axis=1).reshape(-1, side)

    old = own_rows(dual_ref) if first else dual_ref[...]
    fresh = jnp.maximum(old + SIGMA_STEP * (total - own_rows(cap_ref).astype(jnp.float32)), 0.0)
    if last:
        value = fresh.reshape(rows, bands * band, side)
        for a in range(bands):
            dual_out[a] = value[:, a * band : (a + 1) * band]
    else:
        dual_out[...] = fresh
        refs[-1][...] = fresh.astype(jnp.bfloat16)


def part_copies(core, parts, out_ref, sems, used=0):
    copies = []
    for i, ref in parts:
        bands, rows = ref.shape[:2]
        for a in range(bands):
            place = out_ref.at[a, pl.ds(row_part(core, i, rows), rows)]
            copies.append(pltpu.make_async_copy(ref.at[a], place, sems.at[used + len(copies)]))
    return copies


def finish(copies):
    for copy in copies:
        copy.start()
    for copy in copies:
        copy.wait()


def own_results_kernel(core_ref, primal_ref, *refs):
    (*own, other), (primal_out, duals_out, sems) = refs[: PARTS + 1], refs[PARTS + 1 :]
    copies = part_copies(core_ref[0], list(enumerate(own)), duals_out, sems)
    copies += part_copies(1 - core_ref[0], [(0, other)], duals_out, sems, len(copies))
    copies.append(pltpu.make_async_copy(primal_ref, primal_out, sems.at[len(copies)]))
    finish(copies)


def other_results_kernel(core_ref, _, *refs):
    parts, (duals_out, sems) = refs[: PARTS - 1], refs[PARTS - 1 :]
    finish(part_copies(1 - core_ref[0], list(enumerate(parts, 1)), duals_out, sems))


def per_device(
    tile_values, tile_rows, tile_cols, increments, dual_vars, flight_cost, win_start, win_len, capacity
):
    n_row, n_col = lax.axis_size("row"), lax.axis_size("col")
    count, side = tile_values.shape[2], tile_values.shape[3]
    scen_local, window, flight_local = increments.shape
    scen, row_length = dual_vars.shape
    row_tiles = row_length // side
    time_block = window // n_col
    flight_tiles = flight_local * n_col // side
    own_tiles = flight_local // side
    col_tiles = time_block * flight_tiles
    dims = (n_row, n_col, scen_local, time_block, flight_tiles, own_tiles)
    message = (n_row * n_col, scen_local * own_tiles * time_block, side)
    part_rows = row_tiles * scen // (2 * PARTS)
    pitch = scen + PITCH_PAD
    band = 8

    rows, cols = tile_rows.reshape(count), tile_cols.reshape(count)
    core = (lax.axis_index("col") % 2).reshape(1)
    cost = pl.CostEstimate(flops=2 * count * scen * side * side, bytes_accessed=count * side * side, transcendentals=0)
    acc_cols = pltpu.VMEM((col_tiles * pitch, side), jnp.float32)
    picked_duals = pltpu.VMEM((row_tiles, scen, side), jnp.bfloat16)
    messages = jax.ShapeDtypeStruct(message, jnp.bfloat16)
    part_f32 = jax.ShapeDtypeStruct((part_rows, side), jnp.float32)
    part_out = jax.ShapeDtypeStruct((scen // band, row_tiles // (2 * PARTS), band, side), jnp.float32)
    part_bf16 = jax.ShapeDtypeStruct((part_rows, side), jnp.bfloat16)

    def banded(array):
        return array.reshape(scen // band, band, row_tiles, side).transpose(0, 2, 1, 3)

    def in_hbm(array):
        return pltpu.with_memory_space_constraint(array, pltpu.HBM)

    def first_backward(duals):
        return pl.pallas_call(
            functools.partial(first_backward_kernel, dims, pitch),
            in_specs=[scalars()] + [pl.BlockSpec(memory_space=pltpu.HBM)] * 4,
            out_specs=[whole(), whole()],
            out_shape=[messages, pltpu.VMEM((count, side, side), jnp.bfloat16)],
            scratch_shapes=[
                pltpu.SMEM((count,), jnp.int32),
                pltpu.SMEM((count,), jnp.int32),
                pltpu.VMEM(duals.shape, jnp.float32),
                picked_duals,
                acc_cols,
                pltpu.SemaphoreType.DMA((count // FIRST_UNROLL + 3,)),
            ],
            compiler_params=params(),
            cost_estimate=cost,
            name="first_backward_products",
        )(core, in_hbm(rows), in_hbm(cols), in_hbm(duals), in_hbm(tile_values.reshape(count, side, side)))

    def in_vmem(array):
        return pltpu.with_memory_space_constraint(array, pltpu.VMEM)

    def backward(rounded, tiles):
        pieces = [*rounded, *map(swap_core, rounded)]
        cleared = pl.pallas_call(
            functools.partial(clear_kernel, scen, pitch),
            out_specs=whole(),
            out_shape=acc_cols,
            compiler_params=params(),
            name="clear_sums",
        )()
        return pl.pallas_call(
            functools.partial(backward_kernel, dims, pitch),
            in_specs=[scalars()] * 3 + [whole()] * (2 + len(pieces)),
            out_specs=[whole()] * 2,
            out_shape=[messages, acc_cols],
            input_output_aliases={4: 1},
            scratch_shapes=[picked_duals],
            compiler_params=params(),
            cost_estimate=cost,
            name="backward_products",
        )(core, rows, cols, in_vmem(tiles), in_vmem(cleared), *pieces)[0]

    def forward(probe, tiles):
        return pl.pallas_call(
            functools.partial(forward_kernel, dims, pitch),
            in_specs=[scalars()] * 3 + [whole()] * 2,
            out_specs=[whole()] * (1 + PARTS),
            out_shape=[jax.ShapeDtypeStruct((row_tiles * scen, side), jnp.float32)] + [part_bf16] * PARTS,
            scratch_shapes=[acc_cols],
            compiler_params=params(),
            cost_estimate=cost,
            name="forward_products",
        )(core, rows, cols, probe, in_vmem(tiles))

    def primal_step(recv, primal, cumulative, last):
        first = cumulative is None
        state = (primal,) if first else (primal, cumulative)
        shape = jax.ShapeDtypeStruct(primal.shape, jnp.float32)
        out_shape = [pltpu.VMEM(primal.shape, jnp.float32), messages] if last else [shape, messages, shape]
        return pl.pallas_call(
            functools.partial(primal_kernel, dims, first, last),
            in_specs=[whole()] * (4 + len(state)),
            out_specs=[whole()] * len(out_shape),
            out_shape=out_shape,
            compiler_params=params(),
            name="primal_update",
        )(recv, *state, flight_cost, win_start.reshape(1, -1), win_len.reshape(1, -1))

    def swap_core(value):
        return lax.ppermute(value, "col", [(i, i ^ 1) for i in range(n_col)])

    bits = (n_col // 2).bit_length() - 1

    def swap_chip(value, step):
        return lax.ppermute(value, "col", [(i, i ^ (2 << (step + i % 2) % bits)) for i in range(n_col)])

    def bf16_sum(first, second, name):
        return pl.pallas_call(
            sum_kernel,
            in_specs=[whole()] * 2,
            out_specs=whole(),
            out_shape=part_bf16,
            compiler_params=params(),
            name=name,
        )(first, second)

    def dual_step(part, image, away, dual, first, last):
        other = swap_core(away)
        partial = pl.pallas_call(
            functools.partial(pair_kernel, part),
            in_specs=[scalars()] + [whole()] * 2,
            out_specs=whole(),
            out_shape=part_bf16,
            compiler_params=params(),
            name="core_pair_sum",
        )(core, image, other)
        parts = []
        for step in range(bits):
            parts.append(swap_chip(partial, step))
            if step + 1 < bits:
                partial = bf16_sum(partial, parts[-1], "chip_sum")
        out_shape = [part_out] if last else [part_f32, part_bf16]
        return pl.pallas_call(
            functools.partial(dual_kernel, bits, part, first, last),
            in_specs=[scalars()] + [whole()] * (bits + 4),
            out_specs=[whole()] * len(out_shape),
            out_shape=out_shape,
            compiler_params=params(),
            name="dual_update",
        )(core, image, other, *parts, dual, banded(capacity))

    def results(primal, owned):
        duals_shape = jax.ShapeDtypeStruct((scen // band, row_tiles, band, side), jnp.float32)
        hbm = pl.BlockSpec(memory_space=pltpu.HBM)
        copies = scen // band
        others = [swap_core(part) for part in owned]
        primal_out, duals_out = pl.pallas_call(
            own_results_kernel,
            in_specs=[scalars()] + [whole()] * (2 + PARTS),
            out_specs=[hbm, hbm],
            out_shape=[jax.ShapeDtypeStruct(primal.shape, jnp.float32), duals_shape],
            scratch_shapes=[pltpu.SemaphoreType.DMA(((PARTS + 1) * copies + 1,))],
            compiler_params=params(),
            name="own_results",
        )(core, in_vmem(primal), *owned, others[0])
        duals_out = pl.pallas_call(
            other_results_kernel,
            in_specs=[scalars(), hbm] + [whole()] * (PARTS - 1),
            out_specs=hbm,
            out_shape=duals_shape,
            input_output_aliases={1: 0},
            scratch_shapes=[pltpu.SemaphoreType.DMA(((PARTS - 1) * copies,))],
            compiler_params=params(),
            name="other_results",
        )(core, duals_out, *others[1:])
        return primal_out, duals_out.transpose(0, 2, 1, 3).reshape(scen, row_length)

    send, tiles = first_backward(banded(dual_vars))
    duals, primal, cumulative = [banded(dual_vars)] * PARTS, increments, None
    for sweep in range(ITERS):
        last = sweep + 1 == ITERS
        if sweep:
            send = backward(rounded, tiles)
        recv = lax.all_to_all(send, ("row", "col"), 0, 0, tiled=True)
        primal, send, *cumulative = primal_step(recv, primal, cumulative, last)
        cumulative = None if last else cumulative[0]
        probe = lax.all_to_all(send, ("row", "col"), 0, 0, tiled=True)
        image, *aways = forward(probe, tiles)
        updates = [
            dual_step(part, image, aways[part], duals[part], sweep == 0, last)
            for part in range(PARTS)
        ]
        duals = [update[0] for update in updates]
        rounded = None if last else [update[1] for update in updates]
    return results(primal, duals)


def solution(mesh):
    placed = (
        P("row", "col", None, None, None),
        P("row", "col", None),
        P("row", "col", None),
        P("row", None, "col"),
        P(None, "row"),
        P(None, "col"),
        P("col"),
        P("col"),
        P(None, "row"),
    )
    return jax.shard_map(
        per_device,
        mesh=mesh,
        in_specs=placed,
        out_specs=(P("row", None, "col"), P(None, "row")),
        check_vma=False,
    )
```
